32 devices in a mesh: section: 2 (over x), wide: 16 (over z, y, core).
Axes of the slice: x: 2, y: 2, z: 4, core: 2. Of those that a mesh axis runs over, the one named last changes fastest.
Arguments:
- tokens: bfloat16 [4, 4096, 768], P(None, 'wide'), may hold values from -6 to 6
- cotangent: bfloat16 [4, 4096, 768], P(None, 'wide'), may hold values from -6 to 6
- seg_lengths: int32 [4, 1, 17], replicated, may hold values from 1 to 257, 4096 in all within a row
- w_query: bfloat16 [2, 768, 768], P('section'), may hold values from -0.21875 to 0.21875
- w_key: bfloat16 [2, 768, 768], P('section'), may hold values from -0.21875 to 0.21875
- w_value: bfloat16 [2, 768, 768], P('section'), may hold values from -0.21875 to 0.21875
- w_output: bfloat16 [2, 768, 768], P('section'), may hold values from -0.875 to 0.875
- w_gate: bfloat16 [2, 768, 2048], P('section'), may hold values from -0.21875 to 0.21875
- w_up: bfloat16 [2, 768, 2048], P('section'), may hold values from -0.21875 to 0.21875
- w_down: bfloat16 [2, 2048, 768], P('section'), may hold values from -0.1875 to 0.1875
- gain_attn: float32 [2, 768], P('section'), may hold values from 0.25 to 1.75
- gain_mlp: float32 [2, 768], P('section'), may hold values from 0.25 to 1.75
Outputs:
- block_outputs: bfloat16 [2, 4, 4096, 768], P('section', None, 'wide')
- input_grads: bfloat16 [2, 4, 4096, 768], P('section', None, 'wide')
- grad_query: float32 [2, 768, 768], P('section', 'wide')
- grad_key: float32 [2, 768, 768], P('section', 'wide')
- grad_value: float32 [2, 768, 768], P('section', 'wide')
- grad_output: float32 [2, 768, 768], P('section', 'wide')
- grad_gate: float32 [2, 768, 2048], P('section', 'wide')
- grad_up: float32 [2, 768, 2048], P('section', 'wide')
- grad_down: float32 [2, 2048, 768], P('section', 'wide')
- grad_gain_attn: float32 [2, 768], P('section', 'wide')
- grad_gain_mlp: float32 [2, 768], P('section', 'wide')
The draws below stay inside these ranges and needn't reach their ends.
Inputs may be any that keep to these rules, and one draw needn't show every extreme that they name: `seg_lengths`: each row's 17 lengths sum to 4096, and the longest is exactly 257.
All inputs are finite; a program needn't handle non-finite values.
Results may differ from the reference program's by a relative error of at most 0.02.
Values may be sent and summed in bfloat16 or wider, within the bound.
A program may use at most 320 MiB of HBM per device.

```python
import math
import jax
import jax.numpy as jnp
import numpy as np
from jax import lax

D = 768
HEADS = 12
FF = 2048
HEAD_DIM = 64
MB = 4
SEG_MAX = 257
LAYERS = 2
TOKENS_MB = 4096
ROW_LEN = 4096
ROWS_MB = 1
NSEG = 17


def block_scale(stream_key, shape, cuts, low, largest):
    def one(position, blocks):
        steps = jax.random.uniform(jax.random.fold_in(jax.random.fold_in(stream_key, 6), position), (blocks,), jnp.float32, low / len(cuts), largest / len(cuts))
        return jnp.repeat(jnp.exp(steps), shape[position] // blocks).reshape((-1,) + (1,) * (len(shape) - position - 1))

    level = one(*cuts[0])
    for cut in cuts[1:]:
        level = level * one(*cut)
    return level


def split_up(number_of, total, reach, slope):
    loads = [(1 << 20) // math.isqrt(rank ** slope) + 1 for rank in range(2, number_of + 1)]
    surplus, given = total - reach - (number_of - 1), [1] * (number_of - 1)
    while surplus > 0:
        free = [i for i in range(number_of - 1) if given[i] < reach]
        mass, budget = sum([loads[i] for i in free]), surplus
        for i in free:
            addition = min(reach - given[i], max(1, budget * loads[i] // mass), surplus)
            given[i] = given[i] + addition
            surplus = surplus - addition
    return np.array([reach] + given)


def ragged_sizes(rng, count, total, bound, slope):
    if count == 2:
        one = jax.random.randint(rng, (), max(1, total - bound), min(bound, total - 1) + 1)
        return jnp.stack([one, total - one])
    tallies = jnp.asarray(split_up(count, total, bound, slope), jnp.int32)
    couples = (count - 1) // 2
    giver, sink = tallies[1:1 + 2 * couples:2], tallies[2:2 + 2 * couples:2]
    room = jnp.minimum(giver - 1, bound - sink)
    shifted = jax.random.randint(jax.random.fold_in(rng, 1), (couples,), 0, 1 << 20) % (room + 1)
    tallies = tallies.at[1:1 + 2 * couples:2].set(giver - shifted).at[2:2 + 2 * couples:2].set(sink + shifted)
    return tallies[jax.random.permutation(jax.random.fold_in(rng, 2), count)]


def gaussian(own_key, extent, spread, bound, split=(), kind=jnp.bfloat16):
    drawn = spread * jax.random.normal(own_key, extent, jnp.float32)
    if split:
        drawn = drawn * block_scale(own_key, extent, split, -0.22, 0.18)
    return jnp.clip(drawn, -bound, bound).astype(kind)


def setup_inputs(seed: int = 0) -> dict:
    key_of = jax.random.split(jax.random.key(seed), 13)
    tokens = gaussian(key_of[0], (MB, TOKENS_MB, D), 1.0, 6.0, ((1, 16),))
    cotangent = gaussian(key_of[1], (MB, TOKENS_MB, D), 1.0, 6.0, ((1, 16),))
    seg_lengths = jax.vmap(lambda own: ragged_sizes(own, NSEG, ROW_LEN, SEG_MAX, 1))(jax.random.split(key_of[2], MB * ROWS_MB)).reshape((MB, ROWS_MB, NSEG)).astype(jnp.int32)
    w_query = gaussian(key_of[3], (LAYERS, D, D), D ** -0.5, 0.21875, ((0, 2),))
    w_key = gaussian(key_of[4], (LAYERS, D, D), D ** -0.5, 0.21875, ((0, 2),))
    w_value = gaussian(key_of[5], (LAYERS, D, D), D ** -0.5, 0.21875, ((0, 2),))
    w_output = gaussian(key_of[6], (LAYERS, D, D), (D // 16) ** -0.5, 0.875, ((0, 2),))
    w_gate = gaussian(key_of[7], (LAYERS, D, FF), D ** -0.5, 0.21875, ((0, 2),))
    w_up = gaussian(key_of[8], (LAYERS, D, FF), D ** -0.5, 0.21875, ((0, 2),))
    w_down = gaussian(key_of[9], (LAYERS, FF, D), (FF // 2) ** -0.5, 0.1875, ((0, 2),))
    gain_attn = jnp.clip(1.0 + 0.15 * jax.random.normal(key_of[10], (LAYERS, D), jnp.float32), 0.25, 1.75)
    gain_mlp = jnp.clip(1.0 + 0.15 * jax.random.normal(key_of[11], (LAYERS, D), jnp.float32), 0.25, 1.75)
    return dict(tokens=tokens, cotangent=cotangent, seg_lengths=seg_lengths, w_query=w_query, w_key=w_key, w_value=w_value, w_output=w_output, w_gate=w_gate, w_up=w_up, w_down=w_down, gain_attn=gain_attn, gain_mlp=gain_mlp)


EPS = 1e-05
THETA = 10000.0
HIGH = lax.Precision.HIGHEST

@jax.custom_vjp
def low(v):
    return lax.optimization_barrier(v.astype(jnp.bfloat16)).astype(jnp.float32)

@jax.custom_vjp
def low_back(v):
    return v

def low_keep(v):
    return (low(v), None)

def low_pass(kept, grad):
    return (grad,)

def back_keep(v):
    return (v, None)

def back_low(kept, grad):
    return (low(grad),)
low.defvjp(low_keep, low_pass)
low_back.defvjp(back_keep, back_low)

def matmul(left, right):
    return jnp.dot(left, right, precision=HIGH, preferred_element_type=jnp.float32)

def rms_scaled(hidden, gain):
    inverse = lax.rsqrt(lax.optimization_barrier(jnp.mean(hidden * hidden, axis=-1, keepdims=True)) + EPS)
    return hidden * inverse * gain

def rotate(field, offsets, direction):
    head_dim = field.shape[1] // HEADS
    half_dim = head_dim // 2
    freqs = THETA ** (-jnp.arange(half_dim, dtype=jnp.float32) * 2.0 / head_dim)
    angles = offsets[:, None] * freqs[None, :]
    cosine = jnp.cos(angles)[:, None, :]
    sine_part = direction * jnp.sin(angles)[:, None, :]
    shaped = field.reshape(field.shape[0], HEADS, 2, half_dim)
    first = shaped[:, :, 0, :]
    second = shaped[:, :, 1, :]
    turned = jnp.stack([first * cosine - second * sine_part, second * cosine + first * sine_part], axis=2)
    return turned.reshape(field.shape)

def row_segments(length_row):
    positions = jnp.arange(ROW_LEN, dtype=jnp.int32)
    starts = (jnp.cumsum(length_row) - length_row).astype(jnp.int32)
    counted = (lax.optimization_barrier(jnp.sum((starts[None, :] <= positions[:, None]).astype(jnp.int32), axis=1)) - 1).astype(jnp.int32)
    return (positions, starts, counted)

def row_offsets(length_row):
    positions, starts, counted = row_segments(length_row)
    return (positions - starts[counted]).astype(jnp.float32)

def row_attention(packed):
    query_row, key_row, value_row, length_row = packed
    positions, starts, counted = row_segments(length_row)
    block = min(512, ROW_LEN)
    block_count = ROW_LEN // block
    key_pad = jnp.concatenate([jnp.zeros((block, D), jnp.float32), key_row], axis=0)
    value_pad = jnp.concatenate([jnp.zeros((block, D), jnp.float32), value_row], axis=0)
    ids_pad = jnp.concatenate([jnp.full((block,), -1, jnp.int32), counted]).astype(jnp.int32)
    pos_pad = jnp.concatenate([jnp.arange(block, dtype=jnp.int32) - block, positions]).astype(jnp.int32)
    score_scale = HEAD_DIM ** (-0.5)

    def one_block(block_index):
        first = (block_index * block).astype(jnp.int32)
        query_block = lax.dynamic_slice_in_dim(query_row, first, block, 0)
        query_ids = lax.dynamic_slice_in_dim(counted, first, block, 0)
        query_pos = lax.dynamic_slice_in_dim(positions, first, block, 0)
        key_block = lax.dynamic_slice_in_dim(key_pad, first, 2 * block, 0)
        value_block = lax.dynamic_slice_in_dim(value_pad, first, 2 * block, 0)
        key_ids = lax.dynamic_slice_in_dim(ids_pad, first, 2 * block, 0)
        key_pos = lax.dynamic_slice_in_dim(pos_pad, first, 2 * block, 0)
        allowed = (query_ids[:, None] == key_ids[None, :]) & (key_pos[None, :] <= query_pos[:, None]) & (key_ids[None, :] >= 0)
        query_heads = query_block.reshape(block, HEADS, -1)
        key_heads = key_block.reshape(2 * block, HEADS, -1)
        value_heads = value_block.reshape(2 * block, HEADS, -1)
        scores = low_back(jnp.einsum('qhd,khd->hqk', query_heads, key_heads, precision=HIGH) * score_scale)
        masked = jnp.where(allowed[None], scores, -1e+30)
        row_peak = lax.optimization_barrier(jnp.max(masked, axis=2, keepdims=True))
        raw_weights = jnp.exp(masked - row_peak)
        probs = raw_weights / lax.optimization_barrier(jnp.sum(raw_weights, axis=2, keepdims=True))
        attended = jnp.einsum('hqk,khd->qhd', low(probs), value_heads, precision=HIGH)
        return attended.reshape(block, -1)
    pieces = lax.map(jax.checkpoint(one_block), jnp.arange(block_count, dtype=jnp.int32))
    return pieces.reshape(ROW_LEN, -1)

def one_layer(hidden, weights, offsets, lengths_rows):
    w_query, w_key, w_value, w_output, w_gate, w_up, w_down, gain_attn, gain_mlp = weights
    normed = low(rms_scaled(hidden, gain_attn))
    queries = low(rotate(low_back(matmul(normed, w_query)), offsets, 1.0))
    key_rows = low(rotate(low_back(matmul(normed, w_key)), offsets, 1.0))
    value_rows = low(low_back(matmul(normed, w_value)))
    rows_count = lengths_rows.shape[0]
    attended = lax.map(row_attention, (queries.reshape(rows_count, ROW_LEN, D), key_rows.reshape(rows_count, ROW_LEN, D), value_rows.reshape(rows_count, ROW_LEN, D), lengths_rows))
    attended = low(low_back(attended.reshape(-1, D)))
    mixed = hidden + low_back(matmul(attended, w_output))
    normed_two = low(rms_scaled(mixed, gain_mlp))
    gate = low_back(matmul(normed_two, w_gate))
    up_part = low_back(matmul(normed_two, w_up))
    product = low(jax.nn.silu(gate) * up_part)
    return mixed + low_back(matmul(product, w_down))

def reference(tokens, cotangent, seg_lengths, w_query, w_key, w_value, w_output, w_gate, w_up, w_down, gain_attn, gain_mlp):
    lengths_rows = seg_lengths.reshape(-1, seg_lengths.shape[-1]).astype(jnp.int32)
    offsets = jax.vmap(row_offsets)(lengths_rows).reshape(-1)
    params = [w.astype(jnp.float32) for w in (w_query, w_key, w_value, w_output, w_gate, w_up, w_down, gain_attn, gain_mlp)]
    inputs = tokens.reshape(-1, D).astype(jnp.float32)
    probes = jnp.zeros((LAYERS - 1, inputs.shape[0], D), jnp.float32)

    def forward(first_input, probe_set, weights):
        hidden = first_input
        layer_outputs = []
        for layer_index in range(LAYERS):
            if layer_index > 0:
                hidden = low(low_back(hidden + probe_set[layer_index - 1]))
            hidden = one_layer(hidden, [w[layer_index] for w in weights], offsets, lengths_rows)
            layer_outputs.append(hidden)
        return (hidden, jnp.stack(layer_outputs))
    final_value, pullback, outputs = jax.vjp(forward, inputs, probes, params, has_aux=True)
    grad_inputs, grad_probes, grad_params = pullback(cotangent.reshape(-1, D).astype(jnp.float32))
    shape_out = (LAYERS, MB, TOKENS_MB, D)
    block_outputs = outputs.reshape(shape_out).astype(jnp.bfloat16)
    input_grads = jnp.concatenate([grad_inputs[None], grad_probes], axis=0).reshape(shape_out).astype(jnp.bfloat16)
    return (block_outputs, input_grads, grad_params[0], grad_params[1], grad_params[2], grad_params[3], grad_params[4], grad_params[5], grad_params[6], grad_params[7], grad_params[8])
```

```python
import functools

import jax
import jax.numpy as jnp
from jax import lax
from jax.experimental import pallas as pl
from jax.experimental.pallas import tpu as pltpu
from jax.sharding import PartitionSpec as P

HEADS = 12
EPS = 1e-05
THETA = 10000.0

F32 = jnp.float32
BF16 = jnp.bfloat16
MESH = pl.DeviceIdType.MESH
LANES = 128
VMEM_BYTES = 60 * 1024 * 1024


def dot(left, right):
    return jnp.dot(left, right, preferred_element_type=F32)


def dot_nt(left, right):
    return lax.dot_general(
        left, right, (((1,), (1,)), ((), ())), preferred_element_type=F32
    )


def rms_parts(hidden):
    inverse = lax.rsqrt(jnp.mean(hidden * hidden, axis=1, keepdims=True) + EPS)
    return (hidden * inverse, inverse)


def rms_back(upstream, scaled, inverse):
    return inverse * (upstream - scaled * jnp.mean(upstream * scaled, axis=1, keepdims=True))


def low_half(rows):
    lane = lax.broadcasted_iota(jnp.int32, (rows, LANES), 1)
    return lane % 64 < 32


def rope(field, cosine, sine, direction):
    partner = jnp.where(
        low_half(field.shape[0]),
        pltpu.roll(field, 96, 1),
        pltpu.roll(field, 32, 1),
    )
    if direction > 0:
        return field * cosine + partner * sine
    return field * cosine - partner * sine


def split_heads(block):
    lane = lax.broadcasted_iota(jnp.int32, block.shape, 1)
    zero = jnp.zeros_like(block)
    return jnp.concatenate(
        [jnp.where(lane < 64, block, zero), jnp.where(lane >= 64, block, zero)], axis=0
    )


def join_heads(turned):
    count = turned.shape[1] // 2
    row = lax.broadcasted_iota(jnp.int32, (LANES, count), 0)
    return jnp.where(row < 64, turned[:, :count], turned[:, count:]).T


def meet(partners):
    barrier = pltpu.get_barrier_semaphore()
    total = 0
    for condition, device in partners:

        @pl.when(condition)
        def _(device=device):
            pl.semaphore_signal(barrier, inc=1, device_id=device, device_id_type=MESH)

        total = total + condition.astype(jnp.int32)
    pl.semaphore_wait(barrier, total)


def forward_kernel(
    tokens, w_query, w_key, w_value, w_output, w_gate, w_up, w_down,
    gain_attn, gain_mlp, cosine, sine, first_key,
    block_out, x_out, normed_out, q_out, k_out, v_out, probs_out, att_out, mixed_out,
    n2_out, slope_out, silu_out, prod_out,
    wq, wk, wv, wo, wg, wu, wd,
    xs, normed, qs, ks, vs, probs, att, mixed, n2, slope, silu, prod, ys, bias,
    weight_sem, token_sem, save_sem, out_sem, halo_send, halo_recv, hand_send, hand_recv,
):
    section, wide = lax.axis_index("section"), lax.axis_index("wide")
    last_section, last_wide = lax.axis_size("section") - 1, lax.axis_size("wide") - 1
    batches, rows, width = tokens.shape
    hidden_width = wg.shape[1]
    half = rows // 2
    pairs = width // LANES
    own = pl.ds(rows, rows)
    has_left, has_right = wide > 0, wide < last_wide
    has_before, has_after = section > 0, section < last_section
    is_first = jnp.logical_not(has_before)

    meet([
        (has_left, {"wide": wide - 1}), (has_right, {"wide": wide + 1}),
        (has_before, {"section": section - 1}), (has_after, {"section": section + 1}),
    ])

    weights = ((w_query, wq), (w_key, wk), (w_value, wv), (w_output, wo),
               (w_gate, wg), (w_up, wu), (w_down, wd))
    def weight_copy(index):
        source, target = weights[index]
        return pltpu.make_async_copy(source.at[0], target, weight_sem.at[index])

    def token_copy(mb):
        return pltpu.make_async_copy(tokens.at[mb], xs.at[mb, own], token_sem.at[mb])

    def halo_copy(mb, source):
        return pltpu.make_async_remote_copy(
            source, xs.at[mb, pl.ds(0, rows)], halo_send.at[mb], halo_recv.at[mb],
            device_id={"wide": wide + 1}, device_id_type=MESH)

    def hand_copy(mb):
        return pltpu.make_async_remote_copy(
            ys.at[mb], xs.at[mb, own], hand_send.at[mb], hand_recv.at[mb],
            device_id={"section": section + 1}, device_id_type=MESH)

    @pl.when(is_first)
    def _():
        for mb in range(batches):
            token_copy(mb).start()

    @pl.when(is_first & has_right)
    def _():
        for mb in range(batches):
            halo_copy(mb, tokens.at[mb]).start()

    for index in range(7):
        weight_copy(index).start()

    @pl.when(jnp.logical_not(has_left))
    def _():
        xs[:, pl.ds(0, rows), :] = jnp.zeros((batches, rows, width), BF16)

    def saves(mb, slot):
        listed = (
            (xs.at[mb, own], x_out), (normed.at[slot], normed_out), (qs.at[slot], q_out),
            (ks.at[slot], k_out), (vs.at[slot], v_out), (probs.at[slot], probs_out),
            (att.at[slot], att_out), (mixed.at[slot], mixed_out), (n2.at[slot], n2_out),
            (slope.at[slot], slope_out), (silu.at[slot], silu_out), (prod.at[slot], prod_out),
        )
        return [
            pltpu.make_async_copy(source, target.at[mb], save_sem.at[index, slot])
            for index, (source, target) in enumerate(listed)
        ]

    def out_copy(mb):
        return pltpu.make_async_copy(ys.at[mb], block_out.at[mb], out_sem.at[mb])

    def first_use(mb, *indices):
        @pl.when(mb == 0)
        def _():
            for index in indices:
                weight_copy(index).wait()

    def keys_values(mb, slot, part):
        at = pl.ds(part * rows, rows)
        cos_rows, sin_rows = cosine[mb, at, :], sine[mb, at, :]
        rows_n = normed[slot, at, :]
        for start in range(0, width, 256):
            keys = dot(rows_n, wk[:, start:start + 256])
            for inner in range(0, 256, LANES):
                ks[slot, at, start + inner:start + inner + LANES] = rope(
                    keys[:, inner:inner + LANES], cos_rows, sin_rows, 1).astype(BF16)
            vs[slot, at, start:start + 256] = dot(rows_n, wv[:, start:start + 256]).astype(BF16)

    def normalise(mb, slot, part):
        at = pl.ds(part * rows, rows)
        scaled, _ = rms_parts(xs[mb, at, :].astype(F32))
        normed[slot, at, :] = (scaled * gain_attn[...]).astype(BF16)

    def step(mb, carry):
        slot = lax.rem(mb, 2)

        @pl.when(is_first)
        def _():
            token_copy(mb).wait()

        @pl.when(has_before)
        def _():
            hand_copy(mb).wait_recv()

        @pl.when(has_before & has_right)
        def _():
            halo_copy(mb, xs.at[mb, own]).start()

        @pl.when(mb >= 2)
        def _():
            for copy in saves(mb - 2, slot):
                copy.wait()

        for block in range(2):
            key_at = lax.broadcasted_iota(jnp.int32, (3 * half, half), 0) + (block * half - rows)
            query_at = lax.broadcasted_iota(jnp.int32, (3 * half, half), 1) + block * half
            first = first_key[mb, :, block * half:(block + 1) * half]
            seen = (key_at >= first) & (key_at <= query_at)
            bias[block] = jnp.where(seen, 0.0, -1e30)

        normalise(mb, slot, 1)
        first_use(mb, 0, 1, 2)
        cos_rows, sin_rows = cosine[mb, own, :], sine[mb, own, :]
        rows_n = normed[slot, own, :]
        for start in range(0, width, 256):
            queries = dot(rows_n, wq[:, start:start + 256])
            for inner in range(0, 256, LANES):
                turned = rope(queries[:, inner:inner + LANES], cos_rows, sin_rows, 1)
                qs[slot, :, start + inner:start + inner + LANES] = (
                    turned.astype(BF16) * jnp.asarray(0.125, BF16))
        keys_values(mb, slot, 1)

        @pl.when(has_left)
        def _():
            halo_copy(mb, xs.at[mb, own]).wait_recv()

        normalise(mb, slot, 0)
        keys_values(mb, slot, 0)

        def attend(pair, carry):
            lanes = pl.ds(pl.multiple_of(pair * LANES, LANES), LANES)
            key_pair = ks[slot, :, lanes]
            value_turned = vs[slot, :, lanes].T
            for block in range(2):
                queries = split_heads(qs[slot, block * half:(block + 1) * half, lanes])
                low = block * half
                scores = dot_nt(key_pair[low:low + 3 * half, :], queries)
                hidden = bias[block]
                scores = scores + jnp.concatenate([hidden, hidden], axis=1)
                peak = jnp.max(scores, axis=0, keepdims=True)
                raw = jnp.exp(scores - peak)
                scale = 1.0 / jnp.sum(raw, axis=0, keepdims=True)
                probs_b = (raw * scale).astype(BF16)
                probs[slot, pair, block] = probs_b
                turned = dot(value_turned[:, low:low + 3 * half], probs_b)
                att[slot, block * half:(block + 1) * half, lanes] = join_heads(turned).astype(BF16)
            return carry

        lax.fori_loop(0, pairs, attend, 0)

        first_use(mb, 3)
        rows_a = att[slot]
        for start in range(0, width, 256):
            at = slice(start, start + 256)
            mixed[slot, :, at] = xs[mb, own, at].astype(F32) + dot(rows_a, wo[:, at])
        scaled, _ = rms_parts(mixed[slot])
        n2[slot] = (scaled * gain_mlp[...]).astype(BF16)
        first_use(mb, 4, 5)
        rows_n = n2[slot]
        for start in range(0, hidden_width, 256):
            at = slice(start, start + 256)
            gate = dot(rows_n, wg[:, at])
            up = dot(rows_n, wu[:, at])
            sigma = jax.nn.sigmoid(gate)
            gated = gate * sigma
            prod[slot, :, at] = (gated * up).astype(BF16)
            silu[slot, :, at] = gated.astype(BF16)
            slope[slot, :, at] = (up * (sigma * (1.0 + gate * (1.0 - sigma)))).astype(BF16)
        first_use(mb, 6)
        rows_p = prod[slot]
        for start in range(0, width, 256):
            at = slice(start, start + 256)
            ys[mb, :, at] = (mixed[slot, :, at] + dot(rows_p, wd[:, at])).astype(BF16)

        @pl.when(has_after)
        def _():
            hand_copy(mb).start()

        out_copy(mb).start()
        for copy in saves(mb, slot):
            copy.start()
        return carry

    lax.fori_loop(0, batches, step, 0)

    for mb in range(batches):
        if mb >= batches - 2:
            for copy in saves(mb, mb % 2):
                copy.wait()
        out_copy(mb).wait()

    @pl.when(has_after)
    def _():
        for mb in range(batches):
            hand_copy(mb).wait_send()

    @pl.when(has_right)
    def _():
        for mb in range(batches):
            halo_copy(mb, xs.at[mb, own]).wait_send()


def any_spec():
    return pl.BlockSpec(memory_space=pl.ANY)


def vmem_spec():
    return pl.BlockSpec(memory_space=pltpu.VMEM)


def run_forward(tokens, weights, gain_attn, gain_mlp, cosine, sine, first_key):
    batches, rows, width = tokens.shape
    hidden_width = weights[4].shape[2]
    pairs = width // LANES
    both = 2 * rows
    one = (batches, rows, width)
    two = (batches, both, width)
    wide = (batches, rows, hidden_width)
    prob = (batches, pairs, 2, 3 * rows // 2, rows)
    saved = [(one, BF16), (one, BF16), (two, BF16), (one, BF16), (two, BF16), (two, BF16), (prob, BF16),
             (one, BF16), (one, F32), (one, BF16), (wide, BF16), (wide, BF16), (wide, BF16)]
    slots = [pltpu.VMEM((2,) + shape[1:], dtype) for shape, dtype in saved[2:]]
    return pl.pallas_call(
        forward_kernel,
        out_shape=[jax.ShapeDtypeStruct(shape, dtype) for shape, dtype in saved],
        in_specs=[any_spec()] * 8 + [vmem_spec()] * 5,
        out_specs=[any_spec()] * len(saved),
        scratch_shapes=[pltpu.VMEM(w.shape[1:], BF16) for w in weights]
        + [pltpu.VMEM(two, BF16)]
        + slots
        + [
            pltpu.VMEM(one, BF16),
            pltpu.VMEM((2, 3 * rows // 2, rows // 2), F32),
            pltpu.SemaphoreType.DMA((7,)),
            pltpu.SemaphoreType.DMA((batches,)),
            pltpu.SemaphoreType.DMA((12, 2)),
            pltpu.SemaphoreType.DMA((batches,)),
            pltpu.SemaphoreType.DMA((batches,)),
            pltpu.SemaphoreType.DMA((batches,)),
            pltpu.SemaphoreType.DMA((batches,)),
            pltpu.SemaphoreType.DMA((batches,)),
        ],
        compiler_params=pltpu.CompilerParams(
            collective_id=1, has_side_effects=True, vmem_limit_bytes=VMEM_BYTES),
        name="forward",
    )(tokens, *weights, gain_attn, gain_mlp, cosine, sine, first_key)


def backward_kernel(
    cotangent, x_in, q_in, k_in, v_in, probs_in, mixed_in, slope_in, silu_in,
    w_query, w_key, w_value, w_output, w_gate, w_up, w_down,
    gain_attn, gain_mlp, cosine, sine,
    grad_out, g_out, db_out, dg_out, du_out, dq_out, dk_out, dv_out, gains_out,
    wq, wk, wv, wo, wg, wu, wd,
    gs, xs, qs, ks, vs, probs, mixed, slope, silu, branch, d_att, d_mixed, d_norm,
    halo_out, halo_in, dxs,
    weight_sem, load_sem, probs_sem, save_sem, grad_sem, cot_sem, halo_send, halo_recv, hand_send, hand_recv,
):
    section, wide = lax.axis_index("section"), lax.axis_index("wide")
    last_section, last_wide = lax.axis_size("section") - 1, lax.axis_size("wide") - 1
    batches, rows, width = cotangent.shape
    hidden_width = wg.shape[1]
    half = rows // 2
    pairs = width // LANES
    own = pl.ds(rows, rows)
    has_left, has_right = wide > 0, wide < last_wide
    has_before, has_after = section > 0, section < last_section
    is_last = jnp.logical_not(has_after)

    meet([
        (has_left, {"wide": wide - 1}), (has_right, {"wide": wide + 1}),
        (has_before, {"section": section - 1}), (has_after, {"section": section + 1}),
    ])

    weights = ((w_query, wq), (w_key, wk), (w_value, wv), (w_output, wo),
               (w_gate, wg), (w_up, wu), (w_down, wd))
    order = (6, 4, 5, 3, 0, 1, 2)

    def weight_copy(index):
        source, target = weights[index]
        return pltpu.make_async_copy(source.at[0], target, weight_sem.at[index])

    def cot_copy(mb):
        return pltpu.make_async_copy(cotangent.at[mb], gs.at[mb], cot_sem.at[mb])

    loaded = ((slope_in, slope), (silu_in, silu), (mixed_in, mixed), (q_in, qs), (k_in, ks), (v_in, vs), (x_in, xs))

    def load_copy(index, mb):
        source, target = loaded[index]
        return pltpu.make_async_copy(source.at[mb], target.at[mb], load_sem.at[index, mb])

    def probs_copy(mb):
        slot = lax.rem(mb, 2)
        return pltpu.make_async_copy(probs_in.at[mb], probs.at[slot], probs_sem.at[slot])

    def halo_copy(mb):
        return pltpu.make_async_remote_copy(
            halo_out.at[mb], halo_in.at[mb], halo_send.at[mb], halo_recv.at[mb],
            device_id={"wide": wide - 1}, device_id_type=MESH)

    def hand_copy(mb):
        return pltpu.make_async_remote_copy(
            dxs.at[mb], gs.at[mb], hand_send.at[mb], hand_recv.at[mb],
            device_id={"section": section - 1}, device_id_type=MESH)

    def saves(mb):
        listed = ((gs, g_out), (branch, db_out), (slope, dg_out), (silu, du_out), (qs, dq_out), (ks, dk_out), (vs, dv_out))
        return [
            pltpu.make_async_copy(source.at[mb], target.at[mb], save_sem.at[index, mb])
            for index, (source, target) in enumerate(listed)
        ]

    def grad_copy(mb):
        return pltpu.make_async_copy(dxs.at[mb], grad_out.at[mb], grad_sem.at[mb])

    @pl.when(is_last)
    def _():
        for mb in range(batches):
            cot_copy(mb).start()

    weight_copy(6).start()
    load_copy(0, 0).start()
    load_copy(1, 0).start()
    for index in order[1:4]:
        weight_copy(index).start()
    probs_copy(0).start()
    for index in range(2, 7):
        load_copy(index, 0).start()
    for index in order[4:]:
        weight_copy(index).start()
    for mb in range(1, batches):
        for index in range(7):
            load_copy(index, mb).start()

    gains_out[...] = jnp.zeros(gains_out.shape, F32)

    def first_use(mb, *indices):
        @pl.when(mb == 0)
        def _():
            for index in indices:
                weight_copy(index).wait()

    def add_gain(which, product):
        folded = jnp.sum(product.reshape(rows // 8, 8, width), axis=0)
        at = pl.ds(8 * which, 8)
        gains_out[at, :] = gains_out[at, :] + folded

    def step(mb, carry):
        slot = lax.rem(mb, 2)

        @pl.when(mb + 1 < batches)
        def _():
            probs_copy(mb + 1).start()

        @pl.when(is_last)
        def _():
            cot_copy(mb).wait()

        @pl.when(has_after)
        def _():
            hand_copy(mb).wait_recv()

        first_use(mb, 6)
        load_copy(0, mb).wait()
        load_copy(1, mb).wait()
        rows_g = gs[mb]
        for start in range(0, hidden_width, 256):
            at = slice(start, start + 256)
            d_product = dot_nt(rows_g, wd[at, :])
            slope[mb, :, at] = (d_product * slope[mb, :, at].astype(F32)).astype(BF16)
            silu[mb, :, at] = (d_product * silu[mb, :, at].astype(F32)).astype(BF16)
        first_use(mb, 4, 5)
        d_gate, d_up = slope[mb], silu[mb]
        for start in range(0, width, 256):
            at = slice(start, start + 256)
            d_norm[:, at] = dot_nt(d_gate, wg[at, :]) + dot_nt(d_up, wu[at, :])
        load_copy(2, mb).wait()
        scaled, inverse = rms_parts(mixed[mb])
        d_normed = d_norm[...]
        add_gain(1, d_normed * scaled)
        back = rms_back(d_normed * gain_mlp[...], scaled, inverse)
        d_mixed[...] = rows_g.astype(F32) + back
        branch[mb] = d_mixed[...].astype(BF16)
        first_use(mb, 3)
        rows_b = branch[mb]
        for start in range(0, width, 256):
            at = slice(start, start + 256)
            d_att[:, at] = dot_nt(rows_b, wo[at, :]).astype(BF16)

        probs_copy(mb).wait()
        for index in range(3, 7):
            load_copy(index, mb).wait()

        def attend(pair, carry):
            lanes = pl.ds(pl.multiple_of(pair * LANES, LANES), LANES)
            key_pair, value_pair = ks[mb, :, lanes], vs[mb, :, lanes]
            key_turned = key_pair.T
            d_keys, d_values = [], []
            for block in range(2):
                low = block * half
                here = slice(low, low + half)
                band = slice(low, low + 3 * half)
                queries = split_heads(qs[mb, here, lanes])
                d_out = split_heads(d_att[here, lanes])
                probs_b = probs[slot, pair, block]
                weights_f = probs_b.astype(F32)
                d_probs = dot_nt(value_pair[band, :], d_out)
                moved = weights_f * d_probs
                centre = jnp.sum(moved, axis=0, keepdims=True)
                d_scores = (moved - weights_f * centre).astype(BF16)
                d_keys.append(dot(d_scores, queries))
                d_values.append(dot(probs_b, d_out))
                turned = dot(key_turned[:, band], d_scores)
                at = pl.ds(rows + low, half)
                d_query = rope(join_heads(turned) * 0.125, cosine[mb, at, :], sine[mb, at, :], -1)
                qs[mb, here, lanes] = d_query.astype(BF16)

            def overlap(first, second):
                return jnp.concatenate(
                    [first[:half], first[half:] + second[:2 * half], second[2 * half:]], axis=0)

            d_key = rope(overlap(*d_keys), cosine[mb], sine[mb], -1)
            ks[mb, :, lanes] = d_key.astype(BF16)
            vs[mb, :, lanes] = overlap(*d_values).astype(BF16)
            return carry

        lax.fori_loop(0, pairs, attend, 0)

        first_use(mb, 0, 1, 2)
        halo = pl.ds(0, rows)
        d_key, d_value = ks[mb, halo, :], vs[mb, halo, :]
        for start in range(0, width, 256):
            at = slice(start, start + 256)
            part = dot_nt(d_key, wk[at, :]) + dot_nt(d_value, wv[at, :])
            halo_out[mb, :, at] = part.astype(BF16)

        @pl.when(has_left)
        def _():
            halo_copy(mb).start()

        d_query, d_key, d_value = qs[mb], ks[mb, own, :], vs[mb, own, :]
        for start in range(0, width, 256):
            at = slice(start, start + 256)
            d_norm[:, at] = (
                dot_nt(d_query, wq[at, :]) + dot_nt(d_key, wk[at, :]) + dot_nt(d_value, wv[at, :]))
        for copy in saves(mb):
            copy.start()

        @pl.when(has_right)
        def _():
            halo_copy(mb).wait_recv()
            d_norm[...] = d_norm[...] + halo_in[mb].astype(F32)

        scaled, inverse = rms_parts(xs[mb].astype(F32))
        d_normed = d_norm[...]
        add_gain(0, d_normed * scaled)
        back = rms_back(d_normed * gain_attn[...], scaled, inverse)
        dxs[mb] = (d_mixed[...] + back).astype(BF16)

        @pl.when(has_before)
        def _():
            hand_copy(mb).start()

        grad_copy(mb).start()
        return carry

    lax.fori_loop(0, batches, step, 0)

    for mb in range(batches):
        for copy in saves(mb):
            copy.wait()
        grad_copy(mb).wait()

    @pl.when(has_left)
    def _():
        for mb in range(batches):
            halo_copy(mb).wait_send()

    @pl.when(has_before)
    def _():
        for mb in range(batches):
            hand_copy(mb).wait_send()


def run_backward(cotangent, x, q, k, v, probs, mixed, slope, silu, weights, gain_attn, gain_mlp, cosine, sine):
    batches, rows, width = cotangent.shape
    hidden_width = weights[4].shape[2]
    one = (batches, rows, width)
    two = (batches, 2 * rows, width)
    wide = (batches, rows, hidden_width)
    outs = [(one, BF16), (one, BF16), (one, BF16), (wide, BF16), (wide, BF16), (one, BF16), (two, BF16), (two, BF16),
            ((16, width), F32)]
    scratch = [pltpu.VMEM(w.shape[1:], BF16) for w in weights] + [
        pltpu.VMEM(one, BF16),
        pltpu.VMEM(one, BF16),
        pltpu.VMEM(one, BF16),
        pltpu.VMEM(two, BF16),
        pltpu.VMEM(two, BF16),
        pltpu.VMEM((2,) + probs.shape[1:], BF16),
        pltpu.VMEM(one, F32),
        pltpu.VMEM(wide, BF16),
        pltpu.VMEM(wide, BF16),
        pltpu.VMEM(one, BF16),
        pltpu.VMEM(one[1:], BF16),
        pltpu.VMEM(one[1:], F32),
        pltpu.VMEM(one[1:], F32),
        pltpu.VMEM(one, BF16),
        pltpu.VMEM(one, BF16),
        pltpu.VMEM(one, BF16),
        pltpu.SemaphoreType.DMA((7,)),
        pltpu.SemaphoreType.DMA((7, batches)),
        pltpu.SemaphoreType.DMA((2,)),
        pltpu.SemaphoreType.DMA((7, batches)),
    ] + [pltpu.SemaphoreType.DMA((batches,))] * 6
    return pl.pallas_call(
        backward_kernel,
        out_shape=[jax.ShapeDtypeStruct(shape, dtype) for shape, dtype in outs],
        in_specs=[any_spec()] * 16 + [vmem_spec()] * 4,
        out_specs=[any_spec()] * 8 + [vmem_spec()],
        scratch_shapes=scratch,
        compiler_params=pltpu.CompilerParams(
            collective_id=2, has_side_effects=True, vmem_limit_bytes=VMEM_BYTES),
        name="backward",
    )(cotangent, x, q, k, v, probs, mixed, slope, silu, *weights, gain_attn, gain_mlp, cosine, sine)


LAG = 2
SENDS = 4
CHUNK = 256


class Ladder:
    def __init__(self, refs, sems, outer):
        self.dw, self.a_out, self.a_in, self.b_out, self.b_own, self.b_in, self.c_out, self.c_own, self.c_in, self.result = refs
        self.a_send, self.a_recv, self.b_send, self.b_recv, self.c_send, self.c_recv = sems
        wide = lax.axis_index("wide")
        self.outer = outer
        self.core, self.side, self.depth = lax.rem(wide, 2), lax.rem(wide // 2, 2), wide // 4
        self.core_mate = {"wide": wide + 1 - 2 * self.core}
        self.side_mate = {"wide": wide + 2 - 4 * self.side}
        self.column = lax.rem(wide, 4)

    def a_copy(self, j):
        slot = lax.rem(j, SENDS)
        return pltpu.make_async_remote_copy(
            self.a_out.at[slot], self.a_in.at[j], self.a_send.at[slot], self.a_recv.at[j],
            device_id=self.core_mate, device_id_type=MESH)

    def b_copy(self, j):
        slot = lax.rem(j, SENDS)
        return pltpu.make_async_remote_copy(
            self.b_out.at[slot], self.b_in.at[j], self.b_send.at[slot], self.b_recv.at[j],
            device_id=self.side_mate, device_id_type=MESH)

    def c_copy(self, j, step, arriving):
        slot = lax.rem(j, SENDS)
        peer = lax.rem(self.depth + step, self.outer)
        sender = peer if arriving else self.depth
        return pltpu.make_async_remote_copy(
            self.c_out.at[slot, peer], self.c_in.at[j, sender], self.c_send.at[slot, step], self.c_recv.at[j, sender],
            device_id={"wide": peer * 4 + self.column}, device_id_type=MESH)

    def stage_a(self, j):
        slot, held = lax.rem(j, SENDS), lax.rem(j, LAG + 1)

        @pl.when(j >= SENDS)
        def _():
            self.a_copy(j - SENDS).wait_send()

        for index in range(2 * self.outer):
            self.a_out[slot, index] = self.dw[held, 2 * index + 1 - self.core].astype(BF16)
        self.a_copy(j).start()

    def stage_b(self, j):
        slot, held = lax.rem(j, SENDS), lax.rem(j, LAG + 1)

        @pl.when(j >= SENDS)
        def _():
            self.b_copy(j - SENDS).wait_send()

        self.a_copy(j).wait_recv()
        for index in range(self.outer):
            far, near = 2 * index + 1 - self.side, 2 * index + self.side
            self.b_out[slot, index] = (
                self.dw[held, 2 * far + self.core] + self.a_in[j, far].astype(F32)).astype(BF16)
            self.b_own[held, index] = self.dw[held, 2 * near + self.core] + self.a_in[j, near].astype(F32)
        self.b_copy(j).start()

    def stage_c(self, j):
        slot, held = lax.rem(j, SENDS), lax.rem(j, LAG + 1)

        @pl.when(j >= SENDS)
        def _():
            for step in range(1, self.outer):
                self.c_copy(j - SENDS, step, False).wait_send()

        self.b_copy(j).wait_recv()
        for index in range(self.outer):
            self.c_out[slot, index] = (self.b_own[held, index] + self.b_in[j, index].astype(F32)).astype(BF16)
        for step in range(1, self.outer):
            self.c_copy(j, step, False).start()
        self.c_own[held] = self.b_own[held, self.depth] + self.b_in[j, self.depth].astype(F32)

    def stage_d(self, j):
        held = lax.rem(j, LAG + 1)
        total = self.c_own[held]
        for step in range(1, self.outer):
            self.c_copy(j, step, True).wait_recv()
        for step in range(1, self.outer):
            total = total + self.c_in[j, lax.rem(self.depth + step, self.outer)].astype(F32)
        self.result[j] = total

    def drain(self, count):
        for j in range(max(0, count - SENDS), count):
            self.a_copy(j).wait_send()
            self.b_copy(j).wait_send()
            for step in range(1, self.outer):
                self.c_copy(j, step, False).wait_send()


def weight_kernel(
    normed_in, att_in, n2_in, prod_in, g_in, db_in, dg_in, du_in, dq_in, dk_in, dv_in, gains,
    out_m, out_d,
    normed, att, n2, prod, g, turned, turned_halo, turned_prod, dy, *rest,
):
    m_refs, d_refs = rest[:9], rest[9:18]
    m_sems, d_sems = rest[18:24], rest[24:30]
    x_sem, dy_sem = rest[30], rest[31]
    wide, count = lax.axis_index("wide"), lax.axis_size("wide")
    batches, rows, width = g_in.shape
    hidden_width = prod_in.shape[2]
    outer = count // 4
    own = pl.ds(rows, rows)
    m_count, d_count = out_m.shape[0], out_d.shape[0]
    per_wide, per_narrow = hidden_width // CHUNK, width // CHUNK
    ladder_m = Ladder(m_refs + (out_m,), m_sems, outer)
    ladder_d = Ladder(d_refs + (out_d,), d_sems, outer)
    true = wide >= 0
    meet([(true, ladder_m.core_mate), (true, ladder_m.side_mate)] + [
        (true, {"wide": lax.rem(ladder_m.depth + step, outer) * 4 + ladder_m.column}) for step in range(1, outer)])

    loads = ((n2_in, n2), (att_in, att), (normed_in, normed), (prod_in, prod), (g_in, g))

    def x_copy(index):
        source, target = loads[index]
        return pltpu.make_async_copy(source, target, x_sem.at[index])

    kinds = ((dg_in, per_wide), (du_in, per_wide), (db_in, per_narrow), (dq_in, per_narrow), (dk_in, per_narrow), (dv_in, per_narrow))

    def each_load(j, act):
        slot = lax.rem(j, 2)
        base = 0
        for index, (source, parts) in enumerate(kinds):
            @pl.when((j >= base) & (j < base + parts))
            def _(source=source, base=base, index=index):
                lanes = pl.ds(pl.multiple_of((j - base) * CHUNK, CHUNK), CHUNK)
                target = dy.at[slot] if index >= 4 else dy.at[slot, :, own]
                act(pltpu.make_async_copy(source.at[:, :, lanes], target, dy_sem.at[slot]))
            base += parts
        return base

    x_copy(0).start()
    each_load(jnp.int32(0), lambda copy: copy.start())
    for index in range(1, 5):
        x_copy(index).start()

    def turn(source, target, halo):
        for mb in range(batches):
            block = source[mb, :rows] if halo is None else source[mb, halo * rows:(halo + 1) * rows]
            target[:, mb * rows:(mb + 1) * rows] = block.T

    x_copy(0).wait()
    turn(n2, turned.at[0], None)

    kv_first = 2 * per_wide + 2 * per_narrow
    kv_last = kv_first + 2 * per_narrow
    narrow_first = 2 * per_wide

    def compute_m(j):
        slot, held = lax.rem(j, 2), lax.rem(j, LAG + 1)

        @pl.when(j + 1 < kv_last)
        def _():
            each_load(j + 1, lambda copy: copy.start())

        @pl.when(j < kv_last)
        def _():
            each_load(j, lambda copy: copy.wait())
            which = jnp.where(j < narrow_first, 0, jnp.where(j < narrow_first + per_narrow, 1, 2))
            right = dy[slot, :, rows:, :].reshape(batches * rows, CHUNK)
            product = dot(turned[which], right)
            ladder_m.dw[held] = product.reshape(ladder_m.dw.shape[1:])

        @pl.when((j >= kv_first) & (j < kv_last))
        def _():
            right = dy[slot, :, :rows, :].reshape(batches * rows, CHUNK)
            product = dot(turned_halo[...], right)
            ladder_m.dw[held] = ladder_m.dw[held] + product.reshape(ladder_m.dw.shape[1:])

        @pl.when(j == kv_last)
        def _():
            first = jnp.sum(gains[0:8, :], axis=0, keepdims=True)
            second = jnp.sum(gains[8:16, :], axis=0, keepdims=True)
            row = lax.broadcasted_iota(jnp.int32, (LANES, width), 0)
            placed = jnp.where(row == 0, first, jnp.where(row == 1, second, 0.0))
            columns = placed.T
            ladder_m.dw[held] = jnp.concatenate([columns, columns], axis=1).reshape(ladder_m.dw.shape[1:])

    def compute_d(j):
        held = lax.rem(j, LAG + 1)
        lanes = pl.ds(pl.multiple_of(j * LANES, LANES), LANES)
        product = dot(turned_prod[...], g[:, :, lanes].reshape(batches * rows, LANES))
        ladder_d.dw[held] = product.reshape(ladder_d.dw.shape[1:])

    def on_chunk(s, act_m, act_d):
        @pl.when((s >= 0) & (s < narrow_first))
        def _():
            act_m(s)

        @pl.when((s >= narrow_first) & (s < narrow_first + d_count))
        def _():
            act_d(s - narrow_first)

        @pl.when((s >= narrow_first + d_count) & (s < m_count + d_count))
        def _():
            act_m(s - d_count)

    def both(s, name):
        on_chunk(s, getattr(ladder_m, name), getattr(ladder_d, name))

    def step(s, carry):
        @pl.when(s == 4)
        def _():
            x_copy(1).wait()
            turn(att, turned.at[1], None)

        @pl.when(s == 6)
        def _():
            x_copy(2).wait()
            turn(normed, turned.at[2], 1)

        @pl.when(s == 8)
        def _():
            turn(normed, turned_halo, 0)

        @pl.when(s == 10)
        def _():
            x_copy(3).wait()
            x_copy(4).wait()

        for part in range(batches):
            @pl.when(s == 10 + part)
            def _(part=part):
                turned_prod[:, part * rows:(part + 1) * rows] = prod[part].T

        on_chunk(s, compute_m, compute_d)
        both(s, "stage_a")
        both(s - LAG, "stage_b")
        both(s - 2 * LAG, "stage_c")
        both(s - 3 * LAG, "stage_d")
        return carry

    lax.fori_loop(0, m_count + d_count + 3 * LAG, step, 0)
    ladder_m.drain(m_count)
    ladder_d.drain(d_count)


def run_weights(normed, att, n2, prod, g, db, dg, du, dq, dk, dv, gains, count):
    batches, rows, width = g.shape
    hidden_width = prod.shape[2]
    outer = count // 4
    m_count = 2 * (hidden_width // CHUNK) + 4 * (width // CHUNK) + 1
    d_count = width // LANES

    def ladder(chunks, block):
        refs = [
            pltpu.VMEM((LAG + 1, count) + block, F32),
            pltpu.VMEM((SENDS, count // 2) + block, BF16),
            pltpu.VMEM((chunks, count // 2) + block, BF16),
            pltpu.VMEM((SENDS, outer) + block, BF16),
            pltpu.VMEM((LAG + 1, outer) + block, F32),
            pltpu.VMEM((chunks, outer) + block, BF16),
            pltpu.VMEM((SENDS, outer) + block, BF16),
            pltpu.VMEM((LAG + 1,) + block, F32),
            pltpu.VMEM((chunks, outer) + block, BF16),
        ]
        sems = [
            pltpu.SemaphoreType.DMA((SENDS,)),
            pltpu.SemaphoreType.DMA((chunks,)),
            pltpu.SemaphoreType.DMA((SENDS,)),
            pltpu.SemaphoreType.DMA((chunks,)),
            pltpu.SemaphoreType.DMA((SENDS, outer)),
            pltpu.SemaphoreType.DMA((chunks, outer)),
        ]
        return refs, sems

    block_m, block_d = (width // count, CHUNK), (hidden_width // count, LANES)
    m_refs, m_sems = ladder(m_count, block_m)
    d_refs, d_sems = ladder(d_count, block_d)
    tokens = batches * rows
    return pl.pallas_call(
        weight_kernel,
        out_shape=[
            jax.ShapeDtypeStruct((m_count,) + block_m, F32),
            jax.ShapeDtypeStruct((d_count,) + block_d, F32),
        ],
        in_specs=[any_spec()] * 11 + [vmem_spec()],
        out_specs=[vmem_spec()] * 2,
        scratch_shapes=[
            pltpu.VMEM(normed.shape, BF16),
            pltpu.VMEM(att.shape, BF16),
            pltpu.VMEM(n2.shape, BF16),
            pltpu.VMEM(prod.shape, BF16),
            pltpu.VMEM(g.shape, BF16),
            pltpu.VMEM((3, width, tokens), BF16),
            pltpu.VMEM((width, tokens), BF16),
            pltpu.VMEM((hidden_width, tokens), BF16),
            pltpu.VMEM((2, batches, 2 * rows, CHUNK), BF16),
        ] + m_refs + d_refs + m_sems + d_sems + [
            pltpu.SemaphoreType.DMA((5,)),
            pltpu.SemaphoreType.DMA((2,)),
        ],
        compiler_params=pltpu.CompilerParams(
            collective_id=3, has_side_effects=True, vmem_limit_bytes=VMEM_BYTES),
        name="weights",
    )(normed, att, n2, prod, g, db, dg, du, dq, dk, dv, gains)


def summed_weights(normed, att, n2, prod, g, db, dg, du, dq, dk, dv, gains):
    def outer_sum(left, right):
        total = lax.dot_general(
            left, right, (((0, 1), (0, 1)), ((), ())), preferred_element_type=F32)
        return lax.psum_scatter(total[None], "wide", scatter_dimension=1, tiled=True)

    rows = g.shape[1]
    normed_own = normed[:, rows:]
    gain_rows = gains.reshape(2, 8, -1).sum(axis=1)
    gain_parts = [
        lax.psum_scatter(gain_rows[i:i + 1], "wide", scatter_dimension=1, tiled=True) for i in range(2)]
    return (
        outer_sum(normed_own, dq), outer_sum(normed, dk), outer_sum(normed, dv), outer_sum(att, db),
        outer_sum(n2, dg), outer_sum(n2, du), outer_sum(prod, g), *gain_parts,
    )


def weight_grads(normed, att, n2, prod, g, db, dg, du, dq, dk, dv, gains):
    count = lax.axis_size("wide")
    width, hidden_width = g.shape[2], prod.shape[2]
    if count % 4 or width % (16 * count) or hidden_width % (16 * count):
        return summed_weights(normed, att, n2, prod, g, db, dg, du, dq, dk, dv, gains)
    out_m, out_d = run_weights(normed, att, n2, prod, g, db, dg, du, dq, dk, dv, gains, count)

    def spread(chunks):
        return chunks.transpose(1, 0, 2).reshape(1, chunks.shape[1], -1)

    sizes = [hidden_width // CHUNK] * 2 + [width // CHUNK] * 4
    parts, base = [], 0
    for size in sizes:
        parts.append(spread(out_m[base:base + size]))
        base += size
    gate, up, output, query, key, value = parts
    return (
        query, key, value, output, gate, up, spread(out_d),
        out_m[base, :, 0][None], out_m[base, :, 1][None],
    )


def per_device(
    tokens, cotangent, seg_lengths, w_query, w_key, w_value, w_output, w_gate, w_up, w_down, gain_attn, gain_mlp,
):
    weights = (w_query, w_key, w_value, w_output, w_gate, w_up, w_down)
    batches, rows, width = tokens.shape
    start_row = lax.axis_index("wide") * rows
    lengths = seg_lengths.reshape(batches, -1)
    starts = jnp.cumsum(lengths, axis=1) - lengths
    positions = start_row - rows + jnp.arange(2 * rows, dtype=jnp.int32)
    first = jnp.max(
        jnp.where(starts[:, None, :] <= positions[None, :, None], starts[:, None, :], 0), axis=2)
    first_key = (first[:, None, rows:] - start_row).astype(jnp.int32)
    offsets = (positions[None] - first).astype(F32)
    head_dim = width // HEADS
    half_dim = head_dim // 2
    freqs = THETA ** (-jnp.arange(half_dim, dtype=F32) * 2.0 / head_dim)
    angles = offsets[:, :, None] * jnp.tile(freqs, LANES // half_dim)[None, None, :]
    sign = jnp.tile(jnp.repeat(jnp.array([-1.0, 1.0], F32), half_dim), LANES // head_dim)
    cosine, sine = jnp.cos(angles), jnp.sin(angles) * sign

    (block_out, x, normed, q, k, v, probs, att, mixed, n2, slope, silu, prod) = run_forward(
        tokens, weights, gain_attn, gain_mlp, cosine, sine, first_key)
    input_grads, g, db, dg, du, dq, dk, dv, gains = run_backward(
        cotangent, x, q, k, v, probs, mixed, slope, silu, weights, gain_attn, gain_mlp, cosine, sine)
    grads = weight_grads(normed, att, n2, prod, g, db, dg, du, dq, dk, dv, gains)
    return (block_out[None], input_grads[None], *grads)


def solution(mesh):
    in_specs = (
        P(None, "wide", None),
        P(None, "wide", None),
        P(),
        *[P("section", None, None)] * 7,
        *[P("section", None)] * 2,
    )
    out_specs = (
        *[P("section", None, "wide", None)] * 2,
        *[P("section", "wide", None)] * 7,
        *[P("section", "wide")] * 2,
    )
    return jax.shard_map(
        per_device, mesh=mesh, in_specs=in_specs, out_specs=out_specs, check_vma=False
    )
```

```python
import functools

import jax
import jax.numpy as jnp
import ml_dtypes
import numpy as np
from jax import lax
from jax.experimental import pallas as pl
from jax.experimental.pallas import tpu as pltpu
from jax.sharding import PartitionSpec as P

HEADS = 12
EPS = 1e-05
THETA = 10000.0

F32 = jnp.float32
BF16 = jnp.bfloat16
MESH = pl.DeviceIdType.MESH
LANES = 128
BLOCK = 64
VMEM_BYTES = 63 * 1024 * 1024


def dot(left, right):
    return jnp.dot(left, right, preferred_element_type=F32)


def dot_nt(left, right):
    return lax.dot_general(
        left, right, (((1,), (1,)), ((), ())), preferred_element_type=F32
    )


def rms_parts(hidden):
    inverse = lax.rsqrt(jnp.mean(hidden * hidden, axis=1, keepdims=True) + EPS)
    return (hidden * inverse, inverse)


def rms_back(upstream, scaled, inverse):
    return inverse * (upstream - scaled * jnp.mean(upstream * scaled, axis=1, keepdims=True))


def low_half(rows):
    lane = lax.broadcasted_iota(jnp.int32, (rows, LANES), 1)
    return lane % 64 < 32


def rope(field, cosine, sine, direction):
    partner = jnp.where(
        low_half(field.shape[0]),
        pltpu.roll(field, 96, 1),
        pltpu.roll(field, 32, 1),
    )
    if direction > 0:
        return field * cosine + partner * sine
    return field * cosine - partner * sine


def split_heads(block):
    lane = lax.broadcasted_iota(jnp.int32, block.shape, 1)
    zero = jnp.zeros_like(block)
    return jnp.concatenate(
        [jnp.where(lane < 64, block, zero), jnp.where(lane >= 64, block, zero)], axis=0
    )


def join_heads(turned):
    count = turned.shape[1] // 2
    row = lax.broadcasted_iota(jnp.int32, (LANES, count), 0)
    return jnp.where(row < 64, turned[:, :count], turned[:, count:]).T


def meet(partners):
    barrier = pltpu.get_barrier_semaphore()
    total = 0
    for condition, device in partners:

        @pl.when(condition)
        def _(device=device):
            pl.semaphore_signal(barrier, inc=1, device_id=device, device_id_type=MESH)

        total = total + condition.astype(jnp.int32)
    pl.semaphore_wait(barrier, total)


def layers_kernel(
    tokens, cotangent, lengths,
    w_query, w_key, w_value, w_output, w_gate, w_up, w_down,
    gain_attn, gain_mlp, trig,
    block_out, grad_out, normed_out, att_out, n2_out, prod_out,
    g_out, db_out, dg_out, du_out, dq_out, dk_out, dv_out, gains_out,
    wq, wk, wv, wo, wg, wu, wd,
    xs, qs, ks, vs, probs, slope, silu, mixed, normed, att, n2, prod, outs, gs,
    halo_in, halo_out, branch, d_att, d_norm, d_own, cosine, sine, first_key, bias, scale,
    wide_f, left_b, right_b, key_f, value_f,
    weight_sem, trig_sem, token_sem, cot_sem, save_sem, out_sem,
    halo_send, halo_recv, hand_send, hand_recv, back_send, back_recv, turn_send, turn_recv,
):
    section, wide = lax.axis_index("section"), lax.axis_index("wide")
    last_section, last_wide = lax.axis_size("section") - 1, lax.axis_size("wide") - 1
    batches, rows, width = tokens.shape
    hidden_width = wg.shape[1]
    half = rows // 2
    band = rows + half
    pairs = width // LANES
    own, halo = pl.ds(rows, rows), pl.ds(0, rows)
    has_left, has_right = wide > 0, wide < last_wide
    has_before, has_after = section > 0, section < last_section
    is_first, is_last = jnp.logical_not(has_before), jnp.logical_not(has_after)

    weights = ((w_query, wq), (w_key, wk), (w_value, wv), (w_output, wo),
               (w_gate, wg), (w_up, wu), (w_down, wd))

    def weight_copy(index):
        source, target = weights[index]
        return pltpu.make_async_copy(source.at[0], target, weight_sem.at[index])

    def token_copy(mb):
        return pltpu.make_async_copy(tokens.at[mb], xs.at[mb, own], token_sem.at[mb])

    def cot_copy(mb):
        return pltpu.make_async_copy(cotangent.at[mb], gs.at[mb], cot_sem.at[mb])

    def halo_copy(mb, source):
        return pltpu.make_async_remote_copy(
            source, xs.at[mb, halo], halo_send.at[mb], halo_recv.at[mb],
            device_id={"wide": wide + 1}, device_id_type=MESH)

    def hand_copy(mb):
        return pltpu.make_async_remote_copy(
            outs.at[mb], xs.at[mb, own], hand_send.at[mb], hand_recv.at[mb],
            device_id={"section": section + 1}, device_id_type=MESH)

    def back_copy(mb):
        return pltpu.make_async_remote_copy(
            halo_out, halo_in.at[mb], back_send.at[mb], back_recv.at[mb],
            device_id={"wide": wide - 1}, device_id_type=MESH)

    def turn_copy(mb):
        return pltpu.make_async_remote_copy(
            outs.at[mb], gs.at[mb], turn_send.at[mb], turn_recv.at[mb],
            device_id={"section": section - 1}, device_id_type=MESH)

    def out_copy(mb, target):
        return pltpu.make_async_copy(outs.at[mb], target.at[mb], out_sem.at[mb])

    def save(name, mb):
        source, target, index = {
            "normed": (normed, normed_out, 0), "att": (att, att_out, 1), "n2": (n2, n2_out, 2),
            "prod": (prod, prod_out, 3), "branch": (branch.at[lax.rem(mb, 2)], db_out, 4),
            "g": (gs.at[mb], g_out, 5), "dg": (slope.at[mb], dg_out, 6), "du": (silu.at[mb], du_out, 7),
            "dq": (qs.at[mb], dq_out, 8), "dk": (ks.at[mb], dk_out, 9), "dv": (vs.at[mb], dv_out, 10),
        }[name]
        return pltpu.make_async_copy(source, target.at[mb], save_sem.at[index, mb])

    def saved_before(name, mb):
        @pl.when(mb > 0)
        def _():
            save(name, mb - 1).wait()

    @pl.when(is_first)
    def _():
        token_copy(0).start()

    trig_copy = pltpu.make_async_copy(trig, left_b, trig_sem.at[0])
    trig_copy.start()
    for index in range(3):
        weight_copy(index).start()

    meet([
        (has_left, {"wide": wide - 1}), (has_right, {"wide": wide + 1}),
        (has_before, {"section": section - 1}), (has_after, {"section": section + 1}),
    ])

    @pl.when(is_first & has_right)
    def _():
        halo_copy(0, tokens.at[0]).start()

    @pl.when(is_first)
    def _():
        for mb in range(1, batches):
            token_copy(mb).start()

    @pl.when(is_last)
    def _():
        for mb in range(batches):
            cot_copy(mb).start()

    @pl.when(jnp.logical_not(has_left))
    def _():
        xs[:, halo, :] = jnp.zeros((batches, rows, width), BF16)

    gains_out[...] = jnp.zeros(gains_out.shape, F32)

    start_row = wide * rows

    def tables(mb, carry):
        positions = lax.broadcasted_iota(jnp.int32, (2 * rows, LANES), 0) + (start_row - rows)
        query_at = lax.broadcasted_iota(jnp.int32, (8, rows), 1) + start_row

        def later(image, state):
            start, first, first_row = state
            first = jnp.where(positions >= start, start, first)
            first_row = jnp.where(query_at >= start, start, first_row)
            return (start + lengths[mb, image], first, first_row)

        _, first, first_row = lax.fori_loop(
            0, lengths.shape[1], later,
            (jnp.int32(0), jnp.zeros((2 * rows, LANES), jnp.int32), jnp.zeros((8, rows), jnp.int32)))
        offsets = positions - first
        lane = lax.broadcasted_iota(jnp.int32, (2 * rows, LANES), 1)
        one_hot = jnp.concatenate(
            [jnp.where(offsets == lane + base, 1.0, 0.0).astype(BF16) for base in range(0, band, LANES)],
            axis=1)
        for which, table in enumerate((cosine, sine)):
            parts = dot(one_hot, left_b[which])
            table[mb] = parts[:, :LANES] + parts[:, LANES:]
        first_key[mb] = first_row - start_row
        return carry

    trig_copy.wait()
    lax.fori_loop(0, batches, tables, 0)

    items = [(pair, block) for pair in range(pairs) for block in range(2)]

    def place(index):
        pair, block = items[index]
        lanes = slice(pair * LANES, (pair + 1) * LANES)
        low = block * half
        return lanes, slice(low, low + half), slice(low, low + band)

    def pipelined(first, second, third):
        first(0)
        for index in range(len(items)):
            if index + 1 < len(items):
                first(index + 1)
            second(index)
            if index:
                third(index - 1)
        third(len(items) - 1)


    def normalise(mb, part):
        for low in range(part.start, part.start + rows, BLOCK):
            at = slice(low, low + BLOCK)
            scaled, _ = rms_parts(xs[mb, at, :].astype(F32))
            normed[at, :] = (scaled * gain_attn[...]).astype(BF16)

    def keys_values(mb, part):
        cos_rows, sin_rows = cosine[mb, part, :], sine[mb, part, :]
        for start in range(0, width, 256):
            rows_n = normed[part, :]
            keys = dot(rows_n, wk[:, start:start + 256])
            for inner in range(0, 256, LANES):
                ks[mb, part, start + inner:start + inner + LANES] = rope(
                    keys[:, inner:inner + LANES], cos_rows, sin_rows, 1).astype(BF16)
            vs[mb, part, start:start + 256] = dot(rows_n, wv[:, start:start + 256]).astype(BF16)

    def attention(mb):
        def scores(index):
            lanes, here, near = place(index)
            wide_f[index % 2] = dot_nt(ks[mb, near, lanes], split_heads(qs[mb, here, lanes]))

        def soften(index):
            pair, block = items[index]
            for head in range(2):
                at = slice(head * LANES, (head + 1) * LANES)
                masked = wide_f[index % 2, :, at] + bias[block]
                raw = jnp.exp(masked - jnp.max(masked, axis=0, keepdims=True))
                probs[mb, pair, block, :, at] = raw.astype(BF16)

        def collect(index):
            pair, block = items[index]
            lanes, here, near = place(index)
            left = jnp.concatenate([vs[mb, near, lanes].T, jnp.ones((16, band), BF16)], axis=0)
            turned = dot(left, probs[mb, pair, block])
            inverse = 1.0 / turned[LANES:LANES + 1]
            scale[mb, index] = inverse
            att[here, lanes] = join_heads(turned[:LANES] * inverse).astype(BF16)

        pipelined(scores, soften, collect)

    def forward(mb, carry):
        @pl.when(is_first)
        def _():
            token_copy(mb).wait()

            @pl.when(has_right & (mb + 1 < batches))
            def _():
                halo_copy(mb + 1, tokens.at[mb + 1]).start()

        @pl.when(has_before & (mb == 0))
        def _():
            hand_copy(mb).wait_recv()

            @pl.when(has_right)
            def _():
                halo_copy(mb, xs.at[mb, own]).start()

        saved_before("normed", mb)
        normalise(mb, own)

        @pl.when(mb == 0)
        def _():
            for index in range(3):
                weight_copy(index).wait()
            for index in range(3, 7):
                weight_copy(index).start()

        cos_rows, sin_rows = cosine[mb, own, :], sine[mb, own, :]
        for start in range(0, width, 256):
            queries = dot(normed[own, :], wq[:, start:start + 256])
            for inner in range(0, 256, LANES):
                turned = rope(queries[:, inner:inner + LANES], cos_rows, sin_rows, 1)
                qs[mb, :, start + inner:start + inner + LANES] = (turned * 0.125).astype(BF16)
        keys_values(mb, own)
        for block in range(2):
            key_at = lax.broadcasted_iota(jnp.int32, (band, half), 0) + (block * half - rows)
            query_at = lax.broadcasted_iota(jnp.int32, (band, half), 1) + block * half
            first = first_key[mb, 0:1, block * half:(block + 1) * half]
            bias[block] = jnp.where((key_at >= first) & (key_at <= query_at), 0.0, -1e30)

        @pl.when(has_left)
        def _():
            halo_copy(mb, xs.at[mb, own]).wait_recv()

        normalise(mb, halo)
        keys_values(mb, halo)
        save("normed", mb).start()
        saved_before("att", mb)
        attention(mb)
        save("att", mb).start()

        @pl.when(mb == 0)
        def _():
            for index in range(3, 7):
                weight_copy(index).wait()

        saved_before("n2", mb)
        for start in range(0, width, 256):
            at = slice(start, start + 256)
            d_norm[:, at] = xs[mb, own, at].astype(F32) + dot(att[...], wo[:, at])
        for low in range(0, rows, BLOCK):
            at = slice(low, low + BLOCK)
            total = d_norm[at, :]
            scaled, _ = rms_parts(total)
            mixed[mb, at, :] = total.astype(BF16)
            n2[at, :] = (scaled * gain_mlp[...]).astype(BF16)
        save("n2", mb).start()

        @pl.when(has_before & (mb + 1 < batches))
        def _():
            hand_copy(mb + 1).wait_recv()

            @pl.when(has_right)
            def _():
                halo_copy(mb + 1, xs.at[mb + 1, own]).start()

        saved_before("prod", mb)
        for start in range(0, hidden_width, 256):
            at = slice(start, start + 256)
            gate = dot(n2[...], wg[:, at])
            up = dot(n2[...], wu[:, at])
            sigma = jax.nn.sigmoid(gate)
            gated = gate * sigma
            prod[:, at] = (gated * up).astype(BF16)
            silu[mb, :, at] = gated.astype(BF16)
            slope[mb, :, at] = (up * (sigma * (1.0 + gate * (1.0 - sigma)))).astype(BF16)
        save("prod", mb).start()
        for start in range(0, width, 256):
            at = slice(start, start + 256)
            outs[mb, :, at] = (d_norm[:, at] + dot(prod[...], wd[:, at])).astype(BF16)

        @pl.when(has_after)
        def _():
            hand_copy(mb).start()

        out_copy(mb, block_out).start()
        return carry

    lax.fori_loop(0, batches, forward, 0)

    for name in ("normed", "att", "n2", "prod"):
        save(name, batches - 1).wait()
    for mb in range(batches):
        out_copy(mb, block_out).wait()

    @pl.when(has_after)
    def _():
        for mb in range(batches):
            hand_copy(mb).wait_send()


    def add_gain(which, product):
        folded = jnp.sum(product.reshape(product.shape[0] // 8, 8, width), axis=0)
        at = pl.ds(8 * which, 8)
        gains_out[at, :] = gains_out[at, :] + folded

    def attention_back(mb):
        def d_weights(index):
            lanes, here, near = place(index)
            wide_f[index % 2] = dot_nt(vs[mb, near, lanes], split_heads(d_att[here, lanes]))

        def d_soften(index):
            pair, block = items[index]
            for head in range(2):
                at = slice(head * LANES, (head + 1) * LANES)
                weight = probs[mb, pair, block, :, at].astype(F32) * scale[mb, index, :, at]
                moved = weight * wide_f[index % 2, :, at]
                centre = jnp.sum(moved, axis=0, keepdims=True)
                left_b[index % 2, :, at] = (moved - weight * centre).astype(BF16)
                right_b[index % 2, :, at] = weight.astype(BF16)

        def collect(index):
            pair, block = items[index]
            lanes, here, near = place(index)
            d_scores = left_b[index % 2]
            d_keys = dot(d_scores, split_heads(qs[mb, here, lanes]))
            d_values = dot(right_b[index % 2], split_heads(d_att[here, lanes]))
            turned = lax.dot_general(
                ks[mb, near, lanes], d_scores, (((0,), (0,)), ((), ())), preferred_element_type=F32)
            at = pl.ds(rows + block * half, half)
            qs[mb, here, lanes] = rope(
                join_heads(turned) * 0.125, cosine[mb, at, :], sine[mb, at, :], -1).astype(BF16)
            slot = pair % 2
            if block == 0:
                key_f[slot], value_f[slot] = d_keys, d_values
                return
            earlier_k, earlier_v = key_f[slot], value_f[slot]
            pieces = (
                (0, half, earlier_k[:half], earlier_v[:half]),
                (half, band, earlier_k[half:] + d_keys[:rows], earlier_v[half:] + d_values[:rows]),
                (band, 2 * rows, d_keys[rows:], d_values[rows:]),
            )
            for low, high, piece_k, piece_v in pieces:
                ks[mb, low:high, lanes] = rope(
                    piece_k, cosine[mb, low:high, :], sine[mb, low:high, :], -1).astype(BF16)
                vs[mb, low:high, lanes] = piece_v.astype(BF16)

        pipelined(d_weights, d_soften, collect)

    def finish(mb):
        @pl.when(has_right)
        def _():
            back_copy(mb).wait_recv()
            d_own[...] = d_own[...] + halo_in[mb].astype(F32)

        for low in range(0, rows, BLOCK):
            at = slice(low, low + BLOCK)
            scaled, inverse = rms_parts(xs[mb, rows + low:rows + low + BLOCK, :].astype(F32))
            d_normed = d_own[at, :]
            add_gain(0, d_normed * scaled)
            back = rms_back(d_normed * gain_attn[...], scaled, inverse)
            outs[mb, at, :] = (branch[lax.rem(mb, 2), at, :].astype(F32) + back).astype(BF16)

        @pl.when(has_before)
        def _():
            turn_copy(mb).start()

        out_copy(mb, grad_out).start()

    def backward(mb, carry):
        @pl.when(is_last)
        def _():
            cot_copy(mb).wait()

        @pl.when(has_after)
        def _():
            turn_copy(mb).wait_recv()

        save("g", mb).start()
        for start in range(0, hidden_width, 256):
            at = slice(start, start + 256)
            d_product = dot_nt(gs[mb], wd[at, :])
            slope[mb, :, at] = (d_product * slope[mb, :, at].astype(F32)).astype(BF16)
            silu[mb, :, at] = (d_product * silu[mb, :, at].astype(F32)).astype(BF16)
        save("dg", mb).start()
        save("du", mb).start()
        for start in range(0, width, 256):
            at = slice(start, start + 256)
            d_norm[:, at] = dot_nt(slope[mb], wg[at, :]) + dot_nt(silu[mb], wu[at, :])
        slot = lax.rem(mb, 2)

        @pl.when(mb >= 2)
        def _():
            save("branch", mb - 2).wait()

        for low in range(0, rows, BLOCK):
            at = slice(low, low + BLOCK)
            scaled, inverse = rms_parts(mixed[mb, at, :].astype(F32))
            d_normed = d_norm[at, :]
            add_gain(1, d_normed * scaled)
            total = gs[mb, at, :].astype(F32) + rms_back(d_normed * gain_mlp[...], scaled, inverse)
            branch[slot, at, :] = total.astype(BF16)
        save("branch", mb).start()
        for start in range(0, width, 256):
            at = slice(start, start + 256)
            d_att[:, at] = dot_nt(branch[slot], wo[at, :]).astype(BF16)

        @pl.when(mb > 0)
        def _():
            finish(mb - 1)

        attention_back(mb)
        save("dq", mb).start()
        save("dk", mb).start()
        save("dv", mb).start()

        @pl.when(has_left & (mb > 0))
        def _():
            back_copy(mb - 1).wait_send()

        for start in range(0, width, 256):
            at = slice(start, start + 256)
            halo_out[:, at] = (
                dot_nt(ks[mb, halo, :], wk[at, :]) + dot_nt(vs[mb, halo, :], wv[at, :])).astype(BF16)

        @pl.when(has_left)
        def _():
            back_copy(mb).start()

        for start in range(0, width, 256):
            at = slice(start, start + 256)
            d_own[:, at] = (
                dot_nt(qs[mb], wq[at, :]) + dot_nt(ks[mb, own, :], wk[at, :])
                + dot_nt(vs[mb, own, :], wv[at, :]))
        return carry

    lax.fori_loop(0, batches, backward, 0)
    finish(batches - 1)

    for mb in range(batches - 2, batches):
        save("branch", mb).wait()
    for mb in range(batches):
        for name in ("g", "dg", "du", "dq", "dk", "dv"):
            save(name, mb).wait()
        out_copy(mb, grad_out).wait()

    @pl.when(has_left)
    def _():
        back_copy(batches - 1).wait_send()

    @pl.when(has_before)
    def _():
        for mb in range(batches):
            turn_copy(mb).wait_send()

    @pl.when(has_right)
    def _():
        for mb in range(batches):
            halo_copy(mb, xs.at[mb, own]).wait_send()


def any_spec():
    return pl.BlockSpec(memory_space=pl.ANY)


def vmem_spec():
    return pl.BlockSpec(memory_space=pltpu.VMEM)


def trig_table(head_dim, reach):
    half_dim = head_dim // 2
    freqs = np.float32(THETA) ** (-np.arange(half_dim, dtype=np.float32) * np.float32(2.0) / np.float32(head_dim))
    angles = np.arange(reach, dtype=np.float32)[:, None] * np.tile(freqs, LANES // half_dim)[None, :]
    sign = np.tile(np.repeat(np.array([-1.0, 1.0], np.float32), half_dim), LANES // head_dim)
    parts = []
    for table in (np.cos(angles), np.sin(angles) * sign):
        high = table.astype(ml_dtypes.bfloat16)
        low = (table - high.astype(np.float32)).astype(ml_dtypes.bfloat16)
        parts.append(np.concatenate([high, low], axis=1))
    return jnp.asarray(np.stack(parts))


def run_layers(tokens, cotangent, lengths, weights, gain_attn, gain_mlp):
    batches, rows, width = tokens.shape
    hidden_width = weights[4].shape[2]
    pairs = width // LANES
    band = rows + rows // 2
    one = (batches, rows, width)
    two = (batches, 2 * rows, width)
    wide = (batches, rows, hidden_width)
    outs = [(one, BF16), (one, BF16), (two, BF16), (one, BF16), (one, BF16), (wide, BF16),
            (one, BF16), (one, BF16), (wide, BF16), (wide, BF16), (one, BF16), (two, BF16), (two, BF16),
            ((16, width), F32)]
    dma = pltpu.SemaphoreType.DMA
    scratch = [pltpu.VMEM(w.shape[1:], BF16) for w in weights] + [
        pltpu.VMEM(two, BF16),
        pltpu.VMEM(one, BF16),
        pltpu.VMEM(two, BF16),
        pltpu.VMEM(two, BF16),
        pltpu.VMEM((batches, pairs, 2, band, rows), BF16),
        pltpu.VMEM(wide, BF16),
        pltpu.VMEM(wide, BF16),
        pltpu.VMEM(one, BF16),
        pltpu.VMEM(two[1:], BF16),
        pltpu.VMEM(one[1:], BF16),
        pltpu.VMEM(one[1:], BF16),
        pltpu.VMEM(wide[1:], BF16),
        pltpu.VMEM(one, BF16),
        pltpu.VMEM(one, BF16),
        pltpu.VMEM(one, BF16),
        pltpu.VMEM(one[1:], BF16),
        pltpu.VMEM((2,) + one[1:], BF16),
        pltpu.VMEM(one[1:], BF16),
        pltpu.VMEM(one[1:], F32),
        pltpu.VMEM(one[1:], F32),
        pltpu.VMEM((batches, 2 * rows, LANES), F32),
        pltpu.VMEM((batches, 2 * rows, LANES), F32),
        pltpu.VMEM((batches, 8, rows), jnp.int32),
        pltpu.VMEM((2, band, rows // 2), F32),
        pltpu.VMEM((batches, 2 * pairs, 1, rows), F32),
        pltpu.VMEM((2, band, rows), F32),
        pltpu.VMEM((2, band, rows), BF16),
        pltpu.VMEM((2, band, rows), BF16),
        pltpu.VMEM((2, band, LANES), F32),
        pltpu.VMEM((2, band, LANES), F32),
        dma((7,)), dma((1,)), dma((batches,)), dma((batches,)), dma((11, batches)),
    ] + [dma((batches,))] * 9
    trig = trig_table(width // HEADS, band)
    return pl.pallas_call(
        layers_kernel,
        out_shape=[jax.ShapeDtypeStruct(shape, dtype) for shape, dtype in outs],
        in_specs=[any_spec()] * 2 + [pl.BlockSpec(memory_space=pltpu.SMEM)] + [any_spec()] * 7 + [vmem_spec()] * 2 + [any_spec()],
        out_specs=[any_spec()] * 13 + [vmem_spec()],
        scratch_shapes=scratch,
        compiler_params=pltpu.CompilerParams(
            collective_id=1, has_side_effects=True, vmem_limit_bytes=VMEM_BYTES),
        name="layers",
    )(tokens, cotangent, lengths, *weights, gain_attn, gain_mlp, trig)


LAG = 2
SENDS = 4
CHUNK = 256


def dot_tn(left, right):
    return lax.dot_general(
        left, right, (((0,), (0,)), ((), ())), preferred_element_type=F32
    )


class Ladder:
    def __init__(self, refs, sems, outer):
        self.dw, self.a_out, self.a_in, self.b_out, self.b_own, self.b_in, self.c_out, self.c_own, self.c_in, self.result = refs
        self.a_send, self.a_recv, self.b_send, self.b_recv, self.c_send, self.c_recv = sems
        wide = lax.axis_index("wide")
        self.outer = outer
        self.core, self.side, self.depth = lax.rem(wide, 2), lax.rem(wide // 2, 2), wide // 4
        self.core_mate = {"wide": wide + 1 - 2 * self.core}
        self.side_mate = {"wide": wide + 2 - 4 * self.side}
        self.column = lax.rem(wide, 4)

    def a_copy(self, j):
        slot = lax.rem(j, SENDS)
        return pltpu.make_async_remote_copy(
            self.a_out.at[slot], self.a_in.at[j], self.a_send.at[slot], self.a_recv.at[j],
            device_id=self.core_mate, device_id_type=MESH)

    def b_copy(self, j):
        slot = lax.rem(j, SENDS)
        return pltpu.make_async_remote_copy(
            self.b_out.at[slot], self.b_in.at[j], self.b_send.at[slot], self.b_recv.at[j],
            device_id=self.side_mate, device_id_type=MESH)

    def c_copy(self, j, step, arriving):
        slot = lax.rem(j, SENDS)
        peer = lax.rem(self.depth + step, self.outer)
        sender = peer if arriving else self.depth
        return pltpu.make_async_remote_copy(
            self.c_out.at[slot, peer], self.c_in.at[j, sender], self.c_send.at[slot, step], self.c_recv.at[j, sender],
            device_id={"wide": peer * 4 + self.column}, device_id_type=MESH)

    def stage_a(self, j):
        slot, held = lax.rem(j, SENDS), lax.rem(j, LAG + 1)

        @pl.when(j >= SENDS)
        def _():
            self.a_copy(j - SENDS).wait_send()

        for index in range(2 * self.outer):
            self.a_out[slot, index] = self.dw[held, 2 * index + 1 - self.core].astype(BF16)
        self.a_copy(j).start()

    def stage_b(self, j):
        slot, held = lax.rem(j, SENDS), lax.rem(j, LAG + 1)

        @pl.when(j >= SENDS)
        def _():
            self.b_copy(j - SENDS).wait_send()

        self.a_copy(j).wait_recv()
        for index in range(self.outer):
            far, near = 2 * index + 1 - self.side, 2 * index + self.side
            self.b_out[slot, index] = (
                self.dw[held, 2 * far + self.core] + self.a_in[j, far].astype(F32)).astype(BF16)
            self.b_own[held, index] = self.dw[held, 2 * near + self.core] + self.a_in[j, near].astype(F32)
        self.b_copy(j).start()

    def stage_c(self, j):
        slot, held = lax.rem(j, SENDS), lax.rem(j, LAG + 1)

        @pl.when(j >= SENDS)
        def _():
            for step in range(1, self.outer):
                self.c_copy(j - SENDS, step, False).wait_send()

        self.b_copy(j).wait_recv()
        for index in range(self.outer):
            self.c_out[slot, index] = (self.b_own[held, index] + self.b_in[j, index].astype(F32)).astype(BF16)
        for step in range(1, self.outer):
            self.c_copy(j, step, False).start()
        self.c_own[held] = self.b_own[held, self.depth] + self.b_in[j, self.depth].astype(F32)

    def stage_d(self, j):
        held = lax.rem(j, LAG + 1)
        total = self.c_own[held]
        for step in range(1, self.outer):
            self.c_copy(j, step, True).wait_recv()
        for step in range(1, self.outer):
            total = total + self.c_in[j, lax.rem(self.depth + step, self.outer)].astype(F32)
        self.result[j] = total

    def drain(self, count):
        for j in range(max(0, count - SENDS), count):
            self.a_copy(j).wait_send()
            self.b_copy(j).wait_send()
            for step in range(1, self.outer):
                self.c_copy(j, step, False).wait_send()


def weight_kernel(
    normed_in, att_in, n2_in, prod_in, g_in, db_in, dg_in, du_in, dq_in, dk_in, dv_in, gains,
    out_m, out_d,
    normed, att, n2, prod, g, dy, *rest,
):
    m_refs, d_refs = rest[:9], rest[9:18]
    m_sems, d_sems = rest[18:24], rest[24:30]
    x_sem, dy_sem = rest[30], rest[31]
    wide, count = lax.axis_index("wide"), lax.axis_size("wide")
    batches, rows, width = g_in.shape
    hidden_width = prod_in.shape[2]
    outer = count // 4
    own = pl.ds(rows, rows)
    m_count, d_count = out_m.shape[0], out_d.shape[0]
    per_wide, per_narrow = hidden_width // CHUNK, width // CHUNK
    ladder_m = Ladder(m_refs + (out_m,), m_sems, outer)
    ladder_d = Ladder(d_refs + (out_d,), d_sems, outer)
    true = wide >= 0
    meet([(true, ladder_m.core_mate), (true, ladder_m.side_mate)] + [
        (true, {"wide": lax.rem(ladder_m.depth + step, outer) * 4 + ladder_m.column}) for step in range(1, outer)])

    loads = ((n2_in, n2), (att_in, att), (normed_in, normed), (prod_in, prod), (g_in, g))

    def x_copy(index):
        source, target = loads[index]
        return pltpu.make_async_copy(source, target, x_sem.at[index])

    kinds = ((dg_in, per_wide), (du_in, per_wide), (db_in, per_narrow), (dq_in, per_narrow), (dk_in, per_narrow), (dv_in, per_narrow))

    def each_load(j, act):
        slot = lax.rem(j, 2)
        base = 0
        for index, (source, parts) in enumerate(kinds):
            @pl.when((j >= base) & (j < base + parts))
            def _(source=source, base=base, index=index):
                lanes = pl.ds(pl.multiple_of((j - base) * CHUNK, CHUNK), CHUNK)
                target = dy.at[slot] if index >= 4 else dy.at[slot, :, own]
                act(pltpu.make_async_copy(source.at[:, :, lanes], target, dy_sem.at[slot]))
            base += parts
        return base

    x_copy(0).start()
    each_load(jnp.int32(0), lambda copy: copy.start())
    for index in range(1, 5):
        x_copy(index).start()

    kv_first = 2 * per_wide + 2 * per_narrow
    kv_last = kv_first + 2 * per_narrow
    narrow_first = 2 * per_wide

    def compute_m(j):
        slot, held = lax.rem(j, 2), lax.rem(j, LAG + 1)

        @pl.when(j + 1 < kv_last)
        def _():
            each_load(j + 1, lambda copy: copy.start())

        def write(left, right):
            product = dot_tn(left.reshape(-1, width), right.reshape(-1, CHUNK))
            ladder_m.dw[held] = product.reshape(ladder_m.dw.shape[1:])

        @pl.when(j < kv_last)
        def _():
            each_load(j, lambda copy: copy.wait())

        @pl.when(j < narrow_first)
        def _():
            write(n2[...], dy[slot, :, own, :])

        @pl.when((j >= narrow_first) & (j < narrow_first + per_narrow))
        def _():
            write(att[...], dy[slot, :, own, :])

        @pl.when((j >= narrow_first + per_narrow) & (j < kv_first))
        def _():
            write(normed[:, own, :], dy[slot, :, own, :])

        @pl.when((j >= kv_first) & (j < kv_last))
        def _():
            write(normed[...], dy[slot])

        @pl.when(j == kv_last)
        def _():
            first = jnp.sum(gains[0:8, :], axis=0, keepdims=True)
            second = jnp.sum(gains[8:16, :], axis=0, keepdims=True)
            row = lax.broadcasted_iota(jnp.int32, (LANES, width), 0)
            placed = jnp.where(row == 0, first, jnp.where(row == 1, second, 0.0))
            columns = placed.T
            ladder_m.dw[held] = jnp.concatenate([columns, columns], axis=1).reshape(ladder_m.dw.shape[1:])

    def compute_d(j):
        held = lax.rem(j, LAG + 1)
        lanes = pl.ds(pl.multiple_of(j * LANES, LANES), LANES)
        product = dot_tn(prod[...].reshape(-1, hidden_width), g[:, :, lanes].reshape(-1, LANES))
        ladder_d.dw[held] = product.reshape(ladder_d.dw.shape[1:])

    def on_chunk(s, act_m, act_d):
        @pl.when((s >= 0) & (s < narrow_first))
        def _():
            act_m(s)

        @pl.when((s >= narrow_first) & (s < narrow_first + d_count))
        def _():
            act_d(s - narrow_first)

        @pl.when((s >= narrow_first + d_count) & (s < m_count + d_count))
        def _():
            act_m(s - d_count)

    def both(s, name):
        on_chunk(s, getattr(ladder_m, name), getattr(ladder_d, name))

    def step(s, carry):
        for index, first_step in enumerate((0, narrow_first + d_count, narrow_first + d_count + per_narrow)):
            @pl.when(s == first_step)
            def _(index=index):
                x_copy(index).wait()

        @pl.when(s == narrow_first)
        def _():
            x_copy(3).wait()
            x_copy(4).wait()

        on_chunk(s, compute_m, compute_d)
        both(s, "stage_a")
        both(s - LAG, "stage_b")
        both(s - 2 * LAG, "stage_c")
        both(s - 3 * LAG, "stage_d")
        return carry

    lax.fori_loop(0, m_count + d_count + 3 * LAG, step, 0)
    ladder_m.drain(m_count)
    ladder_d.drain(d_count)


def run_weights(normed, att, n2, prod, g, db, dg, du, dq, dk, dv, gains, count):
    batches, rows, width = g.shape
    hidden_width = prod.shape[2]
    outer = count // 4
    m_count = 2 * (hidden_width // CHUNK) + 4 * (width // CHUNK) + 1
    d_count = width // LANES

    def ladder(chunks, block):
        refs = [
            pltpu.VMEM((LAG + 1, count) + block, F32),
            pltpu.VMEM((SENDS, count // 2) + block, BF16),
            pltpu.VMEM((chunks, count // 2) + block, BF16),
            pltpu.VMEM((SENDS, outer) + block, BF16),
            pltpu.VMEM((LAG + 1, outer) + block, F32),
            pltpu.VMEM((chunks, outer) + block, BF16),
            pltpu.VMEM((SENDS, outer) + block, BF16),
            pltpu.VMEM((LAG + 1,) + block, F32),
            pltpu.VMEM((chunks, outer) + block, BF16),
        ]
        sems = [
            pltpu.SemaphoreType.DMA((SENDS,)),
            pltpu.SemaphoreType.DMA((chunks,)),
            pltpu.SemaphoreType.DMA((SENDS,)),
            pltpu.SemaphoreType.DMA((chunks,)),
            pltpu.SemaphoreType.DMA((SENDS, outer)),
            pltpu.SemaphoreType.DMA((chunks, outer)),
        ]
        return refs, sems

    block_m, block_d = (width // count, CHUNK), (hidden_width // count, LANES)
    m_refs, m_sems = ladder(m_count, block_m)
    d_refs, d_sems = ladder(d_count, block_d)
    return pl.pallas_call(
        weight_kernel,
        out_shape=[
            jax.ShapeDtypeStruct((m_count,) + block_m, F32),
            jax.ShapeDtypeStruct((d_count,) + block_d, F32),
        ],
        in_specs=[any_spec()] * 11 + [vmem_spec()],
        out_specs=[vmem_spec()] * 2,
        scratch_shapes=[
            pltpu.VMEM(normed.shape, BF16),
            pltpu.VMEM(att.shape, BF16),
            pltpu.VMEM(n2.shape, BF16),
            pltpu.VMEM(prod.shape, BF16),
            pltpu.VMEM(g.shape, BF16),
            pltpu.VMEM((2, batches, 2 * rows, CHUNK), BF16),
        ] + m_refs + d_refs + m_sems + d_sems + [
            pltpu.SemaphoreType.DMA((5,)),
            pltpu.SemaphoreType.DMA((2,)),
        ],
        compiler_params=pltpu.CompilerParams(
            collective_id=3, has_side_effects=True, vmem_limit_bytes=VMEM_BYTES),
        name="weights",
    )(normed, att, n2, prod, g, db, dg, du, dq, dk, dv, gains)


def summed_weights(normed, att, n2, prod, g, db, dg, du, dq, dk, dv, gains):
    def outer_sum(left, right):
        total = lax.dot_general(
            left, right, (((0, 1), (0, 1)), ((), ())), preferred_element_type=F32)
        return lax.psum_scatter(total[None], "wide", scatter_dimension=1, tiled=True)

    rows = g.shape[1]
    normed_own = normed[:, rows:]
    gain_rows = gains.reshape(2, 8, -1).sum(axis=1)
    gain_parts = [
        lax.psum_scatter(gain_rows[i:i + 1], "wide", scatter_dimension=1, tiled=True) for i in range(2)]
    return (
        outer_sum(normed_own, dq), outer_sum(normed, dk), outer_sum(normed, dv), outer_sum(att, db),
        outer_sum(n2, dg), outer_sum(n2, du), outer_sum(prod, g), *gain_parts,
    )


def arrange_kernel(sizes, block, grads, chunks_m, chunks_d, block_out, grad_out, *rest):
    outs, gains, gain_sem, sem = rest[:9], rest[9], rest[10], rest[11]
    base, copies = 0, []
    for size, index in zip(sizes, (4, 5, 3, 0, 1, 2)):
        for part in range(size):
            copies.append((chunks_m.at[base + part], outs[index].at[0, :, pl.ds(part * CHUNK, CHUNK)]))
        base += size
    for part in range(chunks_d.shape[0]):
        copies.append((chunks_d.at[part], outs[6].at[0, :, pl.ds(part * LANES, LANES)]))
    copies += [(block, block_out.at[0]), (grads, grad_out.at[0])]
    started = [pltpu.make_async_copy(source, target, sem.at[index]) for index, (source, target) in enumerate(copies)]
    gain_copy = pltpu.make_async_copy(chunks_m.at[base, :, pl.ds(0, LANES)], gains, gain_sem.at[0])
    gain_copy.start()
    for copy in reversed(started):
        copy.start()
    gain_copy.wait()
    turned = gains[...].T
    outs[7][...] = turned[0:1, :]
    outs[8][...] = turned[1:2, :]
    for copy in started:
        copy.wait()


def arrange(block, grads, chunks_m, chunks_d, sizes):
    own, own_d = chunks_m.shape[1], chunks_d.shape[1]
    width, hidden_width = block.shape[2], CHUNK * sizes[0]
    shapes = [(1,) + block.shape] * 2
    narrow, broad = (1, own, width), (1, own, hidden_width)
    matrices = [narrow] * 4 + [broad] * 2 + [(1, own_d, width)]
    out_shape = [jax.ShapeDtypeStruct(shape, BF16) for shape in shapes]
    out_shape += [jax.ShapeDtypeStruct(shape, F32) for shape in matrices + [(1, own)] * 2]
    copies = sum(sizes) + chunks_d.shape[0] + 2
    return pl.pallas_call(
        functools.partial(arrange_kernel, sizes),
        out_shape=out_shape,
        in_specs=[any_spec()] * 4,
        out_specs=[any_spec()] * 9 + [vmem_spec()] * 2,
        scratch_shapes=[
            pltpu.VMEM((own, LANES), F32),
            pltpu.SemaphoreType.DMA((1,)),
            pltpu.SemaphoreType.DMA((copies,)),
        ],
        compiler_params=pltpu.CompilerParams(vmem_limit_bytes=VMEM_BYTES),
        name="arrange",
    )(block, grads, chunks_m, chunks_d)


def weight_grads(block_out, input_grads, normed, att, n2, prod, g, db, dg, du, dq, dk, dv, gains):
    count = lax.axis_size("wide")
    width, hidden_width = g.shape[2], prod.shape[2]
    if count % 4 or width % (16 * count) or hidden_width % (16 * count):
        grads = summed_weights(normed, att, n2, prod, g, db, dg, du, dq, dk, dv, gains)
        return (block_out[None], input_grads[None], *grads)
    out_m, out_d = run_weights(normed, att, n2, prod, g, db, dg, du, dq, dk, dv, gains, count)
    sizes = (hidden_width // CHUNK,) * 2 + (width // CHUNK,) * 4
    return tuple(arrange(block_out, input_grads, out_m, out_d, sizes))


def per_device(
    tokens, cotangent, seg_lengths, w_query, w_key, w_value, w_output, w_gate, w_up, w_down, gain_attn, gain_mlp,
):
    weights = (w_query, w_key, w_value, w_output, w_gate, w_up, w_down)
    lengths = seg_lengths.reshape(seg_lengths.shape[0], -1)
    (block_out, input_grads, normed, att, n2, prod, g, db, dg, du, dq, dk, dv, gains) = run_layers(
        tokens, cotangent, lengths, weights, gain_attn, gain_mlp)
    return weight_grads(block_out, input_grads, normed, att, n2, prod, g, db, dg, du, dq, dk, dv, gains)


def solution(mesh):
    in_specs = (
        P(None, "wide", None),
        P(None, "wide", None),
        P(),
        *[P("section", None, None)] * 7,
        *[P("section", None)] * 2,
    )
    out_specs = (
        *[P("section", None, "wide", None)] * 2,
        *[P("section", "wide", None)] * 7,
        *[P("section", "wide")] * 2,
    )
    return jax.shard_map(
        per_device, mesh=mesh, in_specs=in_specs, out_specs=out_specs, check_vma=False
    )
```

```python
import functools

import jax
import jax.numpy as jnp
import ml_dtypes
import numpy as np
from jax import lax
from jax.experimental import pallas as pl
from jax.experimental.pallas import tpu as pltpu
from jax.sharding import PartitionSpec as P

HEADS = 12
EPS = 1e-05
THETA = 10000.0

F32 = jnp.float32
BF16 = jnp.bfloat16
MESH = pl.DeviceIdType.MESH
LANES = 128
BLOCK = 64
VMEM_BYTES = 63 * 1024 * 1024


def dot(left, right):
    return jnp.dot(left, right, preferred_element_type=F32)


def dot_nt(left, right):
    return lax.dot_general(
        left, right, (((1,), (1,)), ((), ())), preferred_element_type=F32
    )


def rms_parts(hidden):
    inverse = lax.rsqrt(jnp.mean(hidden * hidden, axis=1, keepdims=True) + EPS)
    return (hidden * inverse, inverse)


def rms_back(upstream, scaled, inverse):
    return inverse * (upstream - scaled * jnp.mean(upstream * scaled, axis=1, keepdims=True))


def low_half(rows):
    lane = lax.broadcasted_iota(jnp.int32, (rows, LANES), 1)
    return lane % 64 < 32


def rope(field, cosine, sine, direction):
    partner = jnp.where(
        low_half(field.shape[0]),
        pltpu.roll(field, 96, 1),
        pltpu.roll(field, 32, 1),
    )
    if direction > 0:
        return field * cosine + partner * sine
    return field * cosine - partner * sine


def split_heads(block):
    lane = lax.broadcasted_iota(jnp.int32, block.shape, 1)
    zero = jnp.zeros_like(block)
    return jnp.concatenate(
        [jnp.where(lane < 64, block, zero), jnp.where(lane >= 64, block, zero)], axis=0
    )


def join_heads(turned):
    count = turned.shape[1] // 2
    row = lax.broadcasted_iota(jnp.int32, (LANES, count), 0)
    return jnp.where(row < 64, turned[:, :count], turned[:, count:]).T


def meet(partners):
    barrier = pltpu.get_barrier_semaphore()
    total = 0
    for condition, device in partners:

        @pl.when(condition)
        def _(device=device):
            pl.semaphore_signal(barrier, inc=1, device_id=device, device_id_type=MESH)

        total = total + condition.astype(jnp.int32)
    pl.semaphore_wait(barrier, total)


def layers_kernel(
    tokens, cotangent, lengths,
    w_query, w_key, w_value, w_output, w_gate, w_up, w_down,
    gain_attn, gain_mlp, trig,
    block_out, grad_out, normed_out, att_out, n2_out, prod_out,
    g_out, db_out, dg_out, du_out, dq_out, dk_out, dv_out, gains_out,
    wq, wk, wv, wo, wg, wu, wd,
    xs, qs, ks, vs, probs, slope, silu, mixed, normed, att, n2, prod, outs, gs,
    halo_in, halo_out, branch, d_att, d_norm, d_own, cosine, sine, first_key, bias, scale,
    wide_f, left_b, right_b, key_f, value_f,
    weight_sem, trig_sem, token_sem, cot_sem, save_sem, out_sem,
    halo_send, halo_recv, hand_send, hand_recv, back_send, back_recv, turn_send, turn_recv,
):
    section, wide = lax.axis_index("section"), lax.axis_index("wide")
    last_section, last_wide = lax.axis_size("section") - 1, lax.axis_size("wide") - 1
    batches, rows, width = tokens.shape
    hidden_width = wg.shape[1]
    half = rows // 2
    band = rows + half
    pairs = width // LANES
    own, halo = pl.ds(rows, rows), pl.ds(0, rows)
    has_left, has_right = wide > 0, wide < last_wide
    has_before, has_after = section > 0, section < last_section
    is_first, is_last = jnp.logical_not(has_before), jnp.logical_not(has_after)

    weights = ((w_query, wq), (w_key, wk), (w_value, wv), (w_output, wo),
               (w_gate, wg), (w_up, wu), (w_down, wd))

    def weight_copy(index):
        source, target = weights[index]
        return pltpu.make_async_copy(source.at[0], target, weight_sem.at[index])

    def token_copy(mb):
        return pltpu.make_async_copy(tokens.at[mb], xs.at[mb, own], token_sem.at[mb])

    def cot_copy(mb):
        return pltpu.make_async_copy(cotangent.at[mb], gs.at[mb], cot_sem.at[mb])

    def halo_copy(mb, source):
        return pltpu.make_async_remote_copy(
            source, xs.at[mb, halo], halo_send.at[mb], halo_recv.at[mb],
            device_id={"wide": wide + 1}, device_id_type=MESH)

    def hand_copy(mb):
        return pltpu.make_async_remote_copy(
            outs.at[mb], xs.at[mb, own], hand_send.at[mb], hand_recv.at[mb],
            device_id={"section": section + 1}, device_id_type=MESH)

    def back_copy(mb):
        return pltpu.make_async_remote_copy(
            halo_out, halo_in.at[mb], back_send.at[mb], back_recv.at[mb],
            device_id={"wide": wide - 1}, device_id_type=MESH)

    def turn_copy(mb):
        return pltpu.make_async_remote_copy(
            outs.at[mb], gs.at[mb], turn_send.at[mb], turn_recv.at[mb],
            device_id={"section": section - 1}, device_id_type=MESH)

    def out_copy(mb, target):
        return pltpu.make_async_copy(outs.at[mb], target.at[mb], out_sem.at[mb])

    def save(name, mb):
        source, target, index = {
            "normed": (normed, normed_out, 0), "att": (att, att_out, 1), "n2": (n2, n2_out, 2),
            "prod": (prod, prod_out, 3), "branch": (branch.at[lax.rem(mb, 2)], db_out, 4),
            "g": (gs.at[mb], g_out, 5), "dg": (slope.at[mb], dg_out, 6), "du": (silu.at[mb], du_out, 7),
            "dq": (qs.at[mb], dq_out, 8), "dk": (ks.at[mb], dk_out, 9), "dv": (vs.at[mb], dv_out, 10),
        }[name]
        return pltpu.make_async_copy(source, target.at[mb], save_sem.at[index, mb])

    def saved_before(name, mb):
        @pl.when(mb > 0)
        def _():
            save(name, mb - 1).wait()

    @pl.when(is_first)
    def _():
        token_copy(0).start()

    trig_copy = pltpu.make_async_copy(trig, left_b, trig_sem.at[0])
    trig_copy.start()
    for index in range(3):
        weight_copy(index).start()

    meet([
        (has_left, {"wide": wide - 1}), (has_right, {"wide": wide + 1}),
        (has_before, {"section": section - 1}), (has_after, {"section": section + 1}),
    ])

    @pl.when(is_first & has_right)
    def _():
        halo_copy(0, tokens.at[0]).start()

    @pl.when(is_first)
    def _():
        for mb in range(1, batches):
            token_copy(mb).start()

    @pl.when(is_last)
    def _():
        for mb in range(batches):
            cot_copy(mb).start()

    @pl.when(jnp.logical_not(has_left))
    def _():
        xs[:, halo, :] = jnp.zeros((batches, rows, width), BF16)

    gains_out[...] = jnp.zeros(gains_out.shape, F32)

    start_row = wide * rows

    def tables(mb, carry):
        positions = lax.broadcasted_iota(jnp.int32, (2 * rows, LANES), 0) + (start_row - rows)
        query_at = lax.broadcasted_iota(jnp.int32, (8, rows), 1) + start_row

        def later(image, state):
            start, first, first_row = state
            first = jnp.where(positions >= start, start, first)
            first_row = jnp.where(query_at >= start, start, first_row)
            return (start + lengths[mb, image], first, first_row)

        _, first, first_row = lax.fori_loop(
            0, lengths.shape[1], later,
            (jnp.int32(0), jnp.zeros((2 * rows, LANES), jnp.int32), jnp.zeros((8, rows), jnp.int32)))
        offsets = positions - first
        lane = lax.broadcasted_iota(jnp.int32, (2 * rows, LANES), 1)
        one_hot = jnp.concatenate(
            [jnp.where(offsets == lane + base, 1.0, 0.0).astype(BF16) for base in range(0, band, LANES)],
            axis=1)
        for which, table in enumerate((cosine, sine)):
            parts = dot(one_hot, left_b[which])
            table[mb] = parts[:, :LANES] + parts[:, LANES:]
        first_key[mb] = first_row - start_row
        return carry

    trig_copy.wait()
    lax.fori_loop(0, batches, tables, 0)

    items = [(pair, block) for pair in range(pairs) for block in range(2)]

    def place(index):
        pair, block = items[index]
        lanes = slice(pair * LANES, (pair + 1) * LANES)
        low = block * half
        return lanes, slice(low, low + half), slice(low, low + band)

    def pipelined(first, second, third):
        first(0)
        for index in range(len(items)):
            if index + 1 < len(items):
                first(index + 1)
            second(index)
            if index:
                third(index - 1)
        third(len(items) - 1)


    def normalise(mb, part):
        for low in range(part.start, part.start + rows, BLOCK):
            at = slice(low, low + BLOCK)
            scaled, _ = rms_parts(xs[mb, at, :].astype(F32))
            normed[at, :] = (scaled * gain_attn[...]).astype(BF16)

    def keys_values(mb, part):
        cos_rows, sin_rows = cosine[mb, part, :], sine[mb, part, :]
        for start in range(0, width, 256):
            rows_n = normed[part, :]
            keys = dot(rows_n, wk[:, start:start + 256])
            for inner in range(0, 256, LANES):
                ks[mb, part, start + inner:start + inner + LANES] = rope(
                    keys[:, inner:inner + LANES], cos_rows, sin_rows, 1).astype(BF16)
            vs[mb, part, start:start + 256] = dot(rows_n, wv[:, start:start + 256]).astype(BF16)

    def attention(mb):
        def scores(index):
            lanes, here, near = place(index)
            wide_f[index % 2] = dot_nt(ks[mb, near, lanes], split_heads(qs[mb, here, lanes]))

        def soften(index):
            pair, block = items[index]
            for head in range(2):
                at = slice(head * LANES, (head + 1) * LANES)
                masked = wide_f[index % 2, :, at] + bias[block]
                raw = jnp.exp(masked - jnp.max(masked, axis=0, keepdims=True))
                probs[mb, pair, block, :, at] = raw.astype(BF16)

        def collect(index):
            pair, block = items[index]
            lanes, here, near = place(index)
            left = jnp.concatenate([vs[mb, near, lanes].T, jnp.ones((16, band), BF16)], axis=0)
            turned = dot(left, probs[mb, pair, block])
            inverse = 1.0 / turned[LANES:LANES + 1]
            scale[mb, index] = inverse
            att[here, lanes] = join_heads(turned[:LANES] * inverse).astype(BF16)

        pipelined(scores, soften, collect)

    def forward(mb, carry):
        @pl.when(is_first)
        def _():
            token_copy(mb).wait()

            @pl.when(has_right & (mb + 1 < batches))
            def _():
                halo_copy(mb + 1, tokens.at[mb + 1]).start()

        @pl.when(has_before & (mb == 0))
        def _():
            hand_copy(mb).wait_recv()

            @pl.when(has_right)
            def _():
                halo_copy(mb, xs.at[mb, own]).start()

        saved_before("normed", mb)
        normalise(mb, own)

        @pl.when(mb == 0)
        def _():
            for index in range(3):
                weight_copy(index).wait()
            for index in range(3, 7):
                weight_copy(index).start()

        cos_rows, sin_rows = cosine[mb, own, :], sine[mb, own, :]
        for start in range(0, width, 256):
            queries = dot(normed[own, :], wq[:, start:start + 256])
            for inner in range(0, 256, LANES):
                turned = rope(queries[:, inner:inner + LANES], cos_rows, sin_rows, 1)
                qs[mb, :, start + inner:start + inner + LANES] = (turned * 0.125).astype(BF16)
        keys_values(mb, own)
        for block in range(2):
            key_at = lax.broadcasted_iota(jnp.int32, (band, half), 0) + (block * half - rows)
            query_at = lax.broadcasted_iota(jnp.int32, (band, half), 1) + block * half
            first = first_key[mb, 0:1, block * half:(block + 1) * half]
            bias[block] = jnp.where((key_at >= first) & (key_at <= query_at), 0.0, -1e30)

        @pl.when(has_left)
        def _():
            halo_copy(mb, xs.at[mb, own]).wait_recv()

        normalise(mb, halo)
        keys_values(mb, halo)
        save("normed", mb).start()
        saved_before("att", mb)
        attention(mb)
        save("att", mb).start()

        @pl.when(mb == 0)
        def _():
            for index in range(3, 7):
                weight_copy(index).wait()

        saved_before("n2", mb)
        for start in range(0, width, 256):
            at = slice(start, start + 256)
            d_norm[:, at] = xs[mb, own, at].astype(F32) + dot(att[...], wo[:, at])
        for low in range(0, rows, BLOCK):
            at = slice(low, low + BLOCK)
            total = d_norm[at, :]
            scaled, _ = rms_parts(total)
            mixed[mb, at, :] = total.astype(BF16)
            n2[at, :] = (scaled * gain_mlp[...]).astype(BF16)
        save("n2", mb).start()

        @pl.when(has_before & (mb + 1 < batches))
        def _():
            hand_copy(mb + 1).wait_recv()

            @pl.when(has_right)
            def _():
                halo_copy(mb + 1, xs.at[mb + 1, own]).start()

        saved_before("prod", mb)
        for start in range(0, hidden_width, 256):
            at = slice(start, start + 256)
            gate = dot(n2[...], wg[:, at])
            up = dot(n2[...], wu[:, at])
            sigma = jax.nn.sigmoid(gate)
            gated = gate * sigma
            prod[:, at] = (gated * up).astype(BF16)
            silu[mb, :, at] = gated.astype(BF16)
            slope[mb, :, at] = (up * (sigma * (1.0 + gate * (1.0 - sigma)))).astype(BF16)
        save("prod", mb).start()
        for start in range(0, width, 256):
            at = slice(start, start + 256)
            outs[mb, :, at] = (d_norm[:, at] + dot(prod[...], wd[:, at])).astype(BF16)

        @pl.when(has_after)
        def _():
            hand_copy(mb).start()

        out_copy(mb, block_out).start()
        return carry

    lax.fori_loop(0, batches, forward, 0)

    for name in ("normed", "att", "n2", "prod"):
        save(name, batches - 1).wait()
    for mb in range(batches):
        out_copy(mb, block_out).wait()

    @pl.when(has_after)
    def _():
        for mb in range(batches):
            hand_copy(mb).wait_send()


    def add_gain(which, product):
        folded = jnp.sum(product.reshape(product.shape[0] // 8, 8, width), axis=0)
        at = pl.ds(8 * which, 8)
        gains_out[at, :] = gains_out[at, :] + folded

    def attention_back(mb):
        def d_weights(index):
            lanes, here, near = place(index)
            wide_f[index % 2] = dot_nt(vs[mb, near, lanes], split_heads(d_att[here, lanes]))

        def d_soften(index):
            pair, block = items[index]
            for head in range(2):
                at = slice(head * LANES, (head + 1) * LANES)
                weight = probs[mb, pair, block, :, at].astype(F32) * scale[mb, index, :, at]
                moved = weight * wide_f[index % 2, :, at]
                centre = jnp.sum(moved, axis=0, keepdims=True)
                left_b[index % 2, :, at] = (moved - weight * centre).astype(BF16)
                right_b[index % 2, :, at] = weight.astype(BF16)

        def collect(index):
            pair, block = items[index]
            lanes, here, near = place(index)
            d_scores = left_b[index % 2]
            d_keys = dot(d_scores, split_heads(qs[mb, here, lanes]))
            d_values = dot(right_b[index % 2], split_heads(d_att[here, lanes]))
            turned = lax.dot_general(
                ks[mb, near, lanes], d_scores, (((0,), (0,)), ((), ())), preferred_element_type=F32)
            at = pl.ds(rows + block * half, half)
            qs[mb, here, lanes] = rope(
                join_heads(turned) * 0.125, cosine[mb, at, :], sine[mb, at, :], -1).astype(BF16)
            slot = pair % 2
            if block == 0:
                key_f[slot], value_f[slot] = d_keys, d_values
                return
            earlier_k, earlier_v = key_f[slot], value_f[slot]
            pieces = (
                (0, half, earlier_k[:half], earlier_v[:half]),
                (half, band, earlier_k[half:] + d_keys[:rows], earlier_v[half:] + d_values[:rows]),
                (band, 2 * rows, d_keys[rows:], d_values[rows:]),
            )
            for low, high, piece_k, piece_v in pieces:
                ks[mb, low:high, lanes] = rope(
                    piece_k, cosine[mb, low:high, :], sine[mb, low:high, :], -1).astype(BF16)
                vs[mb, low:high, lanes] = piece_v.astype(BF16)

        pipelined(d_weights, d_soften, collect)

    def finish(mb):
        @pl.when(has_right)
        def _():
            back_copy(mb).wait_recv()
            d_own[...] = d_own[...] + halo_in[mb].astype(F32)

        for low in range(0, rows, BLOCK):
            at = slice(low, low + BLOCK)
            scaled, inverse = rms_parts(xs[mb, rows + low:rows + low + BLOCK, :].astype(F32))
            d_normed = d_own[at, :]
            add_gain(0, d_normed * scaled)
            back = rms_back(d_normed * gain_attn[...], scaled, inverse)
            outs[mb, at, :] = (branch[lax.rem(mb, 2), at, :].astype(F32) + back).astype(BF16)

        @pl.when(has_before)
        def _():
            turn_copy(mb).start()

        out_copy(mb, grad_out).start()

    def backward(mb, carry):
        @pl.when(is_last)
        def _():
            cot_copy(mb).wait()

        @pl.when(has_after)
        def _():
            turn_copy(mb).wait_recv()

        save("g", mb).start()
        for start in range(0, hidden_width, 256):
            at = slice(start, start + 256)
            d_product = dot_nt(gs[mb], wd[at, :])
            slope[mb, :, at] = (d_product * slope[mb, :, at].astype(F32)).astype(BF16)
            silu[mb, :, at] = (d_product * silu[mb, :, at].astype(F32)).astype(BF16)
        save("dg", mb).start()
        save("du", mb).start()
        for start in range(0, width, 256):
            at = slice(start, start + 256)
            d_norm[:, at] = dot_nt(slope[mb], wg[at, :]) + dot_nt(silu[mb], wu[at, :])
        slot = lax.rem(mb, 2)

        @pl.when(mb >= 2)
        def _():
            save("branch", mb - 2).wait()

        for low in range(0, rows, BLOCK):
            at = slice(low, low + BLOCK)
            scaled, inverse = rms_parts(mixed[mb, at, :].astype(F32))
            d_normed = d_norm[at, :]
            add_gain(1, d_normed * scaled)
            total = gs[mb, at, :].astype(F32) + rms_back(d_normed * gain_mlp[...], scaled, inverse)
            branch[slot, at, :] = total.astype(BF16)
        save("branch", mb).start()
        for start in range(0, width, 256):
            at = slice(start, start + 256)
            d_att[:, at] = dot_nt(branch[slot], wo[at, :]).astype(BF16)

        @pl.when(mb > 0)
        def _():
            finish(mb - 1)

        attention_back(mb)
        save("dq", mb).start()
        save("dk", mb).start()
        save("dv", mb).start()

        @pl.when(has_left & (mb > 0))
        def _():
            back_copy(mb - 1).wait_send()

        for start in range(0, width, 256):
            at = slice(start, start + 256)
            halo_out[:, at] = (
                dot_nt(ks[mb, halo, :], wk[at, :]) + dot_nt(vs[mb, halo, :], wv[at, :])).astype(BF16)

        @pl.when(has_left)
        def _():
            back_copy(mb).start()

        for start in range(0, width, 256):
            at = slice(start, start + 256)
            d_own[:, at] = (
                dot_nt(qs[mb], wq[at, :]) + dot_nt(ks[mb, own, :], wk[at, :])
                + dot_nt(vs[mb, own, :], wv[at, :]))
        return carry

    lax.fori_loop(0, batches, backward, 0)
    finish(batches - 1)

    for mb in range(batches - 2, batches):
        save("branch", mb).wait()
    for mb in range(batches):
        for name in ("g", "dg", "du", "dq", "dk", "dv"):
            save(name, mb).wait()
        out_copy(mb, grad_out).wait()

    @pl.when(has_left)
    def _():
        back_copy(batches - 1).wait_send()

    @pl.when(has_before)
    def _():
        for mb in range(batches):
            turn_copy(mb).wait_send()

    @pl.when(has_right)
    def _():
        for mb in range(batches):
            halo_copy(mb, xs.at[mb, own]).wait_send()


def any_spec():
    return pl.BlockSpec(memory_space=pl.ANY)


def vmem_spec():
    return pl.BlockSpec(memory_space=pltpu.VMEM)


def trig_table(head_dim, reach):
    half_dim = head_dim // 2
    freqs = np.float32(THETA) ** (-np.arange(half_dim, dtype=np.float32) * np.float32(2.0) / np.float32(head_dim))
    angles = np.arange(reach, dtype=np.float32)[:, None] * np.tile(freqs, LANES // half_dim)[None, :]
    sign = np.tile(np.repeat(np.array([-1.0, 1.0], np.float32), half_dim), LANES // head_dim)
    parts = []
    for table in (np.cos(angles), np.sin(angles) * sign):
        high = table.astype(ml_dtypes.bfloat16)
        low = (table - high.astype(np.float32)).astype(ml_dtypes.bfloat16)
        parts.append(np.concatenate([high, low], axis=1))
    return jnp.asarray(np.stack(parts))


def run_layers(tokens, cotangent, lengths, weights, gain_attn, gain_mlp):
    batches, rows, width = tokens.shape
    hidden_width = weights[4].shape[2]
    pairs = width // LANES
    band = rows + rows // 2
    one = (batches, rows, width)
    two = (batches, 2 * rows, width)
    wide = (batches, rows, hidden_width)
    outs = [(one, BF16), (one, BF16), (two, BF16), (one, BF16), (one, BF16), (wide, BF16),
            (one, BF16), (one, BF16), (wide, BF16), (wide, BF16), (one, BF16), (two, BF16), (two, BF16),
            ((16, width), F32)]
    dma = pltpu.SemaphoreType.DMA
    scratch = [pltpu.VMEM(w.shape[1:], BF16) for w in weights] + [
        pltpu.VMEM(two, BF16),
        pltpu.VMEM(one, BF16),
        pltpu.VMEM(two, BF16),
        pltpu.VMEM(two, BF16),
        pltpu.VMEM((batches, pairs, 2, band, rows), BF16),
        pltpu.VMEM(wide, BF16),
        pltpu.VMEM(wide, BF16),
        pltpu.VMEM(one, BF16),
        pltpu.VMEM(two[1:], BF16),
        pltpu.VMEM(one[1:], BF16),
        pltpu.VMEM(one[1:], BF16),
        pltpu.VMEM(wide[1:], BF16),
        pltpu.VMEM(one, BF16),
        pltpu.VMEM(one, BF16),
        pltpu.VMEM(one, BF16),
        pltpu.VMEM(one[1:], BF16),
        pltpu.VMEM((2,) + one[1:], BF16),
        pltpu.VMEM(one[1:], BF16),
        pltpu.VMEM(one[1:], F32),
        pltpu.VMEM(one[1:], F32),
        pltpu.VMEM((batches, 2 * rows, LANES), F32),
        pltpu.VMEM((batches, 2 * rows, LANES), F32),
        pltpu.VMEM((batches, 8, rows), jnp.int32),
        pltpu.VMEM((2, band, rows // 2), F32),
        pltpu.VMEM((batches, 2 * pairs, 1, rows), F32),
        pltpu.VMEM((2, band, rows), F32),
        pltpu.VMEM((2, band, rows), BF16),
        pltpu.VMEM((2, band, rows), BF16),
        pltpu.VMEM((2, band, LANES), F32),
        pltpu.VMEM((2, band, LANES), F32),
        dma((7,)), dma((1,)), dma((batches,)), dma((batches,)), dma((11, batches)),
    ] + [dma((batches,))] * 9
    trig = trig_table(width // HEADS, band)
    return pl.pallas_call(
        layers_kernel,
        out_shape=[jax.ShapeDtypeStruct(shape, dtype) for shape, dtype in outs],
        in_specs=[any_spec()] * 2 + [pl.BlockSpec(memory_space=pltpu.SMEM)] + [any_spec()] * 7 + [vmem_spec()] * 2 + [any_spec()],
        out_specs=[any_spec()] * 13 + [vmem_spec()],
        scratch_shapes=scratch,
        compiler_params=pltpu.CompilerParams(
            collective_id=1, has_side_effects=True, vmem_limit_bytes=VMEM_BYTES),
        name="layers",
    )(tokens, cotangent, lengths, *weights, gain_attn, gain_mlp, trig)


LAG = 3
SENDS = 4
LENT = 4
MIX = 5
CHUNK = 256


def dot_tn(left, right):
    return lax.dot_general(
        left, right, (((0,), (0,)), ((), ())), preferred_element_type=F32
    )


class Ladder:
    def __init__(self, refs, sems, outer, chunks):
        self.computed = chunks
        self.dw, self.a_out, self.a_in, self.b_out, self.b_own, self.b_in, self.c_out, self.c_own, self.c_in, self.result = refs
        self.a_send, self.a_recv, self.b_send, self.b_recv, self.c_send, self.c_recv = sems
        wide = lax.axis_index("wide")
        self.outer = outer
        self.core, self.side, self.depth = lax.rem(wide, 2), lax.rem(wide // 2, 2), wide // 4
        self.core_mate = {"wide": wide + 1 - 2 * self.core}
        self.side_mate = {"wide": wide + 2 - 4 * self.side}
        self.column = lax.rem(wide, 4)
        self.first, self.count = 0, chunks
        self.lent = None

    def lend(self, refs, sems, section):
        self.x_out, self.x_in, self.r_out, self.r_in = refs
        self.x_send, self.x_recv, self.r_send, self.r_recv = sems
        self.lender = section == 0
        self.lent = self.x_in.shape[0]
        self.partner = {"section": 1 - section}
        self.first = jnp.where(self.lender, self.lent, 0)
        self.count = jnp.where(self.lender, self.computed, self.computed + self.lent)

    def x_copy(self, j):
        return pltpu.make_async_remote_copy(
            self.x_out.at[j], self.x_in.at[j], self.x_send.at[j], self.x_recv.at[j],
            device_id=self.partner, device_id_type=MESH)

    def r_copy(self, j):
        return pltpu.make_async_remote_copy(
            self.r_out.at[j], self.r_in.at[j], self.r_send.at[j], self.r_recv.at[j],
            device_id=self.partner, device_id_type=MESH)

    def stage_x(self, j):
        held = lax.rem(j, LAG + 1)

        self.a_copy(j).wait_recv()
        for index in range(2 * self.outer):
            self.x_out[j, index] = (
                self.dw[held, 2 * index + self.core] + self.a_in[j, index].astype(F32)).astype(BF16)
        self.x_copy(j).start()

    def a_copy(self, j):
        slot = lax.rem(j, SENDS)
        return pltpu.make_async_remote_copy(
            self.a_out.at[slot], self.a_in.at[j], self.a_send.at[slot], self.a_recv.at[j],
            device_id=self.core_mate, device_id_type=MESH)

    def b_copy(self, j):
        slot = lax.rem(j, SENDS)
        return pltpu.make_async_remote_copy(
            self.b_out.at[slot], self.b_in.at[j], self.b_send.at[slot], self.b_recv.at[j],
            device_id=self.side_mate, device_id_type=MESH)

    def c_copy(self, j, step, arriving):
        slot = lax.rem(j, SENDS)
        peer = lax.rem(self.depth + step, self.outer)
        sender = peer if arriving else self.depth
        return pltpu.make_async_remote_copy(
            self.c_out.at[slot, peer], self.c_in.at[j, sender], self.c_send.at[slot, step], self.c_recv.at[j, sender],
            device_id={"wide": peer * 4 + self.column}, device_id_type=MESH)

    def stage_a(self, j):
        slot, held = lax.rem(j, SENDS), lax.rem(j, LAG + 1)

        @pl.when(j >= SENDS)
        def _():
            self.a_copy(j - SENDS).wait_send()

        for index in range(2 * self.outer):
            self.a_out[slot, index] = self.dw[held, 2 * index + 1 - self.core].astype(BF16)
        self.a_copy(j).start()

    def stage_b(self, j):
        slot, held = lax.rem(j, SENDS), lax.rem(j, LAG + 1)

        @pl.when(j >= SENDS + self.first)
        def _():
            self.b_copy(j - SENDS).wait_send()

        def split():
            self.a_copy(j).wait_recv()
            for index in range(self.outer):
                far, near = 2 * index + 1 - self.side, 2 * index + self.side
                self.b_out[slot, index] = (
                    self.dw[held, 2 * far + self.core] + self.a_in[j, far].astype(F32)).astype(BF16)
                self.b_own[held, index] = self.dw[held, 2 * near + self.core] + self.a_in[j, near].astype(F32)

        if self.lent is None:
            split()
        else:
            pl.when(j < self.computed)(split)

            @pl.when(j >= self.computed)
            def _():
                borrowed = j - self.computed
                self.x_copy(borrowed).wait_recv()
                for index in range(self.outer):
                    self.b_out[slot, index] = self.x_in[borrowed, 2 * index + 1 - self.side]
                    self.b_own[held, index] = self.x_in[borrowed, 2 * index + self.side].astype(F32)

        self.b_copy(j).start()

    def stage_c(self, j):
        slot, held = lax.rem(j, SENDS), lax.rem(j, LAG + 1)

        @pl.when(j >= SENDS + self.first)
        def _():
            for step in range(1, self.outer):
                self.c_copy(j - SENDS, step, False).wait_send()

        self.b_copy(j).wait_recv()
        for index in range(self.outer):
            self.c_out[slot, index] = (self.b_own[held, index] + self.b_in[j, index].astype(F32)).astype(BF16)
        for step in range(1, self.outer):
            self.c_copy(j, step, False).start()
        self.c_own[held] = self.b_own[held, self.depth] + self.b_in[j, self.depth].astype(F32)

    def stage_d(self, j):
        held = lax.rem(j, LAG + 1)
        total = self.c_own[held]
        for step in range(1, self.outer):
            self.c_copy(j, step, True).wait_recv()
        for step in range(1, self.outer):
            total = total + self.c_in[j, lax.rem(self.depth + step, self.outer)].astype(F32)
        if self.lent is None:
            self.result[j] = total
            return

        @pl.when(j < self.computed)
        def _():
            self.result[j] = total

        @pl.when(j >= self.computed)
        def _():
            @pl.when(j == self.computed)
            def _():
                pl.semaphore_wait(pltpu.get_barrier_semaphore(), 1)

            self.r_out[j - self.computed] = total
            self.r_copy(j - self.computed).start()

    def drain(self):
        for back in range(1, SENDS + 1):
            self.a_copy(self.computed - back).wait_send()
            j = self.count - back

            @pl.when(j >= self.first)
            def _(j=j):
                self.b_copy(j).wait_send()
                for step in range(1, self.outer):
                    self.c_copy(j, step, False).wait_send()

        if self.lent is not None:
            @pl.when(self.lender)
            def _():
                for j in range(self.lent):
                    self.x_copy(j).wait_send()
                    self.r_copy(j).wait_recv()
                    self.result[j] = self.r_in[j]

            @pl.when(jnp.logical_not(self.lender))
            def _():
                for j in range(self.lent):
                    self.r_copy(j).wait_send()


def weight_kernel(
    normed_in, att_in, n2_in, prod_in, g_in, db_in, dg_in, du_in, dq_in, dk_in, dv_in, gains,
    out_m, out_d,
    normed, att, n2, prod, g, dy, *rest,
):
    m_refs, d_refs, lend_refs = rest[:9], rest[9:18], rest[18:22]
    m_sems, d_sems, lend_sems = rest[22:28], rest[28:34], rest[34:38]
    x_sem, dy_sem = rest[38], rest[39]
    section, wide, count = lax.axis_index("section"), lax.axis_index("wide"), lax.axis_size("wide")
    batches, rows, width = g_in.shape
    hidden_width = prod_in.shape[2]
    outer = count // 4
    own = pl.ds(rows, rows)
    m_count, d_count = out_m.shape[0], out_d.shape[0]
    per_wide, per_narrow = hidden_width // CHUNK, width // CHUNK
    ladder_m = Ladder(m_refs + (out_m,), m_sems, outer, m_count)
    ladder_d = Ladder(d_refs + (out_d,), d_sems, outer, d_count)
    ladder_d.lend(lend_refs, lend_sems, section)
    true = wide >= 0

    loads = ((n2_in, n2), (att_in, att), (normed_in, normed), (prod_in, prod), (g_in, g))

    def x_copy(index):
        source, target = loads[index]
        return pltpu.make_async_copy(source, target, x_sem.at[index])

    kinds = ((dg_in, per_wide), (du_in, per_wide), (db_in, per_narrow), (dq_in, per_narrow), (dk_in, per_narrow), (dv_in, per_narrow))

    def each_load(j, act):
        slot = lax.rem(j, 2)
        base = 0
        for index, (source, parts) in enumerate(kinds):
            @pl.when((j >= base) & (j < base + parts))
            def _(source=source, base=base, index=index):
                lanes = pl.ds(pl.multiple_of((j - base) * CHUNK, CHUNK), CHUNK)
                target = dy.at[slot] if index >= 4 else dy.at[slot, :, own]
                act(pltpu.make_async_copy(source.at[:, :, lanes], target, dy_sem.at[slot]))
            base += parts
        return base

    x_copy(0).start()
    each_load(jnp.int32(0), lambda copy: copy.start())
    for index in (3, 4, 1, 2):
        x_copy(index).start()
    barrier = pltpu.get_barrier_semaphore()
    peers = [ladder_m.core_mate, ladder_m.side_mate] + [
        {"wide": lax.rem(ladder_m.depth + step, outer) * 4 + ladder_m.column} for step in range(1, outer)]
    for peer in peers:
        pl.semaphore_signal(barrier, inc=1, device_id=peer, device_id_type=MESH)
    pl.semaphore_wait(barrier, len(peers) + ladder_d.lender.astype(jnp.int32))
    pl.semaphore_signal(barrier, inc=1, device_id=ladder_d.partner, device_id_type=MESH)

    kv_first = 2 * per_wide + 2 * per_narrow
    kv_last = kv_first + 2 * per_narrow
    narrow_first = 2 * per_wide

    def compute_m(j):
        slot, held = lax.rem(j, 2), lax.rem(j, LAG + 1)

        @pl.when(j + 1 < kv_last)
        def _():
            each_load(j + 1, lambda copy: copy.start())

        def write(left, right):
            product = dot_tn(left.reshape(-1, width), right.reshape(-1, CHUNK))
            ladder_m.dw[held] = product.reshape(ladder_m.dw.shape[1:])

        @pl.when(j < kv_last)
        def _():
            each_load(j, lambda copy: copy.wait())

        for index, first in enumerate((0, narrow_first, narrow_first + per_narrow)):
            @pl.when(j == first)
            def _(index=index):
                x_copy(index).wait()

        @pl.when(j < narrow_first)
        def _():
            write(n2[...], dy[slot, :, own, :])

        @pl.when((j >= narrow_first) & (j < narrow_first + per_narrow))
        def _():
            write(att[...], dy[slot, :, own, :])

        @pl.when((j >= narrow_first + per_narrow) & (j < kv_first))
        def _():
            write(normed[:, own, :], dy[slot, :, own, :])

        @pl.when((j >= kv_first) & (j < kv_last))
        def _():
            write(normed[...], dy[slot])

        @pl.when(j == kv_last)
        def _():
            first = jnp.sum(gains[0:8, :], axis=0, keepdims=True)
            second = jnp.sum(gains[8:16, :], axis=0, keepdims=True)
            row = lax.broadcasted_iota(jnp.int32, (LANES, width), 0)
            placed = jnp.where(row == 0, first, jnp.where(row == 1, second, 0.0))
            columns = placed.T
            ladder_m.dw[held] = jnp.concatenate([columns, columns], axis=1).reshape(ladder_m.dw.shape[1:])

    def compute_d(j):
        held = lax.rem(j, LAG + 1)

        @pl.when(j == 0)
        def _():
            x_copy(3).wait()
            x_copy(4).wait()

        lanes = pl.ds(pl.multiple_of(j * LANES, LANES), LANES)
        product = dot_tn(prod[...].reshape(-1, hidden_width), g[:, :, lanes].reshape(-1, LANES))
        ladder_d.dw[held] = product.reshape(ladder_d.dw.shape[1:])

    lent = ladder_d.lent
    lender = ladder_d.lender

    def on_chunk(s, act_m, act_d):
        mixed = s < MIX * lent
        turn, place = s // MIX, lax.rem(s, MIX)
        j_lender = jnp.where(mixed, (MIX - 1) * turn + place, s - lent)
        d_lender = jnp.where(mixed, turn, s - m_count)
        m_turn = jnp.where(lender & mixed, place < MIX - 1, True)
        j_m = jnp.where(lender, j_lender, s)
        j_d = jnp.where(lender, d_lender, s - m_count)
        last_d = ladder_d.count
        is_m = (s >= 0) & (j_m < m_count) & m_turn
        is_d = (s >= 0) & jnp.where(lender & mixed, place == MIX - 1, j_m >= m_count) & (j_d < last_d)

        @pl.when(is_m)
        def _():
            act_m(j_m)

        @pl.when(is_d)
        def _():
            act_d(j_d)

    def own_d(act):
        def guarded(j):
            pl.when(j < d_count)(lambda: act(j))
        return guarded

    def reduced_d(act):
        def guarded(j):
            pl.when(j >= ladder_d.first)(lambda: act(j))
        return guarded

    def second(j):
        pl.when(j < ladder_d.first)(lambda: ladder_d.stage_x(j))
        pl.when(j >= ladder_d.first)(lambda: ladder_d.stage_b(j))

    def step(s, carry):
        on_chunk(s, compute_m, own_d(compute_d))
        on_chunk(s, ladder_m.stage_a, own_d(ladder_d.stage_a))
        on_chunk(s - LAG, ladder_m.stage_b, second)
        on_chunk(s - 2 * LAG, ladder_m.stage_c, reduced_d(ladder_d.stage_c))
        on_chunk(s - 3 * LAG, ladder_m.stage_d, reduced_d(ladder_d.stage_d))
        return carry

    lax.fori_loop(0, m_count + d_count + lent + 3 * LAG, step, 0)
    ladder_m.drain()
    ladder_d.drain()


def run_weights(normed, att, n2, prod, g, db, dg, du, dq, dk, dv, gains, count):
    batches, rows, width = g.shape
    hidden_width = prod.shape[2]
    outer = count // 4
    m_count = 2 * (hidden_width // CHUNK) + 4 * (width // CHUNK) + 1
    d_count = width // LANES

    def ladder(chunks, lent, block):
        total = chunks + lent
        refs = [
            pltpu.VMEM((LAG + 1, count) + block, F32),
            pltpu.VMEM((SENDS, count // 2) + block, BF16),
            pltpu.VMEM((chunks, count // 2) + block, BF16),
            pltpu.VMEM((SENDS, outer) + block, BF16),
            pltpu.VMEM((LAG + 1, outer) + block, F32),
            pltpu.VMEM((total, outer) + block, BF16),
            pltpu.VMEM((SENDS, outer) + block, BF16),
            pltpu.VMEM((LAG + 1,) + block, F32),
            pltpu.VMEM((total, outer) + block, BF16),
        ]
        sems = [
            pltpu.SemaphoreType.DMA((SENDS,)),
            pltpu.SemaphoreType.DMA((chunks,)),
            pltpu.SemaphoreType.DMA((SENDS,)),
            pltpu.SemaphoreType.DMA((total,)),
            pltpu.SemaphoreType.DMA((SENDS, outer)),
            pltpu.SemaphoreType.DMA((total, outer)),
        ]
        return refs, sems

    block_m, block_d = (width // count, CHUNK), (hidden_width // count, LANES)
    m_refs, m_sems = ladder(m_count, 0, block_m)
    d_refs, d_sems = ladder(d_count, LENT, block_d)
    lend_refs = [
        pltpu.VMEM((LENT, count // 2) + block_d, BF16),
        pltpu.VMEM((LENT, count // 2) + block_d, BF16),
        pltpu.VMEM((LENT,) + block_d, F32),
        pltpu.VMEM((LENT,) + block_d, F32),
    ]
    lend_sems = [pltpu.SemaphoreType.DMA((size,)) for size in (LENT,) * 4]
    return pl.pallas_call(
        weight_kernel,
        out_shape=[
            jax.ShapeDtypeStruct((m_count,) + block_m, F32),
            jax.ShapeDtypeStruct((d_count,) + block_d, F32),
        ],
        in_specs=[any_spec()] * 11 + [vmem_spec()],
        out_specs=[vmem_spec()] * 2,
        scratch_shapes=[
            pltpu.VMEM(normed.shape, BF16),
            pltpu.VMEM(att.shape, BF16),
            pltpu.VMEM(n2.shape, BF16),
            pltpu.VMEM(prod.shape, BF16),
            pltpu.VMEM(g.shape, BF16),
            pltpu.VMEM((2, batches, 2 * rows, CHUNK), BF16),
        ] + m_refs + d_refs + lend_refs + m_sems + d_sems + lend_sems + [
            pltpu.SemaphoreType.DMA((5,)),
            pltpu.SemaphoreType.DMA((2,)),
        ],
        compiler_params=pltpu.CompilerParams(
            collective_id=3, has_side_effects=True, vmem_limit_bytes=VMEM_BYTES),
        name="weights",
    )(normed, att, n2, prod, g, db, dg, du, dq, dk, dv, gains)


def summed_weights(normed, att, n2, prod, g, db, dg, du, dq, dk, dv, gains):
    def outer_sum(left, right):
        total = lax.dot_general(
            left, right, (((0, 1), (0, 1)), ((), ())), preferred_element_type=F32)
        return lax.psum_scatter(total[None], "wide", scatter_dimension=1, tiled=True)

    rows = g.shape[1]
    normed_own = normed[:, rows:]
    gain_rows = gains.reshape(2, 8, -1).sum(axis=1)
    gain_parts = [
        lax.psum_scatter(gain_rows[i:i + 1], "wide", scatter_dimension=1, tiled=True) for i in range(2)]
    return (
        outer_sum(normed_own, dq), outer_sum(normed, dk), outer_sum(normed, dv), outer_sum(att, db),
        outer_sum(n2, dg), outer_sum(n2, du), outer_sum(prod, g), *gain_parts,
    )


def arrange_kernel(sizes, block, grads, chunks_m, chunks_d, block_out, grad_out, *rest):
    outs, (held_block, held_grads, held_m, held_d), (load_sem, store_sem) = rest[:9], rest[9:13], rest[13:]
    batches = block.shape[0]
    loads, stores = [], []
    for mb in range(batches):
        loads += [(block.at[mb], held_block.at[mb]), (grads.at[mb], held_grads.at[mb])]
        stores += [(held_block.at[mb], block_out.at[0, mb]), (held_grads.at[mb], grad_out.at[0, mb])]
    first_load = len(loads)
    loads += [(chunks_m, held_m), (chunks_d, held_d)]
    base = 0
    for size, index in zip(sizes, (4, 5, 3, 0, 1, 2)):
        for part in range(size):
            stores.append((held_m.at[base + part], outs[index].at[0, :, pl.ds(part * CHUNK, CHUNK)]))
        base += size
    for part in range(chunks_d.shape[0]):
        stores.append((held_d.at[part], outs[6].at[0, :, pl.ds(part * LANES, LANES)]))
    loads = [pltpu.make_async_copy(*pair, load_sem.at[index]) for index, pair in enumerate(loads)]
    stores = [pltpu.make_async_copy(*pair, store_sem.at[index]) for index, pair in enumerate(stores)]
    for copy in loads:
        copy.start()
    for index in range(first_load):
        loads[index].wait()
        stores[index].start()
    for copy in loads[first_load:]:
        copy.wait()
    for copy in stores[first_load:]:
        copy.start()
    turned = held_m[base, :, :LANES].T
    outs[7][...] = turned[0:1, :]
    outs[8][...] = turned[1:2, :]
    for copy in stores:
        copy.wait()


def arrange(block, grads, chunks_m, chunks_d, sizes):
    own, own_d = chunks_m.shape[1], chunks_d.shape[1]
    width, hidden_width = block.shape[2], CHUNK * sizes[0]
    shapes = [(1,) + block.shape] * 2
    narrow, broad = (1, own, width), (1, own, hidden_width)
    matrices = [narrow] * 4 + [broad] * 2 + [(1, own_d, width)]
    out_shape = [jax.ShapeDtypeStruct(shape, BF16) for shape in shapes]
    out_shape += [jax.ShapeDtypeStruct(shape, F32) for shape in matrices + [(1, own)] * 2]
    copies = sum(sizes) + chunks_d.shape[0] + 2 * block.shape[0]
    return pl.pallas_call(
        functools.partial(arrange_kernel, sizes),
        out_shape=out_shape,
        in_specs=[any_spec()] * 4,
        out_specs=[any_spec()] * 9 + [vmem_spec()] * 2,
        scratch_shapes=[pltpu.VMEM(held.shape, held.dtype) for held in (block, grads, chunks_m, chunks_d)]
        + [pltpu.SemaphoreType.DMA((2 * block.shape[0] + 2,)), pltpu.SemaphoreType.DMA((copies,))],
        compiler_params=pltpu.CompilerParams(vmem_limit_bytes=VMEM_BYTES),
        name="arrange",
    )(block, grads, chunks_m, chunks_d)


def weight_grads(block_out, input_grads, normed, att, n2, prod, g, db, dg, du, dq, dk, dv, gains):
    count = lax.axis_size("wide")
    width, hidden_width = g.shape[2], prod.shape[2]
    if count % 4 or width % (16 * count) or hidden_width % (16 * count):
        grads = summed_weights(normed, att, n2, prod, g, db, dg, du, dq, dk, dv, gains)
        return (block_out[None], input_grads[None], *grads)
    out_m, out_d = run_weights(normed, att, n2, prod, g, db, dg, du, dq, dk, dv, gains, count)
    sizes = (hidden_width // CHUNK,) * 2 + (width // CHUNK,) * 4
    return tuple(arrange(block_out, input_grads, out_m, out_d, sizes))


def per_device(
    tokens, cotangent, seg_lengths, w_query, w_key, w_value, w_output, w_gate, w_up, w_down, gain_attn, gain_mlp,
):
    weights = (w_query, w_key, w_value, w_output, w_gate, w_up, w_down)
    lengths = seg_lengths.reshape(seg_lengths.shape[0], -1)
    (block_out, input_grads, normed, att, n2, prod, g, db, dg, du, dq, dk, dv, gains) = run_layers(
        tokens, cotangent, lengths, weights, gain_attn, gain_mlp)
    return weight_grads(block_out, input_grads, normed, att, n2, prod, g, db, dg, du, dq, dk, dv, gains)


def solution(mesh):
    in_specs = (
        P(None, "wide", None),
        P(None, "wide", None),
        P(),
        *[P("section", None, None)] * 7,
        *[P("section", None)] * 2,
    )
    out_specs = (
        *[P("section", None, "wide", None)] * 2,
        *[P("section", "wide", None)] * 7,
        *[P("section", "wide")] * 2,
    )
    return jax.shard_map(
        per_device, mesh=mesh, in_specs=in_specs, out_specs=out_specs, check_vma=False
    )
```

```python
import functools

import jax
import jax.numpy as jnp
import ml_dtypes
import numpy as np
from jax import lax
from jax.experimental import pallas as pl
from jax.experimental.pallas import tpu as pltpu
from jax.sharding import PartitionSpec as P

HEADS = 12
EPS = 1e-05
THETA = 10000.0

F32 = jnp.float32
BF16 = jnp.bfloat16
MESH = pl.DeviceIdType.MESH
LANES = 128
BLOCK = 64
PIECE = 256
VMEM_BYTES = 63 * 1024 * 1024


def dot(left, right):
    return jnp.dot(left, right, preferred_element_type=F32)


def dot_nt(left, right):
    return lax.dot_general(
        left, right, (((1,), (1,)), ((), ())), preferred_element_type=F32
    )


def rms_parts(hidden):
    inverse = lax.rsqrt(jnp.mean(hidden * hidden, axis=1, keepdims=True) + EPS)
    return (hidden * inverse, inverse)


def rms_back(upstream, scaled, inverse):
    return inverse * (upstream - scaled * jnp.mean(upstream * scaled, axis=1, keepdims=True))


def low_half(rows):
    lane = lax.broadcasted_iota(jnp.int32, (rows, LANES), 1)
    return lane % 64 < 32


def rope(field, cosine, sine, direction):
    partner = jnp.where(
        low_half(field.shape[0]),
        pltpu.roll(field, 96, 1),
        pltpu.roll(field, 32, 1),
    )
    if direction > 0:
        return field * cosine + partner * sine
    return field * cosine - partner * sine


def split_heads(block):
    lane = lax.broadcasted_iota(jnp.int32, block.shape, 1)
    zero = jnp.zeros_like(block)
    return jnp.concatenate(
        [jnp.where(lane < 64, block, zero), jnp.where(lane >= 64, block, zero)], axis=0
    )


def join_heads(turned):
    count = turned.shape[1] // 2
    row = lax.broadcasted_iota(jnp.int32, (LANES, count), 0)
    return jnp.where(row < 64, turned[:, :count], turned[:, count:]).T


def meet(partners):
    barrier = pltpu.get_barrier_semaphore()
    total = 0
    for condition, device in partners:

        @pl.when(condition)
        def _(device=device):
            pl.semaphore_signal(barrier, inc=1, device_id=device, device_id_type=MESH)

        total = total + condition.astype(jnp.int32)
    pl.semaphore_wait(barrier, total)


def layers_kernel(
    late, tokens, cotangent, lengths,
    w_query, w_key, w_value, w_output, w_gate, w_up, w_down,
    gain_attn, gain_mlp, trig,
    block_out, grad_out, normed_out, att_out, n2_out, prod_out,
    g_out, db_out, dg_out, du_out, dq_out, dk_out, dv_out, own_out, halo_part_out, gains_out,
    wq, wk, wv, wo, wg, wu, wd,
    xs, qs, ks, vs, probs, slope, silu, mixed, normed, att, n2, prod, outs, gs,
    halo_in, halo_out, branch, d_att, d_norm, d_own, cosine, sine, first_key, bias, scale,
    wide_f, left_b, right_b, key_f, value_f,
    weight_sem, trig_sem, late_sem, token_sem, cot_sem, save_sem, out_sem,
    halo_send, halo_recv, hand_send, hand_recv, back_send, back_recv, turn_send, turn_recv,
):
    section, wide = lax.axis_index("section"), lax.axis_index("wide")
    last_section, last_wide = lax.axis_size("section") - 1, lax.axis_size("wide") - 1
    batches, rows, width = tokens.shape
    hidden_width = wg.shape[1]
    half = rows // 2
    band = rows + half
    pairs = width // LANES
    own, halo = pl.ds(rows, rows), pl.ds(0, rows)
    has_left, has_right = wide > 0, wide < last_wide
    has_before, has_after = section > 0, section < last_section
    is_first, is_last = jnp.logical_not(has_before), jnp.logical_not(has_after)

    weights = ((w_query, wq), (w_key, wk), (w_value, wv), (w_output, wo),
               (w_gate, wg), (w_up, wu), (w_down, wd))

    def weight_copy(index):
        source, target = weights[index]
        return pltpu.make_async_copy(source.at[0], target, weight_sem.at[index])

    def token_copy(mb):
        return pltpu.make_async_copy(tokens.at[mb], xs.at[mb, own], token_sem.at[mb])

    def cot_copy(mb):
        return pltpu.make_async_copy(cotangent.at[mb], gs.at[mb], cot_sem.at[mb])

    pieces = range(rows // PIECE)

    def rows_of(piece, base=0):
        return pl.ds(base + piece * PIECE, PIECE)

    def halo_copy(mb, piece, source):
        return pltpu.make_async_remote_copy(
            source, xs.at[mb, rows_of(piece)], halo_send.at[mb, piece], halo_recv.at[mb, piece],
            device_id={"wide": wide + 1}, device_id_type=MESH)

    def own_halo_copy(mb, piece):
        return halo_copy(mb, piece, xs.at[mb, rows_of(piece, rows)])

    def token_halo_copy(mb, piece):
        return halo_copy(mb, piece, tokens.at[mb, rows_of(piece)])

    def hand_copy(mb, piece):
        return pltpu.make_async_remote_copy(
            outs.at[mb, rows_of(piece)], xs.at[mb, rows_of(piece, rows)],
            hand_send.at[mb, piece], hand_recv.at[mb, piece],
            device_id={"section": section + 1}, device_id_type=MESH)

    def back_copy(mb, piece):
        return pltpu.make_async_remote_copy(
            halo_out.at[rows_of(piece)], halo_in.at[mb, rows_of(piece)],
            back_send.at[mb, piece], back_recv.at[mb, piece],
            device_id={"wide": wide - 1}, device_id_type=MESH)

    def turn_copy(mb, piece):
        return pltpu.make_async_remote_copy(
            outs.at[mb, rows_of(piece)], gs.at[mb, rows_of(piece)],
            turn_send.at[mb, piece], turn_recv.at[mb, piece],
            device_id={"section": section - 1}, device_id_type=MESH)

    def relay(mb):
        for piece in pieces:
            hand_copy(mb, piece).wait_recv()

            @pl.when(has_right)
            def _(piece=piece):
                own_halo_copy(mb, piece).start()

    def out_copy(mb, target):
        return pltpu.make_async_copy(outs.at[mb], target.at[mb], out_sem.at[mb])

    def save(name, mb):
        source, target, index = {
            "normed": (normed, normed_out, 0), "att": (att, att_out, 1), "n2": (n2, n2_out, 2),
            "prod": (prod, prod_out, 3), "branch": (branch.at[lax.rem(mb, 2)], db_out, 4),
            "g": (gs.at[mb], g_out, 5), "dg": (slope.at[mb], dg_out, 6), "du": (silu.at[mb], du_out, 7),
            "dq": (qs.at[mb], dq_out, 8), "dk": (ks.at[mb], dk_out, 9), "dv": (vs.at[mb], dv_out, 10),
        }[name]
        return pltpu.make_async_copy(source, target.at[mb], save_sem.at[index, mb])

    def saved_before(name, mb):
        @pl.when(mb > 0)
        def _():
            save(name, mb - 1).wait()

    @pl.when(is_first)
    def _():
        token_copy(0).start()

    trig_copy = pltpu.make_async_copy(trig, left_b, trig_sem.at[0])
    trig_copy.start()
    for index in range(3):
        weight_copy(index).start()

    meet([
        (has_left, {"wide": wide - 1}), (has_right, {"wide": wide + 1}),
        (has_before, {"section": section - 1}), (has_after, {"section": section + 1}),
    ])

    @pl.when(is_first & has_right)
    def _():
        for piece in pieces:
            token_halo_copy(0, piece).start()

    @pl.when(is_first)
    def _():
        for mb in range(1, batches):
            token_copy(mb).start()

    @pl.when(is_last)
    def _():
        for mb in range(batches):
            cot_copy(mb).start()

    @pl.when(jnp.logical_not(has_left))
    def _():
        xs[:, halo, :] = jnp.zeros((batches, rows, width), BF16)

    @pl.when(jnp.logical_not(has_right))
    def _():
        halo_in[...] = jnp.zeros(halo_in.shape, BF16)

    gains_out[...] = jnp.zeros(gains_out.shape, F32)

    start_row = wide * rows

    def tables(mb, carry):
        positions = lax.broadcasted_iota(jnp.int32, (2 * rows, LANES), 0) + (start_row - rows)
        query_at = lax.broadcasted_iota(jnp.int32, (8, rows), 1) + start_row

        def later(image, state):
            start, first, first_row = state
            first = jnp.where(positions >= start, start, first)
            first_row = jnp.where(query_at >= start, start, first_row)
            return (start + lengths[mb, image], first, first_row)

        _, first, first_row = lax.fori_loop(
            0, lengths.shape[1], later,
            (jnp.int32(0), jnp.zeros((2 * rows, LANES), jnp.int32), jnp.zeros((8, rows), jnp.int32)))
        offsets = positions - first
        lane = lax.broadcasted_iota(jnp.int32, (2 * rows, LANES), 1)
        one_hot = jnp.concatenate(
            [jnp.where(offsets == lane + base, 1.0, 0.0).astype(BF16) for base in range(0, band, LANES)],
            axis=1)
        for which, table in enumerate((cosine, sine)):
            parts = dot(one_hot, left_b[which])
            table[mb] = parts[:, :LANES] + parts[:, LANES:]
        first_key[mb] = first_row - start_row
        return carry

    trig_copy.wait()
    lax.fori_loop(0, batches, tables, 0)

    items = [(pair, block) for pair in range(pairs) for block in range(2)]

    def place(index):
        pair, block = items[index]
        lanes = slice(pair * LANES, (pair + 1) * LANES)
        low = block * half
        return lanes, slice(low, low + half), slice(low, low + band)

    def pipelined(first, second, third):
        first(0)
        for index in range(len(items)):
            if index + 1 < len(items):
                first(index + 1)
            second(index)
            if index:
                third(index - 1)
        third(len(items) - 1)


    def normalise(mb, part):
        for low in range(part.start, part.start + rows, BLOCK):
            at = slice(low, low + BLOCK)
            scaled, _ = rms_parts(xs[mb, at, :].astype(F32))
            normed[at, :] = (scaled * gain_attn[...]).astype(BF16)

    def keys_values(mb, part):
        cos_rows, sin_rows = cosine[mb, part, :], sine[mb, part, :]
        for start in range(0, width, 256):
            rows_n = normed[part, :]
            keys = dot(rows_n, wk[:, start:start + 256])
            for inner in range(0, 256, LANES):
                ks[mb, part, start + inner:start + inner + LANES] = rope(
                    keys[:, inner:inner + LANES], cos_rows, sin_rows, 1).astype(BF16)
            vs[mb, part, start:start + 256] = dot(rows_n, wv[:, start:start + 256]).astype(BF16)

    def attention(mb):
        def scores(index):
            lanes, here, near = place(index)
            wide_f[index % 2] = dot_nt(ks[mb, near, lanes], split_heads(qs[mb, here, lanes]))

        def soften(index):
            pair, block = items[index]
            for head in range(2):
                at = slice(head * LANES, (head + 1) * LANES)
                masked = wide_f[index % 2, :, at] + bias[block]
                raw = jnp.exp(masked - jnp.max(masked, axis=0, keepdims=True))
                probs[mb, pair, block, :, at] = raw.astype(BF16)

        def collect(index):
            pair, block = items[index]
            lanes, here, near = place(index)
            left = jnp.concatenate([vs[mb, near, lanes].T, jnp.ones((16, band), BF16)], axis=0)
            turned = dot(left, probs[mb, pair, block])
            inverse = 1.0 / turned[LANES:LANES + 1]
            scale[mb, index] = inverse
            att[here, lanes] = join_heads(turned[:LANES] * inverse).astype(BF16)

        pipelined(scores, soften, collect)

    def forward(mb, carry):
        @pl.when(is_first)
        def _():
            token_copy(mb).wait()

            @pl.when(has_right & (mb + 1 < batches))
            def _():
                for piece in pieces:
                    token_halo_copy(mb + 1, piece).start()

        @pl.when(has_before & (mb == 0))
        def _():
            relay(mb)

        saved_before("normed", mb)
        normalise(mb, own)

        @pl.when(mb == 0)
        def _():
            for index in range(3):
                weight_copy(index).wait()
            for index in range(3, 7):
                weight_copy(index).start()

        cos_rows, sin_rows = cosine[mb, own, :], sine[mb, own, :]
        for start in range(0, width, 256):
            queries = dot(normed[own, :], wq[:, start:start + 256])
            for inner in range(0, 256, LANES):
                turned = rope(queries[:, inner:inner + LANES], cos_rows, sin_rows, 1)
                qs[mb, :, start + inner:start + inner + LANES] = (turned * 0.125).astype(BF16)
        keys_values(mb, own)
        for block in range(2):
            key_at = lax.broadcasted_iota(jnp.int32, (band, half), 0) + (block * half - rows)
            query_at = lax.broadcasted_iota(jnp.int32, (band, half), 1) + block * half
            first = first_key[mb, 0:1, block * half:(block + 1) * half]
            bias[block] = jnp.where((key_at >= first) & (key_at <= query_at), 0.0, -1e30)

        @pl.when(has_left)
        def _():
            for piece in pieces:
                own_halo_copy(mb, piece).wait_recv()

        normalise(mb, halo)
        keys_values(mb, halo)
        save("normed", mb).start()
        saved_before("att", mb)
        attention(mb)
        save("att", mb).start()

        @pl.when(mb == 0)
        def _():
            for index in range(3, 7):
                weight_copy(index).wait()

        saved_before("n2", mb)
        for start in range(0, width, 256):
            at = slice(start, start + 256)
            d_norm[:, at] = xs[mb, own, at].astype(F32) + dot(att[...], wo[:, at])
        for low in range(0, rows, BLOCK):
            at = slice(low, low + BLOCK)
            total = d_norm[at, :]
            scaled, _ = rms_parts(total)
            mixed[mb, at, :] = total.astype(BF16)
            n2[at, :] = (scaled * gain_mlp[...]).astype(BF16)
        save("n2", mb).start()

        @pl.when(has_before & (mb + 1 < batches))
        def _():
            relay(mb + 1)

        saved_before("prod", mb)
        for start in range(0, hidden_width, 256):
            at = slice(start, start + 256)
            gate = dot(n2[...], wg[:, at])
            up = dot(n2[...], wu[:, at])
            sigma = jax.nn.sigmoid(gate)
            gated = gate * sigma
            prod[:, at] = (gated * up).astype(BF16)
            silu[mb, :, at] = gated.astype(BF16)
            slope[mb, :, at] = (up * (sigma * (1.0 + gate * (1.0 - sigma)))).astype(BF16)
        save("prod", mb).start()
        for start in range(0, width, 256):
            at = slice(start, start + 256)
            outs[mb, :, at] = (d_norm[:, at] + dot(prod[...], wd[:, at])).astype(BF16)

        @pl.when(has_after)
        def _():
            for piece in pieces:
                hand_copy(mb, piece).start()

        out_copy(mb, block_out).start()
        return carry

    lax.fori_loop(0, batches, forward, 0)

    for name in ("normed", "att", "n2", "prod"):
        save(name, batches - 1).wait()
    for mb in range(batches):
        out_copy(mb, block_out).wait()

    @pl.when(has_after)
    def _():
        for mb in range(batches):
            for piece in pieces:
                hand_copy(mb, piece).wait_send()


    def add_gain(which, product):
        folded = jnp.sum(product.reshape(product.shape[0] // 8, 8, width), axis=0)
        at = pl.ds(8 * which, 8)
        gains_out[at, :] = gains_out[at, :] + folded

    def attention_back(mb):
        def d_weights(index):
            lanes, here, near = place(index)
            wide_f[index % 2] = dot_nt(vs[mb, near, lanes], split_heads(d_att[here, lanes]))

        def d_soften(index):
            pair, block = items[index]
            for head in range(2):
                at = slice(head * LANES, (head + 1) * LANES)
                weight = probs[mb, pair, block, :, at].astype(F32) * scale[mb, index, :, at]
                moved = weight * wide_f[index % 2, :, at]
                centre = jnp.sum(moved, axis=0, keepdims=True)
                left_b[index % 2, :, at] = (moved - weight * centre).astype(BF16)
                right_b[index % 2, :, at] = weight.astype(BF16)

        def collect(index):
            pair, block = items[index]
            lanes, here, near = place(index)
            d_scores = left_b[index % 2]
            d_keys = dot(d_scores, split_heads(qs[mb, here, lanes]))
            d_values = dot(right_b[index % 2], split_heads(d_att[here, lanes]))
            turned = lax.dot_general(
                ks[mb, near, lanes], d_scores, (((0,), (0,)), ((), ())), preferred_element_type=F32)
            at = pl.ds(rows + block * half, half)
            qs[mb, here, lanes] = rope(
                join_heads(turned) * 0.125, cosine[mb, at, :], sine[mb, at, :], -1).astype(BF16)
            slot = pair % 2
            if block == 0:
                key_f[slot], value_f[slot] = d_keys, d_values
                return
            earlier_k, earlier_v = key_f[slot], value_f[slot]
            pieces = (
                (0, half, earlier_k[:half], earlier_v[:half]),
                (half, band, earlier_k[half:] + d_keys[:rows], earlier_v[half:] + d_values[:rows]),
                (band, 2 * rows, d_keys[rows:], d_values[rows:]),
            )
            for low, high, piece_k, piece_v in pieces:
                ks[mb, low:high, lanes] = rope(
                    piece_k, cosine[mb, low:high, :], sine[mb, low:high, :], -1).astype(BF16)
                vs[mb, low:high, lanes] = piece_v.astype(BF16)

        pipelined(d_weights, d_soften, collect)

    def closes(mb):
        return has_before | (mb < batches - 1) if late else wide >= 0

    def finish(mb):
        for piece in pieces:
            @pl.when(has_right)
            def _(piece=piece):
                back_copy(mb, piece).wait_recv()

            for low in range(piece * PIECE, (piece + 1) * PIECE, BLOCK):
                at = pl.ds(low, BLOCK)
                scaled, inverse = rms_parts(xs[mb, pl.ds(rows + low, BLOCK), :].astype(F32))
                d_normed = d_own[at, :] + halo_in[mb, at, :].astype(F32)
                add_gain(0, d_normed * scaled)
                back = rms_back(d_normed * gain_attn[...], scaled, inverse)
                outs[mb, at, :] = (branch[lax.rem(mb, 2), at, :].astype(F32) + back).astype(BF16)

            @pl.when(has_before)
            def _(piece=piece):
                turn_copy(mb, piece).start()

        out_copy(mb, grad_out).start()

    def backward(mb, carry):
        @pl.when(is_last)
        def _():
            cot_copy(mb).wait()

        @pl.when(has_after)
        def _():
            for piece in pieces:
                turn_copy(mb, piece).wait_recv()

        save("g", mb).start()
        for start in range(0, hidden_width, 256):
            at = slice(start, start + 256)
            d_product = dot_nt(gs[mb], wd[at, :])
            slope[mb, :, at] = (d_product * slope[mb, :, at].astype(F32)).astype(BF16)
            silu[mb, :, at] = (d_product * silu[mb, :, at].astype(F32)).astype(BF16)
        save("dg", mb).start()
        save("du", mb).start()
        for start in range(0, width, 256):
            at = slice(start, start + 256)
            d_norm[:, at] = dot_nt(slope[mb], wg[at, :]) + dot_nt(silu[mb], wu[at, :])
        slot = lax.rem(mb, 2)

        @pl.when(mb >= 2)
        def _():
            save("branch", mb - 2).wait()

        for low in range(0, rows, BLOCK):
            at = slice(low, low + BLOCK)
            scaled, inverse = rms_parts(mixed[mb, at, :].astype(F32))
            d_normed = d_norm[at, :]
            add_gain(1, d_normed * scaled)
            total = gs[mb, at, :].astype(F32) + rms_back(d_normed * gain_mlp[...], scaled, inverse)
            branch[slot, at, :] = total.astype(BF16)
        save("branch", mb).start()
        for start in range(0, width, 256):
            at = slice(start, start + 256)
            d_att[:, at] = dot_nt(branch[slot], wo[at, :]).astype(BF16)

        @pl.when(mb > 0)
        def _():
            finish(mb - 1)

        attention_back(mb)
        save("dq", mb).start()
        save("dk", mb).start()
        save("dv", mb).start()

        @pl.when(has_left & (mb > 0))
        def _():
            for piece in pieces:
                back_copy(mb - 1, piece).wait_send()

        for start in range(0, width, 256):
            at = slice(start, start + 256)
            halo_out[:, at] = (
                dot_nt(ks[mb, halo, :], wk[at, :]) + dot_nt(vs[mb, halo, :], wv[at, :])).astype(BF16)

        @pl.when(has_left & closes(mb))
        def _():
            for piece in pieces:
                back_copy(mb, piece).start()

        for start in range(0, width, 256):
            at = slice(start, start + 256)
            d_own[:, at] = (
                dot_nt(qs[mb], wq[at, :]) + dot_nt(ks[mb, own, :], wk[at, :])
                + dot_nt(vs[mb, own, :], wv[at, :]))
        return carry

    lax.fori_loop(0, batches, backward, 0)
    closed = closes(batches - 1)

    @pl.when(closed)
    def _():
        finish(batches - 1)

    @pl.when(jnp.logical_not(closed))
    def _():
        copies = [pltpu.make_async_copy(d_own, own_out, late_sem.at[0]),
                  pltpu.make_async_copy(halo_out, halo_part_out, late_sem.at[1])]
        for copy in copies:
            copy.start()
        for copy in copies:
            copy.wait()

    for mb in range(batches - 2, batches):
        save("branch", mb).wait()
    for mb in range(batches):
        for name in ("g", "dg", "du", "dq", "dk", "dv"):
            save(name, mb).wait()
    for mb in range(batches - 1):
        out_copy(mb, grad_out).wait()

    @pl.when(closed)
    def _():
        out_copy(batches - 1, grad_out).wait()

    @pl.when(has_left & closed)
    def _():
        for piece in pieces:
            back_copy(batches - 1, piece).wait_send()

    @pl.when(has_before)
    def _():
        for mb in range(batches):
            for piece in pieces:
                turn_copy(mb, piece).wait_send()

    @pl.when(has_right)
    def _():
        for mb in range(batches):
            for piece in pieces:
                own_halo_copy(mb, piece).wait_send()


def any_spec():
    return pl.BlockSpec(memory_space=pl.ANY)


def vmem_spec():
    return pl.BlockSpec(memory_space=pltpu.VMEM)


def trig_table(head_dim, reach):
    half_dim = head_dim // 2
    freqs = np.float32(THETA) ** (-np.arange(half_dim, dtype=np.float32) * np.float32(2.0) / np.float32(head_dim))
    angles = np.arange(reach, dtype=np.float32)[:, None] * np.tile(freqs, LANES // half_dim)[None, :]
    sign = np.tile(np.repeat(np.array([-1.0, 1.0], np.float32), half_dim), LANES // head_dim)
    parts = []
    for table in (np.cos(angles), np.sin(angles) * sign):
        high = table.astype(ml_dtypes.bfloat16)
        low = (table - high.astype(np.float32)).astype(ml_dtypes.bfloat16)
        parts.append(np.concatenate([high, low], axis=1))
    return jnp.asarray(np.stack(parts))


def run_layers(tokens, cotangent, lengths, weights, gain_attn, gain_mlp, late=False):
    batches, rows, width = tokens.shape
    hidden_width = weights[4].shape[2]
    pairs = width // LANES
    band = rows + rows // 2
    one = (batches, rows, width)
    two = (batches, 2 * rows, width)
    wide = (batches, rows, hidden_width)
    outs = [(one, BF16), (one, BF16), (two, BF16), (one, BF16), (one, BF16), (wide, BF16),
            (one, BF16), (one, BF16), (wide, BF16), (wide, BF16), (one, BF16), (two, BF16), (two, BF16),
            (one[1:], F32), (one[1:], BF16), ((16, width), F32)]
    dma = pltpu.SemaphoreType.DMA
    scratch = [pltpu.VMEM(w.shape[1:], BF16) for w in weights] + [
        pltpu.VMEM(two, BF16),
        pltpu.VMEM(one, BF16),
        pltpu.VMEM(two, BF16),
        pltpu.VMEM(two, BF16),
        pltpu.VMEM((batches, pairs, 2, band, rows), BF16),
        pltpu.VMEM(wide, BF16),
        pltpu.VMEM(wide, BF16),
        pltpu.VMEM(one, BF16),
        pltpu.VMEM(two[1:], BF16),
        pltpu.VMEM(one[1:], BF16),
        pltpu.VMEM(one[1:], BF16),
        pltpu.VMEM(wide[1:], BF16),
        pltpu.VMEM(one, BF16),
        pltpu.VMEM(one, BF16),
        pltpu.VMEM(one, BF16),
        pltpu.VMEM(one[1:], BF16),
        pltpu.VMEM((2,) + one[1:], BF16),
        pltpu.VMEM(one[1:], BF16),
        pltpu.VMEM(one[1:], F32),
        pltpu.VMEM(one[1:], F32),
        pltpu.VMEM((batches, 2 * rows, LANES), F32),
        pltpu.VMEM((batches, 2 * rows, LANES), F32),
        pltpu.VMEM((batches, 8, rows), jnp.int32),
        pltpu.VMEM((2, band, rows // 2), F32),
        pltpu.VMEM((batches, 2 * pairs, 1, rows), F32),
        pltpu.VMEM((2, band, rows), F32),
        pltpu.VMEM((2, band, rows), BF16),
        pltpu.VMEM((2, band, rows), BF16),
        pltpu.VMEM((2, band, LANES), F32),
        pltpu.VMEM((2, band, LANES), F32),
        dma((7,)), dma((1,)), dma((2,)), dma((batches,)), dma((batches,)), dma((11, batches)),
    ] + [dma((batches,))] + [dma((batches, rows // PIECE))] * 8
    trig = trig_table(width // HEADS, band)
    return pl.pallas_call(
        functools.partial(layers_kernel, late),
        out_shape=[jax.ShapeDtypeStruct(shape, dtype) for shape, dtype in outs],
        in_specs=[any_spec()] * 2 + [pl.BlockSpec(memory_space=pltpu.SMEM)] + [any_spec()] * 7 + [vmem_spec()] * 2 + [any_spec()],
        out_specs=[any_spec()] * 15 + [vmem_spec()],
        scratch_shapes=scratch,
        compiler_params=pltpu.CompilerParams(
            collective_id=1, has_side_effects=True, vmem_limit_bytes=VMEM_BYTES),
        name="layers",
    )(tokens, cotangent, lengths, *weights, gain_attn, gain_mlp, trig)


LAG = 3
SENDS = 4
LAG_PAIR = 1
LENT = 3
MIX = 6
LATE = 8
CHUNK = 256


def dot_tn(left, right):
    return lax.dot_general(
        left, right, (((0,), (0,)), ((), ())), preferred_element_type=F32
    )


class Ladder:
    def __init__(self, refs, sems, outer, chunks):
        self.computed = chunks
        self.dw, self.a_out, self.a_in, self.b_out, self.b_own, self.b_in, self.c_out, self.c_own, self.c_in, self.result = refs
        self.a_send, self.a_recv, self.b_send, self.b_recv, self.c_send, self.c_recv = sems
        wide = lax.axis_index("wide")
        self.outer = outer
        self.core, self.side, self.depth = lax.rem(wide, 2), lax.rem(wide // 2, 2), wide // 4
        self.core_mate = {"wide": wide + 1 - 2 * self.core}
        self.side_mate = {"wide": wide + 2 - 4 * self.side}
        self.column = lax.rem(wide, 4)
        self.first, self.count = 0, chunks
        self.lent = None

    def lend(self, refs, sems, section):
        self.x_out, self.x_in, self.r_out, self.r_in = refs
        self.x_send, self.x_recv, self.r_send, self.r_recv = sems
        self.lender = section == 0
        self.lent = self.x_in.shape[0]
        self.partner = {"section": 1 - section}
        self.first = jnp.where(self.lender, self.lent, 0)
        self.count = jnp.where(self.lender, self.computed, self.computed + self.lent)

    def x_copy(self, j):
        return pltpu.make_async_remote_copy(
            self.x_out.at[j], self.x_in.at[j], self.x_send.at[j], self.x_recv.at[j],
            device_id=self.partner, device_id_type=MESH)

    def r_copy(self, j):
        return pltpu.make_async_remote_copy(
            self.r_out.at[j], self.r_in.at[j], self.r_send.at[j], self.r_recv.at[j],
            device_id=self.partner, device_id_type=MESH)

    def stage_x(self, j):
        held = lax.rem(j, LAG + 1)

        self.a_copy(j).wait_recv()
        for index in range(2 * self.outer):
            self.x_out[j, index] = (
                self.dw[held, 2 * index + self.core] + self.a_in[j, index].astype(F32)).astype(BF16)
        self.x_copy(j).start()

    def a_copy(self, j):
        slot = lax.rem(j, SENDS)
        return pltpu.make_async_remote_copy(
            self.a_out.at[slot], self.a_in.at[j], self.a_send.at[slot], self.a_recv.at[j],
            device_id=self.core_mate, device_id_type=MESH)

    def b_copy(self, j):
        slot = lax.rem(j, SENDS)
        return pltpu.make_async_remote_copy(
            self.b_out.at[slot], self.b_in.at[j], self.b_send.at[slot], self.b_recv.at[j],
            device_id=self.side_mate, device_id_type=MESH)

    def c_copy(self, j, step, arriving):
        slot = lax.rem(j, SENDS)
        peer = lax.rem(self.depth + step, self.outer)
        sender = peer if arriving else self.depth
        return pltpu.make_async_remote_copy(
            self.c_out.at[slot, peer], self.c_in.at[j, sender], self.c_send.at[slot, step], self.c_recv.at[j, sender],
            device_id={"wide": peer * 4 + self.column}, device_id_type=MESH)

    def stage_a(self, j):
        slot, held = lax.rem(j, SENDS), lax.rem(j, LAG + 1)

        @pl.when(j >= SENDS)
        def _():
            self.a_copy(j - SENDS).wait_send()

        for index in range(2 * self.outer):
            self.a_out[slot, index] = self.dw[held, 2 * index + 1 - self.core].astype(BF16)
        self.a_copy(j).start()

    def stage_b(self, j):
        slot, held = lax.rem(j, SENDS), lax.rem(j, LAG + 1)

        @pl.when(j >= SENDS + self.first)
        def _():
            self.b_copy(j - SENDS).wait_send()

        def split():
            self.a_copy(j).wait_recv()
            for index in range(self.outer):
                far, near = 2 * index + 1 - self.side, 2 * index + self.side
                self.b_out[slot, index] = (
                    self.dw[held, 2 * far + self.core] + self.a_in[j, far].astype(F32)).astype(BF16)
                self.b_own[held, index] = self.dw[held, 2 * near + self.core] + self.a_in[j, near].astype(F32)

        if self.lent is None:
            split()
        else:
            pl.when(j < self.computed)(split)

            @pl.when(j >= self.computed)
            def _():
                borrowed = j - self.computed
                self.x_copy(borrowed).wait_recv()
                for index in range(self.outer):
                    self.b_out[slot, index] = self.x_in[borrowed, 2 * index + 1 - self.side]
                    self.b_own[held, index] = self.x_in[borrowed, 2 * index + self.side].astype(F32)

        self.b_copy(j).start()

    def stage_c(self, j):
        slot, held = lax.rem(j, SENDS), lax.rem(j, LAG + 1)

        @pl.when(j >= SENDS + self.first)
        def _():
            for step in range(1, self.outer):
                self.c_copy(j - SENDS, step, False).wait_send()

        self.b_copy(j).wait_recv()
        for index in range(self.outer):
            self.c_out[slot, index] = (self.b_own[held, index] + self.b_in[j, index].astype(F32)).astype(BF16)
        for step in range(1, self.outer):
            self.c_copy(j, step, False).start()
        self.c_own[held] = self.b_own[held, self.depth] + self.b_in[j, self.depth].astype(F32)

    def stage_d(self, j):
        held = lax.rem(j, LAG + 1)
        total = self.c_own[held]
        for step in range(1, self.outer):
            self.c_copy(j, step, True).wait_recv()
        for step in range(1, self.outer):
            total = total + self.c_in[j, lax.rem(self.depth + step, self.outer)].astype(F32)
        if self.lent is None:
            self.result[j] = total
            return

        @pl.when(j < self.computed)
        def _():
            self.result[j] = total

        @pl.when(j >= self.computed)
        def _():
            @pl.when(j == self.computed)
            def _():
                pl.semaphore_wait(pltpu.get_barrier_semaphore(), 1)

            self.r_out[j - self.computed] = total
            self.r_copy(j - self.computed).start()

    def drain(self):
        for back in range(1, SENDS + 1):
            self.a_copy(self.computed - back).wait_send()
            j = self.count - back

            @pl.when(j >= self.first)
            def _(j=j):
                self.b_copy(j).wait_send()
                for step in range(1, self.outer):
                    self.c_copy(j, step, False).wait_send()

        if self.lent is not None:
            @pl.when(self.lender)
            def _():
                for j in range(self.lent):
                    self.x_copy(j).wait_send()
                    self.r_copy(j).wait_recv()
                    self.result[j] = self.r_in[j]

            @pl.when(jnp.logical_not(self.lender))
            def _():
                for j in range(self.lent):
                    self.r_copy(j).wait_send()


def weight_kernel(
    normed_in, att_in, n2_in, prod_in, g_in, db_in, dg_in, du_in, dq_in, dk_in, dv_in,
    own_in, halo_part_in, tokens, gains, gain_attn,
    out_m, out_d, late_grad,
    normed, att, n2, prod, g, dy, late_own, late_part, late_halo, late_x, late_branch, late_gain, late_sem, *rest,
):
    m_refs, d_refs, lend_refs = rest[:9], rest[9:18], rest[18:22]
    m_sems, d_sems, lend_sems = rest[22:28], rest[28:34], rest[34:38]
    x_sem, dy_sem = rest[38], rest[39]
    section, wide, count = lax.axis_index("section"), lax.axis_index("wide"), lax.axis_size("wide")
    batches, rows, width = g_in.shape
    hidden_width = prod_in.shape[2]
    outer = count // 4
    own = pl.ds(rows, rows)
    m_count, d_count = out_m.shape[0], out_d.shape[0]
    per_wide, per_narrow = hidden_width // CHUNK, width // CHUNK
    ladder_m = Ladder(m_refs + (out_m,), m_sems, outer, m_count)
    ladder_d = Ladder(d_refs + (out_d,), d_sems, outer, d_count)
    ladder_d.lend(lend_refs, lend_sems, section)
    has_left, has_right = wide > 0, wide < count - 1

    late_loads = [
        pltpu.make_async_copy(source, target, late_sem.at[index])
        for index, (source, target) in enumerate((
            (halo_part_in, late_part), (own_in, late_own), (tokens.at[batches - 1], late_x),
            (db_in.at[batches - 1], late_branch)))]
    late_copy = pltpu.make_async_remote_copy(
        late_part, late_halo, late_sem.at[4], late_sem.at[5], device_id={"wide": wide - 1}, device_id_type=MESH)

    def finish_late():
        for copy in late_loads[1:]:
            copy.wait()
        pl.when(has_right)(lambda: late_copy.wait_recv())
        for low in range(0, rows, BLOCK):
            at = pl.ds(low, BLOCK)
            scaled, inverse = rms_parts(late_x[at, :].astype(F32))
            d_normed = late_own[at, :] + late_halo[at, :].astype(F32)
            product = (d_normed * scaled).reshape(BLOCK // 8, 8, width)
            late_gain[...] = late_gain[...] + jnp.sum(product, axis=0)
            back = rms_back(d_normed * gain_attn[...], scaled, inverse)
            late_grad[at, :] = (late_branch[at, :].astype(F32) + back).astype(BF16)


    loads = ((n2_in, n2), (att_in, att), (normed_in, normed), (prod_in, prod), (g_in, g))

    def x_copy(index):
        source, target = loads[index]
        return pltpu.make_async_copy(source, target, x_sem.at[index])

    kinds = ((dg_in, per_wide), (du_in, per_wide), (db_in, per_narrow), (dq_in, per_narrow), (dk_in, per_narrow), (dv_in, per_narrow))

    def each_load(j, act):
        slot = lax.rem(j, 2)
        base = 0
        for index, (source, parts) in enumerate(kinds):
            @pl.when((j >= base) & (j < base + parts))
            def _(source=source, base=base, index=index):
                lanes = pl.ds(pl.multiple_of((j - base) * CHUNK, CHUNK), CHUNK)
                target = dy.at[slot] if index >= 4 else dy.at[slot, :, own]
                act(pltpu.make_async_copy(source.at[:, :, lanes], target, dy_sem.at[slot]))
            base += parts
        return base

    x_copy(0).start()
    each_load(jnp.int32(0), lambda copy: copy.start())

    @pl.when(ladder_d.lender)
    def _():
        for copy in late_loads:
            copy.start()

    for index in (3, 4, 1, 2):
        x_copy(index).start()
    late_gain[...] = jnp.zeros(late_gain.shape, F32)

    @pl.when(jnp.logical_not(has_right))
    def _():
        late_halo[...] = jnp.zeros(late_halo.shape, BF16)

    barrier = pltpu.get_barrier_semaphore()
    peers = [ladder_m.core_mate, ladder_m.side_mate] + [
        {"wide": lax.rem(ladder_m.depth + step, outer) * 4 + ladder_m.column} for step in range(1, outer)]
    for peer in peers:
        pl.semaphore_signal(barrier, inc=1, device_id=peer, device_id_type=MESH)
    for condition, step in ((has_left, -1), (has_right, 1)):
        @pl.when(condition)
        def _(step=step):
            pl.semaphore_signal(barrier, inc=1, device_id={"wide": wide + step}, device_id_type=MESH)
    greeted = len(peers) + has_left.astype(jnp.int32) + has_right.astype(jnp.int32)
    pl.semaphore_wait(barrier, greeted + ladder_d.lender.astype(jnp.int32))
    pl.semaphore_signal(barrier, inc=1, device_id=ladder_d.partner, device_id_type=MESH)

    @pl.when(ladder_d.lender)
    def _():
        late_loads[0].wait()
        pl.when(has_left)(lambda: late_copy.start())


    kv_first = 2 * per_wide + 2 * per_narrow
    kv_last = kv_first + 2 * per_narrow
    narrow_first = 2 * per_wide

    def compute_m(j):
        slot, held = lax.rem(j, 2), lax.rem(j, LAG + 1)

        @pl.when(j + 1 < kv_last)
        def _():
            each_load(j + 1, lambda copy: copy.start())

        def write(left, right):
            product = dot_tn(left.reshape(-1, width), right.reshape(-1, CHUNK))
            ladder_m.dw[held] = product.reshape(ladder_m.dw.shape[1:])

        @pl.when(j < kv_last)
        def _():
            each_load(j, lambda copy: copy.wait())

        for index, first in enumerate((0, narrow_first, narrow_first + per_narrow)):
            @pl.when(j == first)
            def _(index=index):
                x_copy(index).wait()

        @pl.when(j < narrow_first)
        def _():
            write(n2[...], dy[slot, :, own, :])

        @pl.when((j >= narrow_first) & (j < narrow_first + per_narrow))
        def _():
            write(att[...], dy[slot, :, own, :])

        @pl.when((j >= narrow_first + per_narrow) & (j < kv_first))
        def _():
            write(normed[:, own, :], dy[slot, :, own, :])

        @pl.when((j >= kv_first) & (j < kv_last))
        def _():
            write(normed[...], dy[slot])

        @pl.when(j == kv_last)
        def _():
            first = jnp.sum(gains[0:8, :] + late_gain[...], axis=0, keepdims=True)
            second = jnp.sum(gains[8:16, :], axis=0, keepdims=True)
            row = lax.broadcasted_iota(jnp.int32, (LANES, width), 0)
            placed = jnp.where(row == 0, first, jnp.where(row == 1, second, 0.0))
            columns = placed.T
            ladder_m.dw[held] = jnp.concatenate([columns, columns], axis=1).reshape(ladder_m.dw.shape[1:])

    def compute_d(j):
        held = lax.rem(j, LAG + 1)

        @pl.when(j == 0)
        def _():
            x_copy(3).wait()
            x_copy(4).wait()

        lanes = pl.ds(pl.multiple_of(j * LANES, LANES), LANES)
        product = dot_tn(prod[...].reshape(-1, hidden_width), g[:, :, lanes].reshape(-1, LANES))
        ladder_d.dw[held] = product.reshape(ladder_d.dw.shape[1:])

    lent = ladder_d.lent
    lender = ladder_d.lender

    def on_chunk(s, act_m, act_d):
        mixed = s < MIX * lent
        turn, place = s // MIX, lax.rem(s, MIX)
        j_lender = jnp.where(mixed, (MIX - 1) * turn + place, s - lent)
        d_lender = jnp.where(mixed, turn, s - m_count)
        m_turn = jnp.where(lender & mixed, place < MIX - 1, True)
        j_m = jnp.where(lender, j_lender, s)
        j_d = jnp.where(lender, d_lender, s - m_count)
        last_d = ladder_d.count
        is_m = (s >= 0) & (j_m < m_count) & m_turn
        is_d = (s >= 0) & jnp.where(lender & mixed, place == MIX - 1, j_m >= m_count) & (j_d < last_d)

        @pl.when(is_m)
        def _():
            act_m(j_m)

        @pl.when(is_d)
        def _():
            act_d(j_d)

    def own_d(act):
        def guarded(j):
            pl.when(j < d_count)(lambda: act(j))
        return guarded

    def reduced_d(act):
        def guarded(j):
            pl.when(j >= ladder_d.first)(lambda: act(j))
        return guarded

    def second(j):
        pl.when(j < ladder_d.first)(lambda: ladder_d.stage_x(j))
        pl.when(j >= ladder_d.first)(lambda: ladder_d.stage_b(j))

    def step(s, carry):
        pl.when(ladder_d.lender & (s == LATE))(finish_late)
        on_chunk(s, compute_m, own_d(compute_d))
        on_chunk(s, ladder_m.stage_a, own_d(ladder_d.stage_a))
        on_chunk(s - LAG_PAIR, ladder_m.stage_b, second)
        on_chunk(s - LAG_PAIR - LAG, ladder_m.stage_c, reduced_d(ladder_d.stage_c))
        on_chunk(s - LAG_PAIR - 2 * LAG, ladder_m.stage_d, reduced_d(ladder_d.stage_d))
        return carry

    lax.fori_loop(0, m_count + d_count + lent + LAG_PAIR + 2 * LAG, step, 0)
    ladder_m.drain()
    ladder_d.drain()
    pl.when(ladder_d.lender & has_left)(lambda: late_copy.wait_send())


def run_weights(normed, att, n2, prod, g, db, dg, du, dq, dk, dv, own, part, tokens, gains, gain_attn, count):
    batches, rows, width = g.shape
    hidden_width = prod.shape[2]
    outer = count // 4
    m_count = 2 * (hidden_width // CHUNK) + 4 * (width // CHUNK) + 1
    d_count = width // LANES

    def ladder(chunks, lent, block):
        total = chunks + lent
        refs = [
            pltpu.VMEM((LAG + 1, count) + block, F32),
            pltpu.VMEM((SENDS, count // 2) + block, BF16),
            pltpu.VMEM((chunks, count // 2) + block, BF16),
            pltpu.VMEM((SENDS, outer) + block, BF16),
            pltpu.VMEM((LAG + 1, outer) + block, F32),
            pltpu.VMEM((total, outer) + block, BF16),
            pltpu.VMEM((SENDS, outer) + block, BF16),
            pltpu.VMEM((LAG + 1,) + block, F32),
            pltpu.VMEM((total, outer) + block, BF16),
        ]
        sems = [
            pltpu.SemaphoreType.DMA((SENDS,)),
            pltpu.SemaphoreType.DMA((chunks,)),
            pltpu.SemaphoreType.DMA((SENDS,)),
            pltpu.SemaphoreType.DMA((total,)),
            pltpu.SemaphoreType.DMA((SENDS, outer)),
            pltpu.SemaphoreType.DMA((total, outer)),
        ]
        return refs, sems

    block_m, block_d = (width // count, CHUNK), (hidden_width // count, LANES)
    m_refs, m_sems = ladder(m_count, 0, block_m)
    d_refs, d_sems = ladder(d_count, LENT, block_d)
    lend_refs = [
        pltpu.VMEM((LENT, count // 2) + block_d, BF16),
        pltpu.VMEM((LENT, count // 2) + block_d, BF16),
        pltpu.VMEM((LENT,) + block_d, F32),
        pltpu.VMEM((LENT,) + block_d, F32),
    ]
    lend_sems = [pltpu.SemaphoreType.DMA((size,)) for size in (LENT,) * 4]
    return pl.pallas_call(
        weight_kernel,
        out_shape=[
            jax.ShapeDtypeStruct((m_count,) + block_m, F32),
            jax.ShapeDtypeStruct((d_count,) + block_d, F32),
            jax.ShapeDtypeStruct(part.shape, BF16),
        ],
        in_specs=[any_spec()] * 14 + [vmem_spec()] * 2,
        out_specs=[vmem_spec()] * 3,
        scratch_shapes=[
            pltpu.VMEM(normed.shape, BF16),
            pltpu.VMEM(att.shape, BF16),
            pltpu.VMEM(n2.shape, BF16),
            pltpu.VMEM(prod.shape, BF16),
            pltpu.VMEM(g.shape, BF16),
            pltpu.VMEM((2, batches, 2 * rows, CHUNK), BF16),
            pltpu.VMEM(own.shape, F32),
        ] + [pltpu.VMEM(part.shape, BF16)] * 4 + [
            pltpu.VMEM((8, width), F32),
            pltpu.SemaphoreType.DMA((6,)),
        ] + m_refs + d_refs + lend_refs + m_sems + d_sems + lend_sems + [
            pltpu.SemaphoreType.DMA((5,)),
            pltpu.SemaphoreType.DMA((2,)),
        ],
        compiler_params=pltpu.CompilerParams(
            collective_id=3, has_side_effects=True, vmem_limit_bytes=VMEM_BYTES),
        name="weights",
    )(normed, att, n2, prod, g, db, dg, du, dq, dk, dv, own, part, tokens, gains, gain_attn)


def summed_weights(normed, att, n2, prod, g, db, dg, du, dq, dk, dv, gains):
    def outer_sum(left, right):
        total = lax.dot_general(
            left, right, (((0, 1), (0, 1)), ((), ())), preferred_element_type=F32)
        return lax.psum_scatter(total[None], "wide", scatter_dimension=1, tiled=True)

    rows = g.shape[1]
    normed_own = normed[:, rows:]
    gain_rows = gains.reshape(2, 8, -1).sum(axis=1)
    gain_parts = [
        lax.psum_scatter(gain_rows[i:i + 1], "wide", scatter_dimension=1, tiled=True) for i in range(2)]
    return (
        outer_sum(normed_own, dq), outer_sum(normed, dk), outer_sum(normed, dv), outer_sum(att, db),
        outer_sum(n2, dg), outer_sum(n2, du), outer_sum(prod, g), *gain_parts,
    )


def arrange_kernel(sizes, block, grads, late, chunks_m, chunks_d, block_out, grad_out, *rest):
    outs, (held_block, held_grads, held_m, held_d), (load_sem, store_sem) = rest[:9], rest[9:13], rest[13:]
    batches = block.shape[0]
    loads, stores = [], []
    for mb in range(batches):
        loads += [(block.at[mb], held_block.at[mb]), (grads.at[mb], held_grads.at[mb])]
        stores += [(held_block.at[mb], block_out.at[0, mb]), (held_grads.at[mb], grad_out.at[0, mb])]
    first_load = len(loads)
    loads += [(chunks_m, held_m), (chunks_d, held_d)]
    base = 0
    for size, index in zip(sizes, (4, 5, 3, 0, 1, 2)):
        for part in range(size):
            stores.append((held_m.at[base + part], outs[index].at[0, :, pl.ds(part * CHUNK, CHUNK)]))
        base += size
    for part in range(chunks_d.shape[0]):
        stores.append((held_d.at[part], outs[6].at[0, :, pl.ds(part * LANES, LANES)]))
    loads = [pltpu.make_async_copy(*pair, load_sem.at[index]) for index, pair in enumerate(loads)]
    stores = [pltpu.make_async_copy(*pair, store_sem.at[index]) for index, pair in enumerate(stores)]
    is_late = lax.axis_index("section") == 0
    last = first_load - 1
    late_load = pltpu.make_async_copy(late, held_grads.at[batches - 1], load_sem.at[last])
    pl.when(is_late)(lambda: late_load.start())
    pl.when(jnp.logical_not(is_late))(lambda: loads[last].start())
    for index, copy in enumerate(loads):
        if index != last:
            copy.start()
    for index in range(first_load):
        loads[index].wait()
        stores[index].start()
    for copy in loads[first_load:]:
        copy.wait()
    for copy in stores[first_load:]:
        copy.start()
    turned = held_m[base, :, :LANES].T
    outs[7][...] = turned[0:1, :]
    outs[8][...] = turned[1:2, :]
    for copy in stores:
        copy.wait()


def arrange(block, grads, late, chunks_m, chunks_d, sizes):
    own, own_d = chunks_m.shape[1], chunks_d.shape[1]
    width, hidden_width = block.shape[2], CHUNK * sizes[0]
    shapes = [(1,) + block.shape] * 2
    narrow, broad = (1, own, width), (1, own, hidden_width)
    matrices = [narrow] * 4 + [broad] * 2 + [(1, own_d, width)]
    out_shape = [jax.ShapeDtypeStruct(shape, BF16) for shape in shapes]
    out_shape += [jax.ShapeDtypeStruct(shape, F32) for shape in matrices + [(1, own)] * 2]
    copies = sum(sizes) + chunks_d.shape[0] + 2 * block.shape[0]
    return pl.pallas_call(
        functools.partial(arrange_kernel, sizes),
        out_shape=out_shape,
        in_specs=[any_spec()] * 5,
        out_specs=[any_spec()] * 9 + [vmem_spec()] * 2,
        scratch_shapes=[pltpu.VMEM(held.shape, held.dtype) for held in (block, grads, chunks_m, chunks_d)]
        + [pltpu.SemaphoreType.DMA((2 * block.shape[0] + 2,)), pltpu.SemaphoreType.DMA((copies,))],
        compiler_params=pltpu.CompilerParams(vmem_limit_bytes=VMEM_BYTES),
        name="arrange",
    )(block, grads, late, chunks_m, chunks_d)


def per_device(
    tokens, cotangent, seg_lengths, w_query, w_key, w_value, w_output, w_gate, w_up, w_down, gain_attn, gain_mlp,
):
    weights = (w_query, w_key, w_value, w_output, w_gate, w_up, w_down)
    lengths = seg_lengths.reshape(seg_lengths.shape[0], -1)
    count = lax.axis_size("wide")
    width, hidden_width = w_gate.shape[1:]
    whole_tiles = count % 4 == 0 and width % (16 * count) == 0 and hidden_width % (16 * count) == 0
    block_out, input_grads, *saved, own, part, gains = run_layers(
        tokens, cotangent, lengths, weights, gain_attn, gain_mlp, late=whole_tiles)
    if not whole_tiles:
        return (block_out[None], input_grads[None], *summed_weights(*saved, gains))
    out_m, out_d, late = run_weights(*saved, own, part, tokens, gains, gain_attn, count)
    sizes = (hidden_width // CHUNK,) * 2 + (width // CHUNK,) * 4
    return tuple(arrange(block_out, input_grads, late, out_m, out_d, sizes))


def solution(mesh):
    in_specs = (
        P(None, "wide", None),
        P(None, "wide", None),
        P(),
        *[P("section", None, None)] * 7,
        *[P("section", None)] * 2,
    )
    out_specs = (
        *[P("section", None, "wide", None)] * 2,
        *[P("section", "wide", None)] * 7,
        *[P("section", "wide")] * 2,
    )
    return jax.shard_map(
        per_device, mesh=mesh, in_specs=in_specs, out_specs=out_specs, check_vma=False
    )
```

```python
import functools

import jax
import jax.numpy as jnp
import ml_dtypes
import numpy as np
from jax import lax
from jax.experimental import pallas as pl
from jax.experimental.pallas import tpu as pltpu
from jax.sharding import PartitionSpec as P

HEADS = 12
EPS = 1e-05
THETA = 10000.0

F32 = jnp.float32
BF16 = jnp.bfloat16
MESH = pl.DeviceIdType.MESH
LANES = 128
BLOCK = 64
PIECE = 256
VMEM_BYTES = 63 * 1024 * 1024


def dot(left, right):
    return jnp.dot(left, right, preferred_element_type=F32)


def dot_nt(left, right):
    return lax.dot_general(
        left, right, (((1,), (1,)), ((), ())), preferred_element_type=F32
    )


def rms_parts(hidden):
    inverse = lax.rsqrt(jnp.mean(hidden * hidden, axis=1, keepdims=True) + EPS)
    return (hidden * inverse, inverse)


def rms_back(upstream, scaled, inverse):
    return inverse * (upstream - scaled * jnp.mean(upstream * scaled, axis=1, keepdims=True))


def low_half(rows):
    lane = lax.broadcasted_iota(jnp.int32, (rows, LANES), 1)
    return lane % 64 < 32


def rope(field, cosine, sine, direction):
    partner = jnp.where(
        low_half(field.shape[0]),
        pltpu.roll(field, 96, 1),
        pltpu.roll(field, 32, 1),
    )
    if direction > 0:
        return field * cosine + partner * sine
    return field * cosine - partner * sine


def split_heads(block):
    lane = lax.broadcasted_iota(jnp.int32, block.shape, 1)
    zero = jnp.zeros_like(block)
    return jnp.concatenate(
        [jnp.where(lane < 64, block, zero), jnp.where(lane >= 64, block, zero)], axis=0
    )


def join_heads(turned):
    count = turned.shape[1] // 2
    row = lax.broadcasted_iota(jnp.int32, (LANES, count), 0)
    return jnp.where(row < 64, turned[:, :count], turned[:, count:]).T


def meet(partners):
    barrier = pltpu.get_barrier_semaphore()
    total = 0
    for condition, device in partners:

        @pl.when(condition)
        def _(device=device):
            pl.semaphore_signal(barrier, inc=1, device_id=device, device_id_type=MESH)

        total = total + condition.astype(jnp.int32)
    pl.semaphore_wait(barrier, total)


def layers_kernel(
    late, tokens, cotangent, lengths,
    w_query, w_key, w_value, w_output, w_gate, w_up, w_down,
    gain_attn, gain_mlp, trig,
    block_out, grad_out, normed_out, att_out, n2_out, prod_out,
    g_out, db_out, dg_out, du_out, dq_out, dk_out, dv_out, own_out, halo_part_out, gains_out,
    wq, wk, wv, wo, wg, wu, wd,
    xs, qs, ks, vs, probs, slope, silu, mixed, normed, att, n2, prod, outs, gs,
    halo_in, halo_out, branch, d_att, d_norm, d_own, cosine, sine, first_key, bias, scale,
    wide_f, left_b, right_b, key_f, value_f,
    weight_sem, trig_sem, late_sem, token_sem, cot_sem, save_sem, out_sem,
    halo_send, halo_recv, hand_send, hand_recv, back_send, back_recv, turn_send, turn_recv,
):
    section, wide = lax.axis_index("section"), lax.axis_index("wide")
    last_section, last_wide = lax.axis_size("section") - 1, lax.axis_size("wide") - 1
    batches, rows, width = tokens.shape
    hidden_width = wg.shape[1]
    half = rows // 2
    band = rows + half
    pairs = width // LANES
    own, halo = pl.ds(rows, rows), pl.ds(0, rows)
    has_left, has_right = wide > 0, wide < last_wide
    has_before, has_after = section > 0, section < last_section
    is_first, is_last = jnp.logical_not(has_before), jnp.logical_not(has_after)

    weights = ((w_query, wq), (w_key, wk), (w_value, wv), (w_output, wo),
               (w_gate, wg), (w_up, wu), (w_down, wd))

    def weight_copy(index):
        source, target = weights[index]
        return pltpu.make_async_copy(source.at[0], target, weight_sem.at[index])

    def token_copy(mb):
        return pltpu.make_async_copy(tokens.at[mb], xs.at[mb, own], token_sem.at[mb])

    def cot_copy(mb):
        return pltpu.make_async_copy(cotangent.at[mb], gs.at[mb], cot_sem.at[mb])

    pieces = range(rows // PIECE)

    def rows_of(piece, base=0):
        return pl.ds(base + piece * PIECE, PIECE)

    def halo_copy(mb, piece, source):
        return pltpu.make_async_remote_copy(
            source, xs.at[mb, rows_of(piece)], halo_send.at[mb, piece], halo_recv.at[mb, piece],
            device_id={"wide": wide + 1}, device_id_type=MESH)

    def own_halo_copy(mb, piece):
        return halo_copy(mb, piece, xs.at[mb, rows_of(piece, rows)])

    def token_halo_copy(mb, piece):
        return halo_copy(mb, piece, tokens.at[mb, rows_of(piece)])

    def hand_copy(mb, piece):
        return pltpu.make_async_remote_copy(
            outs.at[mb, rows_of(piece)], xs.at[mb, rows_of(piece, rows)],
            hand_send.at[mb, piece], hand_recv.at[mb, piece],
            device_id={"section": section + 1}, device_id_type=MESH)

    def back_copy(mb, piece):
        return pltpu.make_async_remote_copy(
            halo_out.at[rows_of(piece)], halo_in.at[mb, rows_of(piece)],
            back_send.at[mb, piece], back_recv.at[mb, piece],
            device_id={"wide": wide - 1}, device_id_type=MESH)

    def turn_copy(mb, piece):
        return pltpu.make_async_remote_copy(
            outs.at[mb, rows_of(piece)], gs.at[mb, rows_of(piece)],
            turn_send.at[mb, piece], turn_recv.at[mb, piece],
            device_id={"section": section - 1}, device_id_type=MESH)

    def relay(mb):
        for piece in pieces:
            hand_copy(mb, piece).wait_recv()

            @pl.when(has_right)
            def _(piece=piece):
                own_halo_copy(mb, piece).start()

    def out_copy(mb, target):
        return pltpu.make_async_copy(outs.at[mb], target.at[mb], out_sem.at[mb])

    def save(name, mb):
        source, target, index = {
            "normed": (normed, normed_out, 0), "att": (att, att_out, 1), "n2": (n2, n2_out, 2),
            "prod": (prod, prod_out, 3), "branch": (branch.at[lax.rem(mb, 2)], db_out, 4),
            "g": (gs.at[mb], g_out, 5), "dg": (slope.at[mb], dg_out, 6), "du": (silu.at[mb], du_out, 7),
            "dq": (qs.at[mb], dq_out, 8), "dk": (ks.at[mb], dk_out, 9), "dv": (vs.at[mb], dv_out, 10),
        }[name]
        return pltpu.make_async_copy(source, target.at[mb], save_sem.at[index, mb])

    def saved_before(name, mb):
        @pl.when(mb > 0)
        def _():
            save(name, mb - 1).wait()

    @pl.when(is_first)
    def _():
        token_copy(0).start()

    trig_copy = pltpu.make_async_copy(trig, left_b, trig_sem.at[0])
    trig_copy.start()
    for index in range(3):
        weight_copy(index).start()

    meet([
        (has_left, {"wide": wide - 1}), (has_right, {"wide": wide + 1}),
        (has_before, {"section": section - 1}), (has_after, {"section": section + 1}),
    ])

    @pl.when(is_first & has_right)
    def _():
        for piece in pieces:
            token_halo_copy(0, piece).start()

    @pl.when(is_first)
    def _():
        for mb in range(1, batches):
            token_copy(mb).start()

    @pl.when(is_last)
    def _():
        for mb in range(batches):
            cot_copy(mb).start()

    @pl.when(jnp.logical_not(has_left))
    def _():
        xs[:, halo, :] = jnp.zeros((batches, rows, width), BF16)

    @pl.when(jnp.logical_not(has_right))
    def _():
        halo_in[...] = jnp.zeros(halo_in.shape, BF16)

    gains_out[...] = jnp.zeros(gains_out.shape, F32)

    start_row = wide * rows

    def tables(mb, carry):
        positions = lax.broadcasted_iota(jnp.int32, (2 * rows, LANES), 0) + (start_row - rows)
        query_at = lax.broadcasted_iota(jnp.int32, (8, rows), 1) + start_row

        def later(image, state):
            start, first, first_row = state
            first = jnp.where(positions >= start, start, first)
            first_row = jnp.where(query_at >= start, start, first_row)
            return (start + lengths[mb, image], first, first_row)

        _, first, first_row = lax.fori_loop(
            0, lengths.shape[1], later,
            (jnp.int32(0), jnp.zeros((2 * rows, LANES), jnp.int32), jnp.zeros((8, rows), jnp.int32)))
        offsets = positions - first
        lane = lax.broadcasted_iota(jnp.int32, (2 * rows, LANES), 1)
        one_hot = jnp.concatenate(
            [jnp.where(offsets == lane + base, 1.0, 0.0).astype(BF16) for base in range(0, band, LANES)],
            axis=1)
        for which, table in enumerate((cosine, sine)):
            parts = dot(one_hot, left_b[which])
            table[mb] = parts[:, :LANES] + parts[:, LANES:]
        first_key[mb] = first_row - start_row
        return carry

    trig_copy.wait()
    lax.fori_loop(0, batches, tables, 0)

    items = [(pair, block) for pair in range(pairs) for block in range(2)]

    def place(index):
        pair, block = items[index]
        lanes = slice(pair * LANES, (pair + 1) * LANES)
        low = block * half
        return lanes, slice(low, low + half), slice(low, low + band)

    def pipelined(first, second, third):
        first(0)
        for index in range(len(items)):
            if index + 1 < len(items):
                first(index + 1)
            second(index)
            if index:
                third(index - 1)
        third(len(items) - 1)


    def normalise(mb, part):
        for low in range(part.start, part.start + rows, BLOCK):
            at = slice(low, low + BLOCK)
            scaled, _ = rms_parts(xs[mb, at, :].astype(F32))
            normed[at, :] = (scaled * gain_attn[...]).astype(BF16)

    def keys_values(mb, part):
        cos_rows, sin_rows = cosine[mb, part, :], sine[mb, part, :]
        for start in range(0, width, 256):
            rows_n = normed[part, :]
            keys = dot(rows_n, wk[:, start:start + 256])
            for inner in range(0, 256, LANES):
                ks[mb, part, start + inner:start + inner + LANES] = rope(
                    keys[:, inner:inner + LANES], cos_rows, sin_rows, 1).astype(BF16)
            vs[mb, part, start:start + 256] = dot(rows_n, wv[:, start:start + 256]).astype(BF16)

    def attention(mb):
        def scores(index):
            lanes, here, near = place(index)
            wide_f[index % 2] = dot_nt(ks[mb, near, lanes], split_heads(qs[mb, here, lanes]))

        def soften(index):
            pair, block = items[index]
            for head in range(2):
                at = slice(head * LANES, (head + 1) * LANES)
                masked = wide_f[index % 2, :, at] + bias[block]
                raw = jnp.exp(masked - jnp.max(masked, axis=0, keepdims=True))
                probs[mb, pair, block, :, at] = raw.astype(BF16)

        def collect(index):
            pair, block = items[index]
            lanes, here, near = place(index)
            left = jnp.concatenate([vs[mb, near, lanes].T, jnp.ones((16, band), BF16)], axis=0)
            turned = dot(left, probs[mb, pair, block])
            inverse = 1.0 / turned[LANES:LANES + 1]
            scale[mb, index] = inverse
            att[here, lanes] = join_heads(turned[:LANES] * inverse).astype(BF16)

        pipelined(scores, soften, collect)

    def forward(mb, carry):
        @pl.when(is_first)
        def _():
            token_copy(mb).wait()

            @pl.when(has_right & (mb + 1 < batches))
            def _():
                for piece in pieces:
                    token_halo_copy(mb + 1, piece).start()

        @pl.when(has_before & (mb == 0))
        def _():
            relay(mb)

        saved_before("normed", mb)
        normalise(mb, own)

        @pl.when(mb == 0)
        def _():
            for index in range(3):
                weight_copy(index).wait()
            for index in range(3, 7):
                weight_copy(index).start()

        cos_rows, sin_rows = cosine[mb, own, :], sine[mb, own, :]
        for start in range(0, width, 256):
            queries = dot(normed[own, :], wq[:, start:start + 256])
            for inner in range(0, 256, LANES):
                turned = rope(queries[:, inner:inner + LANES], cos_rows, sin_rows, 1)
                qs[mb, :, start + inner:start + inner + LANES] = (turned * 0.125).astype(BF16)
        keys_values(mb, own)
        for block in range(2):
            key_at = lax.broadcasted_iota(jnp.int32, (band, half), 0) + (block * half - rows)
            query_at = lax.broadcasted_iota(jnp.int32, (band, half), 1) + block * half
            first = first_key[mb, 0:1, block * half:(block + 1) * half]
            bias[block] = jnp.where((key_at >= first) & (key_at <= query_at), 0.0, -1e30)

        @pl.when(has_left)
        def _():
            for piece in pieces:
                own_halo_copy(mb, piece).wait_recv()

        normalise(mb, halo)
        keys_values(mb, halo)
        save("normed", mb).start()
        saved_before("att", mb)
        attention(mb)
        save("att", mb).start()

        @pl.when(mb == 0)
        def _():
            for index in range(3, 7):
                weight_copy(index).wait()

        saved_before("n2", mb)
        for start in range(0, width, 256):
            at = slice(start, start + 256)
            d_norm[:, at] = xs[mb, own, at].astype(F32) + dot(att[...], wo[:, at])
        for low in range(0, rows, BLOCK):
            at = slice(low, low + BLOCK)
            total = d_norm[at, :]
            scaled, _ = rms_parts(total)
            mixed[mb, at, :] = total.astype(BF16)
            n2[at, :] = (scaled * gain_mlp[...]).astype(BF16)
        save("n2", mb).start()

        @pl.when(has_before & (mb + 1 < batches))
        def _():
            relay(mb + 1)

        saved_before("prod", mb)
        for start in range(0, hidden_width, 256):
            at = slice(start, start + 256)
            gate = dot(n2[...], wg[:, at])
            up = dot(n2[...], wu[:, at])
            sigma = jax.nn.sigmoid(gate)
            gated = gate * sigma
            prod[:, at] = (gated * up).astype(BF16)
            silu[mb, :, at] = gated.astype(BF16)
            slope[mb, :, at] = (up * (sigma * (1.0 + gate * (1.0 - sigma)))).astype(BF16)
        save("prod", mb).start()
        for start in range(0, width, 256):
            at = slice(start, start + 256)
            outs[mb, :, at] = (d_norm[:, at] + dot(prod[...], wd[:, at])).astype(BF16)

        @pl.when(has_after)
        def _():
            for piece in pieces:
                hand_copy(mb, piece).start()

        out_copy(mb, block_out).start()
        return carry

    lax.fori_loop(0, batches, forward, 0)

    for name in ("normed", "att", "n2", "prod"):
        save(name, batches - 1).wait()
    for mb in range(batches):
        out_copy(mb, block_out).wait()

    @pl.when(has_after)
    def _():
        for mb in range(batches):
            for piece in pieces:
                hand_copy(mb, piece).wait_send()


    def add_gain(which, product):
        folded = jnp.sum(product.reshape(product.shape[0] // 8, 8, width), axis=0)
        at = pl.ds(8 * which, 8)
        gains_out[at, :] = gains_out[at, :] + folded

    def attention_back(mb):
        def d_weights(index):
            lanes, here, near = place(index)
            wide_f[index % 2] = dot_nt(vs[mb, near, lanes], split_heads(d_att[here, lanes]))

        def d_soften(index):
            pair, block = items[index]
            for head in range(2):
                at = slice(head * LANES, (head + 1) * LANES)
                weight = probs[mb, pair, block, :, at].astype(F32) * scale[mb, index, :, at]
                moved = weight * wide_f[index % 2, :, at]
                centre = jnp.sum(moved, axis=0, keepdims=True)
                left_b[index % 2, :, at] = (moved - weight * centre).astype(BF16)
                right_b[index % 2, :, at] = weight.astype(BF16)

        def collect(index):
            pair, block = items[index]
            lanes, here, near = place(index)
            d_scores = left_b[index % 2]
            d_keys = dot(d_scores, split_heads(qs[mb, here, lanes]))
            d_values = dot(right_b[index % 2], split_heads(d_att[here, lanes]))
            turned = lax.dot_general(
                ks[mb, near, lanes], d_scores, (((0,), (0,)), ((), ())), preferred_element_type=F32)
            at = pl.ds(rows + block * half, half)
            qs[mb, here, lanes] = rope(
                join_heads(turned) * 0.125, cosine[mb, at, :], sine[mb, at, :], -1).astype(BF16)
            slot = pair % 2
            if block == 0:
                key_f[slot], value_f[slot] = d_keys, d_values
                return
            earlier_k, earlier_v = key_f[slot], value_f[slot]
            pieces = (
                (0, half, earlier_k[:half], earlier_v[:half]),
                (half, band, earlier_k[half:] + d_keys[:rows], earlier_v[half:] + d_values[:rows]),
                (band, 2 * rows, d_keys[rows:], d_values[rows:]),
            )
            for low, high, piece_k, piece_v in pieces:
                ks[mb, low:high, lanes] = rope(
                    piece_k, cosine[mb, low:high, :], sine[mb, low:high, :], -1).astype(BF16)
                vs[mb, low:high, lanes] = piece_v.astype(BF16)

        pipelined(d_weights, d_soften, collect)

    def closes(mb):
        return has_before | (mb < batches - 1) if late else wide >= 0

    def finish(mb):
        for piece in pieces:
            @pl.when(has_right)
            def _(piece=piece):
                back_copy(mb, piece).wait_recv()

            for low in range(piece * PIECE, (piece + 1) * PIECE, BLOCK):
                at = pl.ds(low, BLOCK)
                scaled, inverse = rms_parts(xs[mb, pl.ds(rows + low, BLOCK), :].astype(F32))
                d_normed = d_own[at, :] + halo_in[mb, at, :].astype(F32)
                add_gain(0, d_normed * scaled)
                back = rms_back(d_normed * gain_attn[...], scaled, inverse)
                outs[mb, at, :] = (branch[lax.rem(mb, 2), at, :].astype(F32) + back).astype(BF16)

            @pl.when(has_before)
            def _(piece=piece):
                turn_copy(mb, piece).start()

        out_copy(mb, grad_out).start()

    def backward(mb, carry):
        @pl.when(is_last)
        def _():
            cot_copy(mb).wait()

        @pl.when(has_after)
        def _():
            for piece in pieces:
                turn_copy(mb, piece).wait_recv()

        save("g", mb).start()
        for start in range(0, hidden_width, 256):
            at = slice(start, start + 256)
            d_product = dot_nt(gs[mb], wd[at, :])
            slope[mb, :, at] = (d_product * slope[mb, :, at].astype(F32)).astype(BF16)
            silu[mb, :, at] = (d_product * silu[mb, :, at].astype(F32)).astype(BF16)
        save("dg", mb).start()
        save("du", mb).start()
        for start in range(0, width, 256):
            at = slice(start, start + 256)
            d_norm[:, at] = dot_nt(slope[mb], wg[at, :]) + dot_nt(silu[mb], wu[at, :])
        slot = lax.rem(mb, 2)

        @pl.when(mb >= 2)
        def _():
            save("branch", mb - 2).wait()

        for low in range(0, rows, BLOCK):
            at = slice(low, low + BLOCK)
            scaled, inverse = rms_parts(mixed[mb, at, :].astype(F32))
            d_normed = d_norm[at, :]
            add_gain(1, d_normed * scaled)
            total = gs[mb, at, :].astype(F32) + rms_back(d_normed * gain_mlp[...], scaled, inverse)
            branch[slot, at, :] = total.astype(BF16)
        save("branch", mb).start()
        for start in range(0, width, 256):
            at = slice(start, start + 256)
            d_att[:, at] = dot_nt(branch[slot], wo[at, :]).astype(BF16)

        @pl.when(mb > 0)
        def _():
            finish(mb - 1)

        attention_back(mb)
        save("dq", mb).start()
        save("dk", mb).start()
        save("dv", mb).start()

        @pl.when(has_left & (mb > 0))
        def _():
            for piece in pieces:
                back_copy(mb - 1, piece).wait_send()

        for start in range(0, width, 256):
            at = slice(start, start + 256)
            halo_out[:, at] = (
                dot_nt(ks[mb, halo, :], wk[at, :]) + dot_nt(vs[mb, halo, :], wv[at, :])).astype(BF16)

        @pl.when(has_left & closes(mb))
        def _():
            for piece in pieces:
                back_copy(mb, piece).start()

        for start in range(0, width, 256):
            at = slice(start, start + 256)
            d_own[:, at] = (
                dot_nt(qs[mb], wq[at, :]) + dot_nt(ks[mb, own, :], wk[at, :])
                + dot_nt(vs[mb, own, :], wv[at, :]))
        return carry

    lax.fori_loop(0, batches, backward, 0)
    closed = closes(batches - 1)

    @pl.when(closed)
    def _():
        finish(batches - 1)

    @pl.when(jnp.logical_not(closed))
    def _():
        copies = [pltpu.make_async_copy(d_own, own_out, late_sem.at[0]),
                  pltpu.make_async_copy(halo_out, halo_part_out, late_sem.at[1])]
        for copy in copies:
            copy.start()
        for copy in copies:
            copy.wait()

    for mb in range(batches - 2, batches):
        save("branch", mb).wait()
    for mb in range(batches):
        for name in ("g", "dg", "du", "dq", "dk", "dv"):
            save(name, mb).wait()
    for mb in range(batches - 1):
        out_copy(mb, grad_out).wait()

    @pl.when(closed)
    def _():
        out_copy(batches - 1, grad_out).wait()

    @pl.when(has_left & closed)
    def _():
        for piece in pieces:
            back_copy(batches - 1, piece).wait_send()

    @pl.when(has_before)
    def _():
        for mb in range(batches):
            for piece in pieces:
                turn_copy(mb, piece).wait_send()

    @pl.when(has_right)
    def _():
        for mb in range(batches):
            for piece in pieces:
                own_halo_copy(mb, piece).wait_send()


def any_spec():
    return pl.BlockSpec(memory_space=pl.ANY)


def vmem_spec():
    return pl.BlockSpec(memory_space=pltpu.VMEM)


def trig_table(head_dim, reach):
    half_dim = head_dim // 2
    freqs = np.float32(THETA) ** (-np.arange(half_dim, dtype=np.float32) * np.float32(2.0) / np.float32(head_dim))
    angles = np.arange(reach, dtype=np.float32)[:, None] * np.tile(freqs, LANES // half_dim)[None, :]
    sign = np.tile(np.repeat(np.array([-1.0, 1.0], np.float32), half_dim), LANES // head_dim)
    parts = []
    for table in (np.cos(angles), np.sin(angles) * sign):
        high = table.astype(ml_dtypes.bfloat16)
        low = (table - high.astype(np.float32)).astype(ml_dtypes.bfloat16)
        parts.append(np.concatenate([high, low], axis=1))
    return jnp.asarray(np.stack(parts))


def run_layers(tokens, cotangent, lengths, weights, gain_attn, gain_mlp, late=False):
    batches, rows, width = tokens.shape
    hidden_width = weights[4].shape[2]
    pairs = width // LANES
    band = rows + rows // 2
    one = (batches, rows, width)
    two = (batches, 2 * rows, width)
    wide = (batches, rows, hidden_width)
    outs = [(one, BF16), (one, BF16), (two, BF16), (one, BF16), (one, BF16), (wide, BF16),
            (one, BF16), (one, BF16), (wide, BF16), (wide, BF16), (one, BF16), (two, BF16), (two, BF16),
            (one[1:], F32), (one[1:], BF16), ((16, width), F32)]
    dma = pltpu.SemaphoreType.DMA
    scratch = [pltpu.VMEM(w.shape[1:], BF16) for w in weights] + [
        pltpu.VMEM(two, BF16),
        pltpu.VMEM(one, BF16),
        pltpu.VMEM(two, BF16),
        pltpu.VMEM(two, BF16),
        pltpu.VMEM((batches, pairs, 2, band, rows), BF16),
        pltpu.VMEM(wide, BF16),
        pltpu.VMEM(wide, BF16),
        pltpu.VMEM(one, BF16),
        pltpu.VMEM(two[1:], BF16),
        pltpu.VMEM(one[1:], BF16),
        pltpu.VMEM(one[1:], BF16),
        pltpu.VMEM(wide[1:], BF16),
        pltpu.VMEM(one, BF16),
        pltpu.VMEM(one, BF16),
        pltpu.VMEM(one, BF16),
        pltpu.VMEM(one[1:], BF16),
        pltpu.VMEM((2,) + one[1:], BF16),
        pltpu.VMEM(one[1:], BF16),
        pltpu.VMEM(one[1:], F32),
        pltpu.VMEM(one[1:], F32),
        pltpu.VMEM((batches, 2 * rows, LANES), F32),
        pltpu.VMEM((batches, 2 * rows, LANES), F32),
        pltpu.VMEM((batches, 8, rows), jnp.int32),
        pltpu.VMEM((2, band, rows // 2), F32),
        pltpu.VMEM((batches, 2 * pairs, 1, rows), F32),
        pltpu.VMEM((2, band, rows), F32),
        pltpu.VMEM((2, band, rows), BF16),
        pltpu.VMEM((2, band, rows), BF16),
        pltpu.VMEM((2, band, LANES), F32),
        pltpu.VMEM((2, band, LANES), F32),
        dma((7,)), dma((1,)), dma((2,)), dma((batches,)), dma((batches,)), dma((11, batches)),
    ] + [dma((batches,))] + [dma((batches, rows // PIECE))] * 8
    trig = trig_table(width // HEADS, band)
    return pl.pallas_call(
        functools.partial(layers_kernel, late),
        out_shape=[jax.ShapeDtypeStruct(shape, dtype) for shape, dtype in outs],
        in_specs=[any_spec()] * 2 + [pl.BlockSpec(memory_space=pltpu.SMEM)] + [any_spec()] * 7 + [vmem_spec()] * 2 + [any_spec()],
        out_specs=[any_spec()] * 15 + [vmem_spec()],
        scratch_shapes=scratch,
        compiler_params=pltpu.CompilerParams(
            collective_id=1, has_side_effects=True, vmem_limit_bytes=VMEM_BYTES),
        name="layers",
    )(tokens, cotangent, lengths, *weights, gain_attn, gain_mlp, trig)


LAG = 4
SENDS = 6
LAG_PAIR = 1
LENT = 3
MIX_LENDER = 5
MIX_PARTNER = 4
CROSS = 6
LATE = 8
CHUNK = 256


def dot_tn(left, right):
    return lax.dot_general(
        left, right, (((0,), (0,)), ((), ())), preferred_element_type=F32
    )


class Place:
    def __init__(self, count):
        wide = lax.axis_index("wide")
        self.outer = count // 4
        self.core, self.side, self.depth = lax.rem(wide, 2), lax.rem(wide // 2, 2), wide // 4
        self.core_mate = {"wide": wide + 1 - 2 * self.core}
        self.side_mate = {"wide": wide + 2 - 4 * self.side}
        self.low, self.high = lax.rem(self.depth, 2), self.depth // 2
        self.low_mate = {"wide": wide + 4 - 8 * self.low}
        self.high_mate = {"wide": wide + 8 - 16 * self.high}


class Pairs:
    def __init__(self, place, refs, sems):
        self.place = place
        self.dw, self.out, self.arrived = refs
        self.sent, self.received = sems

    def copy(self, j):
        slot = lax.rem(j, SENDS)
        return pltpu.make_async_remote_copy(
            self.out.at[slot], self.arrived.at[j], self.sent.at[slot], self.received.at[j],
            device_id=self.place.core_mate, device_id_type=MESH)

    def send(self, j):
        slot, held = lax.rem(j, SENDS), lax.rem(j, LAG_PAIR + 1)

        @pl.when(j >= SENDS)
        def _():
            self.copy(j - SENDS).wait_send()

        for index in range(2 * self.place.outer):
            self.out[slot, index] = self.dw[held, 2 * index + 1 - self.place.core].astype(BF16)
        self.copy(j).start()

    def total(self, j, index):
        return self.dw[lax.rem(j, LAG_PAIR + 1), 2 * index + self.place.core] + self.arrived[j, index].astype(F32)

    def drain(self, count):
        for back in range(1, SENDS + 1):
            self.copy(count - back).wait_send()


class Halve:
    def __init__(self, mate, bit, refs, sems, first=0):
        self.mate, self.bit, self.first = mate, bit, first
        self.out, self.own, self.arrived = refs
        self.sent, self.received = sems

    def copy(self, j):
        slot = lax.rem(j, SENDS)
        return pltpu.make_async_remote_copy(
            self.out.at[slot], self.arrived.at[j], self.sent.at[slot], self.received.at[j],
            device_id=self.mate, device_id_type=MESH)

    def free(self, j):
        @pl.when(j >= SENDS + self.first)
        def _():
            self.copy(j - SENDS).wait_send()

    def split(self, j, part, place_of):
        slot, held = lax.rem(j, SENDS), lax.rem(j, LAG + 1)
        for k in range(self.out.shape[1]):
            self.out[slot, k] = part(place_of(k, 1 - self.bit)).astype(BF16)
            self.own[held, k] = part(place_of(k, self.bit)).astype(F32)

    def take_from(self, j, earlier, place_of):
        self.free(j)
        earlier.copy(j).wait_recv()
        self.split(j, lambda index: earlier.total(j, index), place_of)
        self.copy(j).start()

    def total(self, j, index):
        return self.own[lax.rem(j, LAG + 1), index] + self.arrived[j, index].astype(F32)

    def close(self, j):
        self.copy(j).wait_recv()
        return self.total(j, 0)

    def drain(self, count):
        for back in range(1, SENDS + 1):
            j = count - back

            @pl.when(j >= self.first)
            def _(j=j):
                self.copy(j).wait_send()


def lowest(k, bit):
    return 2 * k + bit


class Lent:
    def __init__(self, refs, sems, section, chunks):
        self.x_out, self.x_in, self.r_out, self.r_in = refs
        self.x_send, self.x_recv, self.r_send, self.r_recv = sems
        self.lender = section == 0
        self.lent = self.x_in.shape[0]
        self.partner = {"section": 1 - section}
        self.first = jnp.where(self.lender, self.lent, 0)
        self.computed = chunks
        self.count = jnp.where(self.lender, chunks, chunks + self.lent)

    def x_copy(self, j):
        return pltpu.make_async_remote_copy(
            self.x_out.at[j], self.x_in.at[j], self.x_send.at[j], self.x_recv.at[j],
            device_id=self.partner, device_id_type=MESH)

    def r_copy(self, j):
        return pltpu.make_async_remote_copy(
            self.r_out.at[j], self.r_in.at[j], self.r_send.at[j], self.r_recv.at[j],
            device_id=self.partner, device_id_type=MESH)

    def give(self, j, pairs):
        pairs.copy(j).wait_recv()
        for index in range(self.x_out.shape[1]):
            self.x_out[j, index] = pairs.total(j, index).astype(BF16)
        self.x_copy(j).start()

    def give_back(self, j):
        @pl.when(j == self.computed)
        def _():
            pl.semaphore_wait(pltpu.get_barrier_semaphore(), 1)

        self.r_copy(j - self.computed).start()

    def drain(self, result):
        @pl.when(self.lender)
        def _():
            for j in range(self.lent):
                self.x_copy(j).wait_send()
                self.r_copy(j).wait_recv()
                result[j] = self.r_in[j]

        @pl.when(jnp.logical_not(self.lender))
        def _():
            for j in range(self.lent):
                self.r_copy(j).wait_send()


def weight_kernel(
    normed_in, att_in, n2_in, prod_in, g_in, db_in, dg_in, du_in, dq_in, dk_in, dv_in,
    own_in, halo_part_in, tokens, gains, gain_attn,
    out_m, out_d, late_grad,
    normed, att, n2, prod, g, dy, late_own, late_part, late_halo, late_x, late_branch, late_gain, late_sem, *rest,
):
    rest = list(rest)

    def take(number):
        taken, rest[:number] = rest[:number], []
        return taken

    section, wide, count = lax.axis_index("section"), lax.axis_index("wide"), lax.axis_size("wide")
    batches, rows, width = g_in.shape
    hidden_width = prod_in.shape[2]
    own = pl.ds(rows, rows)
    m_count, d_count = out_m.shape[0], out_d.shape[0]
    per_wide, per_narrow = hidden_width // CHUNK, width // CHUNK
    place = Place(count)
    lent = Lent(take(4), take(4), section, d_count)
    pairs_m, pairs_d = Pairs(place, take(3), take(2)), Pairs(place, take(3), take(2))
    mates = ((place.side_mate, place.side), (place.low_mate, place.low), (place.high_mate, place.high))
    side_m, low_m, high_m = [Halve(*mate, take(3), take(2)) for mate in mates]
    side_d, low_d, high_d = [Halve(*mate, take(3), take(2), lent.first) for mate in mates]
    low_z, high_z, side_z = [Halve(*mates[index], take(3), take(2)) for index in (1, 2, 0)]
    x_sem, dy_sem = take(2)
    z_count = m_count // CROSS
    y_count = m_count - z_count
    has_left, has_right = wide > 0, wide < count - 1

    late_loads = [
        pltpu.make_async_copy(source, target, late_sem.at[index])
        for index, (source, target) in enumerate((
            (halo_part_in, late_part), (own_in, late_own), (tokens.at[batches - 1], late_x),
            (db_in.at[batches - 1], late_branch)))]
    late_copy = pltpu.make_async_remote_copy(
        late_part, late_halo, late_sem.at[4], late_sem.at[5], device_id={"wide": wide - 1}, device_id_type=MESH)

    def finish_late():
        for copy in late_loads[1:]:
            copy.wait()
        pl.when(has_right)(lambda: late_copy.wait_recv())
        for low in range(0, rows, BLOCK):
            at = pl.ds(low, BLOCK)
            scaled, inverse = rms_parts(late_x[at, :].astype(F32))
            d_normed = late_own[at, :] + late_halo[at, :].astype(F32)
            product = (d_normed * scaled).reshape(BLOCK // 8, 8, width)
            late_gain[...] = late_gain[...] + jnp.sum(product, axis=0)
            back = rms_back(d_normed * gain_attn[...], scaled, inverse)
            late_grad[at, :] = (late_branch[at, :].astype(F32) + back).astype(BF16)


    loads = ((n2_in, n2), (att_in, att), (normed_in, normed), (prod_in, prod), (g_in, g))

    def x_copy(index):
        source, target = loads[index]
        return pltpu.make_async_copy(source, target, x_sem.at[index])

    kinds = ((dg_in, per_wide), (du_in, per_wide), (db_in, per_narrow), (dq_in, per_narrow), (dk_in, per_narrow), (dv_in, per_narrow))

    def each_load(j, act):
        slot = lax.rem(j, 2)
        base = 0
        for index, (source, parts) in enumerate(kinds):
            @pl.when((j >= base) & (j < base + parts))
            def _(source=source, base=base, index=index):
                lanes = pl.ds(pl.multiple_of((j - base) * CHUNK, CHUNK), CHUNK)
                target = dy.at[slot] if index >= 4 else dy.at[slot, :, own]
                act(pltpu.make_async_copy(source.at[:, :, lanes], target, dy_sem.at[slot]))
            base += parts
        return base

    x_copy(0).start()
    each_load(jnp.int32(0), lambda copy: copy.start())

    @pl.when(lent.lender)
    def _():
        for copy in late_loads:
            copy.start()

    for index in (3, 4, 1, 2):
        x_copy(index).start()
    late_gain[...] = jnp.zeros(late_gain.shape, F32)

    @pl.when(jnp.logical_not(has_right))
    def _():
        late_halo[...] = jnp.zeros(late_halo.shape, BF16)

    barrier = pltpu.get_barrier_semaphore()
    peers = [place.core_mate, place.side_mate, place.low_mate, place.high_mate]
    for peer in peers:
        pl.semaphore_signal(barrier, inc=1, device_id=peer, device_id_type=MESH)
    for condition, step in ((has_left, -1), (has_right, 1)):
        @pl.when(condition)
        def _(step=step):
            pl.semaphore_signal(barrier, inc=1, device_id={"wide": wide + step}, device_id_type=MESH)
    greeted = len(peers) + has_left.astype(jnp.int32) + has_right.astype(jnp.int32)
    pl.semaphore_wait(barrier, greeted + lent.lender.astype(jnp.int32))
    pl.semaphore_signal(barrier, inc=1, device_id=lent.partner, device_id_type=MESH)

    @pl.when(lent.lender)
    def _():
        late_loads[0].wait()
        pl.when(has_left)(lambda: late_copy.start())


    kv_first = 2 * per_wide + 2 * per_narrow
    kv_last = kv_first + 2 * per_narrow
    narrow_first = 2 * per_wide

    def compute_m(j):
        slot, held = lax.rem(j, 2), lax.rem(j, LAG_PAIR + 1)

        @pl.when(j + 1 < kv_last)
        def _():
            each_load(j + 1, lambda copy: copy.start())

        def write(left, right):
            product = dot_tn(left.reshape(-1, width), right.reshape(-1, CHUNK))
            pairs_m.dw[held] = product.reshape(pairs_m.dw.shape[1:])

        @pl.when(j < kv_last)
        def _():
            each_load(j, lambda copy: copy.wait())

        for index, first in enumerate((0, narrow_first, narrow_first + per_narrow)):
            @pl.when(j == first)
            def _(index=index):
                x_copy(index).wait()

        @pl.when(j < narrow_first)
        def _():
            write(n2[...], dy[slot, :, own, :])

        @pl.when((j >= narrow_first) & (j < narrow_first + per_narrow))
        def _():
            write(att[...], dy[slot, :, own, :])

        @pl.when((j >= narrow_first + per_narrow) & (j < kv_first))
        def _():
            write(normed[:, own, :], dy[slot, :, own, :])

        @pl.when((j >= kv_first) & (j < kv_last))
        def _():
            write(normed[...], dy[slot])

        @pl.when(j == kv_last)
        def _():
            first = jnp.sum(gains[0:8, :] + late_gain[...], axis=0, keepdims=True)
            second = jnp.sum(gains[8:16, :], axis=0, keepdims=True)
            row = lax.broadcasted_iota(jnp.int32, (LANES, width), 0)
            placed = jnp.where(row == 0, first, jnp.where(row == 1, second, 0.0))
            columns = placed.T
            pairs_m.dw[held] = jnp.concatenate([columns, columns], axis=1).reshape(pairs_m.dw.shape[1:])

    def compute_d(j):
        held = lax.rem(j, LAG_PAIR + 1)

        @pl.when(j == 0)
        def _():
            x_copy(3).wait()
            x_copy(4).wait()

        lanes = pl.ds(pl.multiple_of(j * LANES, LANES), LANES)
        product = dot_tn(prod[...].reshape(-1, hidden_width), g[:, :, lanes].reshape(-1, LANES))
        pairs_d.dw[held] = product.reshape(pairs_d.dw.shape[1:])

    def on_chunk(s, act_m, act_d):
        period = jnp.where(lent.lender, MIX_LENDER, MIX_PARTNER)
        turn = jnp.where(lent.lender, s // MIX_LENDER, s // MIX_PARTNER)
        spot = s - period * turn
        mixed = turn < lent.count
        j_m = jnp.where(mixed, (period - 1) * turn + spot, s - lent.count)
        j_d = turn
        is_d = (s >= 0) & mixed & (spot == period - 1)
        is_m = (s >= 0) & (j_m < m_count) & jnp.logical_not(is_d)

        @pl.when(is_m)
        def _():
            act_m(j_m)

        @pl.when(is_d)
        def _():
            act_d(j_d)

    def either(act_y, act_z):
        def act(j):
            crossing = lax.rem(j, CROSS) == CROSS - 1
            pl.when(jnp.logical_not(crossing))(lambda: act_y(j, j - j // CROSS))
            pl.when(crossing)(lambda: act_z(j, j // CROSS))
        return act

    def nothing(*_):
        pass

    def below(limit, act):
        return lambda j: pl.when(j < limit)(lambda: act(j))

    def reduced(act):
        return lambda j: pl.when(j >= lent.first)(lambda: act(j))

    def open_y(j, c):
        side_m.free(c)
        pairs_m.copy(j).wait_recv()
        side_m.split(c, lambda index: pairs_m.total(j, index), lowest)
        side_m.copy(c).start()

    def open_z(j, z):
        low_z.free(z)
        pairs_m.copy(j).wait_recv()
        low_z.split(z, lambda index: pairs_m.total(j, index), lambda k, bit: ((k // 2) * 2 + bit) * 2 + k % 2)
        low_z.copy(z).start()

    def open_d(j):
        pl.when(j < lent.first)(lambda: lent.give(j, pairs_d))

        @pl.when(j >= lent.first)
        def _():
            side_d.free(j)

            @pl.when(j < d_count)
            def _():
                pairs_d.copy(j).wait_recv()
                side_d.split(j, lambda index: pairs_d.total(j, index), lowest)

            @pl.when(j >= d_count)
            def _():
                lent.x_copy(j - d_count).wait_recv()
                side_d.split(j, lambda index: lent.x_in[j - d_count, index], lowest)

            side_d.copy(j).start()

    def close_y(j, c):
        out_m[j] = high_m.close(c)

    def close_z(j, z):
        out_m[j] = side_z.close(z)

    def close_d(j):
        total = high_d.close(j)

        @pl.when(j < d_count)
        def _():
            out_d[j] = total

        @pl.when(j >= d_count)
        def _():
            lent.r_out[j - d_count] = total
            lent.give_back(j)

    def step(s, carry):
        pl.when(lent.lender & (s == LATE))(finish_late)
        on_chunk(s, compute_m, below(d_count, compute_d))
        on_chunk(s, pairs_m.send, below(d_count, pairs_d.send))
        on_chunk(s - LAG_PAIR, either(open_y, open_z), open_d)
        on_chunk(
            s - LAG_PAIR - LAG,
            either(lambda j, c: low_m.take_from(c, side_m, lowest),
                   lambda j, z: high_z.take_from(z, low_z, lambda k, bit: 2 * bit + k)),
            reduced(lambda j: low_d.take_from(j, side_d, lowest)))
        on_chunk(
            s - LAG_PAIR - 2 * LAG,
            either(lambda j, c: high_m.take_from(c, low_m, lowest),
                   lambda j, z: side_z.take_from(z, high_z, lowest)),
            reduced(lambda j: high_d.take_from(j, low_d, lowest)))
        on_chunk(s - LAG_PAIR - 3 * LAG, either(close_y, close_z), reduced(close_d))
        return carry

    total = d_count + lent.lent
    steps = max(m_count + total, MIX_PARTNER * total, MIX_LENDER * d_count)
    lax.fori_loop(0, steps + LAG_PAIR + 3 * LAG, step, 0)
    pairs_m.drain(m_count)
    pairs_d.drain(d_count)
    for stage in (side_m, low_m, high_m):
        stage.drain(y_count)
    for stage in (side_d, low_d, high_d):
        stage.drain(lent.count)
    for stage in (low_z, high_z, side_z):
        stage.drain(z_count)
    lent.drain(out_d)
    pl.when(lent.lender & has_left)(lambda: late_copy.wait_send())


def run_weights(normed, att, n2, prod, g, db, dg, du, dq, dk, dv, own, part, tokens, gains, gain_attn, count):
    batches, rows, width = g.shape
    hidden_width = prod.shape[2]
    m_count = 2 * (hidden_width // CHUNK) + 4 * (width // CHUNK) + 1
    d_count = width // LANES

    dma = pltpu.SemaphoreType.DMA
    block_m, block_d = (width // count, CHUNK), (hidden_width // count, LANES)
    z_count = m_count // CROSS
    y_count = m_count - z_count

    def pairs(chunks, block):
        return [
            pltpu.VMEM((LAG_PAIR + 1, count) + block, F32),
            pltpu.VMEM((SENDS, count // 2) + block, BF16),
            pltpu.VMEM((chunks, count // 2) + block, BF16),
            dma((SENDS,)), dma((chunks,)),
        ]

    def halves(chunks, block):
        refs = []
        for blocks in (count // 4, count // 8, count // 16):
            refs += [
                pltpu.VMEM((SENDS, blocks) + block, BF16),
                pltpu.VMEM((LAG + 1, blocks) + block, F32),
                pltpu.VMEM((chunks, blocks) + block, BF16),
                dma((SENDS,)), dma((chunks,)),
            ]
        return refs

    ladders = [
        pltpu.VMEM((LENT, count // 2) + block_d, BF16),
        pltpu.VMEM((LENT, count // 2) + block_d, BF16),
        pltpu.VMEM((LENT,) + block_d, F32),
        pltpu.VMEM((LENT,) + block_d, F32),
    ] + [dma((LENT,))] * 4
    ladders += pairs(m_count, block_m) + pairs(d_count, block_d)
    ladders += halves(y_count, block_m) + halves(d_count + LENT, block_d) + halves(z_count, block_m)
    return pl.pallas_call(
        weight_kernel,
        out_shape=[
            jax.ShapeDtypeStruct((m_count,) + block_m, F32),
            jax.ShapeDtypeStruct((d_count,) + block_d, F32),
            jax.ShapeDtypeStruct(part.shape, BF16),
        ],
        in_specs=[any_spec()] * 14 + [vmem_spec()] * 2,
        out_specs=[vmem_spec()] * 3,
        scratch_shapes=[
            pltpu.VMEM(normed.shape, BF16),
            pltpu.VMEM(att.shape, BF16),
            pltpu.VMEM(n2.shape, BF16),
            pltpu.VMEM(prod.shape, BF16),
            pltpu.VMEM(g.shape, BF16),
            pltpu.VMEM((2, batches, 2 * rows, CHUNK), BF16),
            pltpu.VMEM(own.shape, F32),
        ] + [pltpu.VMEM(part.shape, BF16)] * 4 + [
            pltpu.VMEM((8, width), F32),
            pltpu.SemaphoreType.DMA((6,)),
        ] + ladders + [
            pltpu.SemaphoreType.DMA((5,)),
            pltpu.SemaphoreType.DMA((2,)),
        ],
        compiler_params=pltpu.CompilerParams(
            collective_id=3, has_side_effects=True, vmem_limit_bytes=VMEM_BYTES),
        name="weights",
    )(normed, att, n2, prod, g, db, dg, du, dq, dk, dv, own, part, tokens, gains, gain_attn)


def summed_weights(normed, att, n2, prod, g, db, dg, du, dq, dk, dv, gains):
    def outer_sum(left, right):
        total = lax.dot_general(
            left, right, (((0, 1), (0, 1)), ((), ())), preferred_element_type=F32)
        return lax.psum_scatter(total[None], "wide", scatter_dimension=1, tiled=True)

    rows = g.shape[1]
    normed_own = normed[:, rows:]
    gain_rows = gains.reshape(2, 8, -1).sum(axis=1)
    gain_parts = [
        lax.psum_scatter(gain_rows[i:i + 1], "wide", scatter_dimension=1, tiled=True) for i in range(2)]
    return (
        outer_sum(normed_own, dq), outer_sum(normed, dk), outer_sum(normed, dv), outer_sum(att, db),
        outer_sum(n2, dg), outer_sum(n2, du), outer_sum(prod, g), *gain_parts,
    )


def arrange_kernel(sizes, block, grads, late, chunks_m, chunks_d, block_out, grad_out, *rest):
    outs, (held_block, held_grads, held_m, held_d), (load_sem, store_sem) = rest[:9], rest[9:13], rest[13:]
    batches = block.shape[0]
    loads, stores = [], []
    for mb in range(batches):
        loads += [(block.at[mb], held_block.at[mb]), (grads.at[mb], held_grads.at[mb])]
        stores += [(held_block.at[mb], block_out.at[0, mb]), (held_grads.at[mb], grad_out.at[0, mb])]
    first_load = len(loads)
    loads += [(chunks_m, held_m), (chunks_d, held_d)]
    base = 0
    for size, index in zip(sizes, (4, 5, 3, 0, 1, 2)):
        for part in range(size):
            stores.append((held_m.at[base + part], outs[index].at[0, :, pl.ds(part * CHUNK, CHUNK)]))
        base += size
    for part in range(chunks_d.shape[0]):
        stores.append((held_d.at[part], outs[6].at[0, :, pl.ds(part * LANES, LANES)]))
    loads = [pltpu.make_async_copy(*pair, load_sem.at[index]) for index, pair in enumerate(loads)]
    stores = [pltpu.make_async_copy(*pair, store_sem.at[index]) for index, pair in enumerate(stores)]
    is_late = lax.axis_index("section") == 0
    last = first_load - 1
    late_load = pltpu.make_async_copy(late, held_grads.at[batches - 1], load_sem.at[last])
    pl.when(is_late)(lambda: late_load.start())
    pl.when(jnp.logical_not(is_late))(lambda: loads[last].start())
    for index, copy in enumerate(loads):
        if index != last:
            copy.start()
    for index in range(first_load):
        loads[index].wait()
        stores[index].start()
    for copy in loads[first_load:]:
        copy.wait()
    for copy in stores[first_load:]:
        copy.start()
    turned = held_m[base, :, :LANES].T
    outs[7][...] = turned[0:1, :]
    outs[8][...] = turned[1:2, :]
    for copy in stores:
        copy.wait()


def arrange(block, grads, late, chunks_m, chunks_d, sizes):
    own, own_d = chunks_m.shape[1], chunks_d.shape[1]
    width, hidden_width = block.shape[2], CHUNK * sizes[0]
    shapes = [(1,) + block.shape] * 2
    narrow, broad = (1, own, width), (1, own, hidden_width)
    matrices = [narrow] * 4 + [broad] * 2 + [(1, own_d, width)]
    out_shape = [jax.ShapeDtypeStruct(shape, BF16) for shape in shapes]
    out_shape += [jax.ShapeDtypeStruct(shape, F32) for shape in matrices + [(1, own)] * 2]
    copies = sum(sizes) + chunks_d.shape[0] + 2 * block.shape[0]
    return pl.pallas_call(
        functools.partial(arrange_kernel, sizes),
        out_shape=out_shape,
        in_specs=[any_spec()] * 5,
        out_specs=[any_spec()] * 9 + [vmem_spec()] * 2,
        scratch_shapes=[pltpu.VMEM(held.shape, held.dtype) for held in (block, grads, chunks_m, chunks_d)]
        + [pltpu.SemaphoreType.DMA((2 * block.shape[0] + 2,)), pltpu.SemaphoreType.DMA((copies,))],
        compiler_params=pltpu.CompilerParams(vmem_limit_bytes=VMEM_BYTES),
        name="arrange",
    )(block, grads, late, chunks_m, chunks_d)


def per_device(
    tokens, cotangent, seg_lengths, w_query, w_key, w_value, w_output, w_gate, w_up, w_down, gain_attn, gain_mlp,
):
    weights = (w_query, w_key, w_value, w_output, w_gate, w_up, w_down)
    lengths = seg_lengths.reshape(seg_lengths.shape[0], -1)
    count = lax.axis_size("wide")
    width, hidden_width = w_gate.shape[1:]
    whole_tiles = count == 16 and width % (16 * count) == 0 and hidden_width % (16 * count) == 0
    block_out, input_grads, *saved, own, part, gains = run_layers(
        tokens, cotangent, lengths, weights, gain_attn, gain_mlp, late=whole_tiles)
    if not whole_tiles:
        return (block_out[None], input_grads[None], *summed_weights(*saved, gains))
    out_m, out_d, late = run_weights(*saved, own, part, tokens, gains, gain_attn, count)
    sizes = (hidden_width // CHUNK,) * 2 + (width // CHUNK,) * 4
    return tuple(arrange(block_out, input_grads, late, out_m, out_d, sizes))


def solution(mesh):
    in_specs = (
        P(None, "wide", None),
        P(None, "wide", None),
        P(),
        *[P("section", None, None)] * 7,
        *[P("section", None)] * 2,
    )
    out_specs = (
        *[P("section", None, "wide", None)] * 2,
        *[P("section", "wide", None)] * 7,
        *[P("section", "wide")] * 2,
    )
    return jax.shard_map(
        per_device, mesh=mesh, in_specs=in_specs, out_specs=out_specs, check_vma=False
    )
```

```python
import functools

import jax
import jax.numpy as jnp
import ml_dtypes
import numpy as np
from jax import lax
from jax.experimental import pallas as pl
from jax.experimental.pallas import tpu as pltpu
from jax.sharding import PartitionSpec as P

HEADS = 12
EPS = 1e-05
THETA = 10000.0

F32 = jnp.float32
BF16 = jnp.bfloat16
MESH = pl.DeviceIdType.MESH
LANES = 128
BLOCK = 64
PIECE = 256
VMEM_BYTES = 63 * 1024 * 1024


def dot(left, right):
    return jnp.dot(left, right, preferred_element_type=F32)


def dot_nt(left, right):
    return lax.dot_general(
        left, right, (((1,), (1,)), ((), ())), preferred_element_type=F32
    )


def rms_parts(hidden):
    inverse = lax.rsqrt(jnp.mean(hidden * hidden, axis=1, keepdims=True) + EPS)
    return (hidden * inverse, inverse)


def rms_back(upstream, scaled, inverse):
    return inverse * (upstream - scaled * jnp.mean(upstream * scaled, axis=1, keepdims=True))


def low_half(rows):
    lane = lax.broadcasted_iota(jnp.int32, (rows, LANES), 1)
    return lane % 64 < 32


def rope(field, cosine, sine, direction):
    partner = jnp.where(
        low_half(field.shape[0]),
        pltpu.roll(field, 96, 1),
        pltpu.roll(field, 32, 1),
    )
    if direction > 0:
        return field * cosine + partner * sine
    return field * cosine - partner * sine


def split_heads(block):
    lane = lax.broadcasted_iota(jnp.int32, block.shape, 1)
    zero = jnp.zeros_like(block)
    return jnp.concatenate(
        [jnp.where(lane < 64, block, zero), jnp.where(lane >= 64, block, zero)], axis=0
    )


def join_heads(turned):
    count = turned.shape[1] // 2
    row = lax.broadcasted_iota(jnp.int32, (LANES, count), 0)
    return jnp.where(row < 64, turned[:, :count], turned[:, count:]).T


def meet(partners):
    barrier = pltpu.get_barrier_semaphore()
    total = 0
    for condition, device in partners:

        @pl.when(condition)
        def _(device=device):
            pl.semaphore_signal(barrier, inc=1, device_id=device, device_id_type=MESH)

        total = total + condition.astype(jnp.int32)
    pl.semaphore_wait(barrier, total)


def layers_kernel(
    late, tokens, cotangent, lengths,
    w_query, w_key, w_value, w_output, w_gate, w_up, w_down,
    gain_attn, gain_mlp, trig,
    block_out, grad_out, normed_out, att_out, n2_out, prod_out,
    g_out, db_out, dg_out, du_out, dq_out, dk_out, dv_out, own_out, halo_part_out, gains_out,
    wq, wk, wv, wo, wg, wu, wd,
    xs, qs, ks, vs, probs, slope, silu, mixed, normed, att, n2, prod, outs, gs,
    halo_in, halo_out, branch, d_att, d_norm, d_own, cosine, sine, first_key, bias, scale,
    wide_f, left_b, right_b, key_f, value_f,
    weight_sem, trig_sem, late_sem, token_sem, cot_sem, save_sem, out_sem,
    halo_send, halo_recv, hand_send, hand_recv, back_send, back_recv, turn_send, turn_recv,
):
    section, wide = lax.axis_index("section"), lax.axis_index("wide")
    last_section, last_wide = lax.axis_size("section") - 1, lax.axis_size("wide") - 1
    batches, rows, width = tokens.shape
    hidden_width = wg.shape[1]
    half = rows // 2
    band = rows + half
    pairs = width // LANES
    own, halo = pl.ds(rows, rows), pl.ds(0, rows)
    has_left, has_right = wide > 0, wide < last_wide
    has_before, has_after = section > 0, section < last_section
    is_first, is_last = jnp.logical_not(has_before), jnp.logical_not(has_after)

    weights = ((w_query, wq), (w_key, wk), (w_value, wv), (w_output, wo),
               (w_gate, wg), (w_up, wu), (w_down, wd))

    def weight_copy(index):
        source, target = weights[index]
        return pltpu.make_async_copy(source.at[0], target, weight_sem.at[index])

    def token_copy(mb):
        return pltpu.make_async_copy(tokens.at[mb], xs.at[mb, own], token_sem.at[mb])

    def cot_copy(mb):
        return pltpu.make_async_copy(cotangent.at[mb], gs.at[mb], cot_sem.at[mb])

    pieces = range(rows // PIECE)

    def rows_of(piece, base=0):
        return pl.ds(base + piece * PIECE, PIECE)

    def halo_copy(mb, piece, source):
        return pltpu.make_async_remote_copy(
            source, xs.at[mb, rows_of(piece)], halo_send.at[mb, piece], halo_recv.at[mb, piece],
            device_id={"wide": wide + 1}, device_id_type=MESH)

    def own_halo_copy(mb, piece):
        return halo_copy(mb, piece, xs.at[mb, rows_of(piece, rows)])

    def token_halo_copy(mb, piece):
        return halo_copy(mb, piece, tokens.at[mb, rows_of(piece)])

    def hand_copy(mb, piece):
        return pltpu.make_async_remote_copy(
            outs.at[mb, rows_of(piece)], xs.at[mb, rows_of(piece, rows)],
            hand_send.at[mb, piece], hand_recv.at[mb, piece],
            device_id={"section": section + 1}, device_id_type=MESH)

    def back_copy(mb, piece):
        return pltpu.make_async_remote_copy(
            halo_out.at[rows_of(piece)], halo_in.at[mb, rows_of(piece)],
            back_send.at[mb, piece], back_recv.at[mb, piece],
            device_id={"wide": wide - 1}, device_id_type=MESH)

    def turn_copy(mb, piece):
        return pltpu.make_async_remote_copy(
            outs.at[mb, rows_of(piece)], gs.at[mb, rows_of(piece)],
            turn_send.at[mb, piece], turn_recv.at[mb, piece],
            device_id={"section": section - 1}, device_id_type=MESH)

    def relay(mb):
        for piece in pieces:
            hand_copy(mb, piece).wait_recv()

            @pl.when(has_right)
            def _(piece=piece):
                own_halo_copy(mb, piece).start()

    def out_copy(mb, target):
        return pltpu.make_async_copy(outs.at[mb], target.at[mb], out_sem.at[mb])

    def save(name, mb):
        source, target, index = {
            "normed": (normed, normed_out, 0), "att": (att, att_out, 1), "n2": (n2, n2_out, 2),
            "prod": (prod, prod_out, 3), "branch": (branch.at[lax.rem(mb, 2)], db_out, 4),
            "g": (gs.at[mb], g_out, 5), "dg": (slope.at[mb], dg_out, 6), "du": (silu.at[mb], du_out, 7),
            "dq": (qs.at[mb], dq_out, 8), "dk": (ks.at[mb], dk_out, 9), "dv": (vs.at[mb], dv_out, 10),
        }[name]
        return pltpu.make_async_copy(source, target.at[mb], save_sem.at[index, mb])

    def saved_before(name, mb):
        @pl.when(mb > 0)
        def _():
            save(name, mb - 1).wait()

    @pl.when(is_first)
    def _():
        token_copy(0).start()

    trig_copy = pltpu.make_async_copy(trig, left_b, trig_sem.at[0])
    trig_copy.start()
    for index in range(3):
        weight_copy(index).start()

    meet([
        (has_left, {"wide": wide - 1}), (has_right, {"wide": wide + 1}),
        (has_before, {"section": section - 1}), (has_after, {"section": section + 1}),
    ])

    @pl.when(is_first & has_right)
    def _():
        for piece in pieces:
            token_halo_copy(0, piece).start()

    @pl.when(is_first)
    def _():
        for mb in range(1, batches):
            token_copy(mb).start()

    @pl.when(is_last)
    def _():
        for mb in range(batches):
            cot_copy(mb).start()

    @pl.when(jnp.logical_not(has_left))
    def _():
        xs[:, halo, :] = jnp.zeros((batches, rows, width), BF16)

    @pl.when(jnp.logical_not(has_right))
    def _():
        halo_in[...] = jnp.zeros(halo_in.shape, BF16)

    gains_out[...] = jnp.zeros(gains_out.shape, F32)

    start_row = wide * rows

    def tables(mb, carry):
        positions = lax.broadcasted_iota(jnp.int32, (2 * rows, LANES), 0) + (start_row - rows)
        query_at = lax.broadcasted_iota(jnp.int32, (8, rows), 1) + start_row

        def later(image, state):
            start, first, first_row = state
            first = jnp.where(positions >= start, start, first)
            first_row = jnp.where(query_at >= start, start, first_row)
            return (start + lengths[mb, image], first, first_row)

        _, first, first_row = lax.fori_loop(
            0, lengths.shape[1], later,
            (jnp.int32(0), jnp.zeros((2 * rows, LANES), jnp.int32), jnp.zeros((8, rows), jnp.int32)))
        offsets = positions - first
        lane = lax.broadcasted_iota(jnp.int32, (2 * rows, LANES), 1)
        one_hot = jnp.concatenate(
            [jnp.where(offsets == lane + base, 1.0, 0.0).astype(BF16) for base in range(0, band, LANES)],
            axis=1)
        for which, table in enumerate((cosine, sine)):
            parts = dot(one_hot, left_b[which])
            table[mb] = parts[:, :LANES] + parts[:, LANES:]
        first_key[mb] = first_row - start_row
        return carry

    trig_copy.wait()
    lax.fori_loop(0, batches, tables, 0)

    items = [(pair, block) for pair in range(pairs) for block in range(2)]

    def place(index):
        pair, block = items[index]
        lanes = slice(pair * LANES, (pair + 1) * LANES)
        low = block * half
        return lanes, slice(low, low + half), slice(low, low + band)

    def pipelined(first, second, third):
        first(0)
        for index in range(len(items)):
            if index + 1 < len(items):
                first(index + 1)
            second(index)
            if index:
                third(index - 1)
        third(len(items) - 1)


    def normalise(mb, part):
        for low in range(part.start, part.start + rows, BLOCK):
            at = slice(low, low + BLOCK)
            scaled, _ = rms_parts(xs[mb, at, :].astype(F32))
            normed[at, :] = (scaled * gain_attn[...]).astype(BF16)

    def keys_values(mb, part):
        cos_rows, sin_rows = cosine[mb, part, :], sine[mb, part, :]
        for start in range(0, width, 256):
            rows_n = normed[part, :]
            keys = dot(rows_n, wk[:, start:start + 256])
            for inner in range(0, 256, LANES):
                ks[mb, part, start + inner:start + inner + LANES] = rope(
                    keys[:, inner:inner + LANES], cos_rows, sin_rows, 1).astype(BF16)
            vs[mb, part, start:start + 256] = dot(rows_n, wv[:, start:start + 256]).astype(BF16)

    def attention(mb):
        def scores(index):
            lanes, here, near = place(index)
            wide_f[index % 2] = dot_nt(ks[mb, near, lanes], split_heads(qs[mb, here, lanes]))

        def soften(index):
            pair, block = items[index]
            for head in range(2):
                at = slice(head * LANES, (head + 1) * LANES)
                masked = wide_f[index % 2, :, at] + bias[block]
                raw = jnp.exp(masked - jnp.max(masked, axis=0, keepdims=True))
                probs[mb, pair, block, :, at] = raw.astype(BF16)

        def collect(index):
            pair, block = items[index]
            lanes, here, near = place(index)
            left = jnp.concatenate([vs[mb, near, lanes].T, jnp.ones((16, band), BF16)], axis=0)
            turned = dot(left, probs[mb, pair, block])
            inverse = 1.0 / turned[LANES:LANES + 1]
            scale[mb, index] = inverse
            att[here, lanes] = join_heads(turned[:LANES] * inverse).astype(BF16)

        pipelined(scores, soften, collect)

    def forward(mb, carry):
        @pl.when(is_first)
        def _():
            token_copy(mb).wait()

            @pl.when(has_right & (mb + 1 < batches))
            def _():
                for piece in pieces:
                    token_halo_copy(mb + 1, piece).start()

        @pl.when(has_before & (mb == 0))
        def _():
            relay(mb)

        saved_before("normed", mb)
        normalise(mb, own)

        @pl.when(mb == 0)
        def _():
            for index in range(3):
                weight_copy(index).wait()
            for index in range(3, 7):
                weight_copy(index).start()

        cos_rows, sin_rows = cosine[mb, own, :], sine[mb, own, :]
        for start in range(0, width, 256):
            queries = dot(normed[own, :], wq[:, start:start + 256])
            for inner in range(0, 256, LANES):
                turned = rope(queries[:, inner:inner + LANES], cos_rows, sin_rows, 1)
                qs[mb, :, start + inner:start + inner + LANES] = (turned * 0.125).astype(BF16)
        keys_values(mb, own)
        for block in range(2):
            key_at = lax.broadcasted_iota(jnp.int32, (band, half), 0) + (block * half - rows)
            query_at = lax.broadcasted_iota(jnp.int32, (band, half), 1) + block * half
            first = first_key[mb, 0:1, block * half:(block + 1) * half]
            bias[block] = jnp.where((key_at >= first) & (key_at <= query_at), 0.0, -1e30)

        @pl.when(has_left)
        def _():
            for piece in pieces:
                own_halo_copy(mb, piece).wait_recv()

        normalise(mb, halo)
        keys_values(mb, halo)
        save("normed", mb).start()
        saved_before("att", mb)
        attention(mb)
        save("att", mb).start()

        @pl.when(mb == 0)
        def _():
            for index in range(3, 7):
                weight_copy(index).wait()

        saved_before("n2", mb)
        for start in range(0, width, 256):
            at = slice(start, start + 256)
            d_norm[:, at] = xs[mb, own, at].astype(F32) + dot(att[...], wo[:, at])
        for low in range(0, rows, BLOCK):
            at = slice(low, low + BLOCK)
            total = d_norm[at, :]
            scaled, _ = rms_parts(total)
            mixed[mb, at, :] = total.astype(BF16)
            n2[at, :] = (scaled * gain_mlp[...]).astype(BF16)
        save("n2", mb).start()

        @pl.when(has_before & (mb + 1 < batches))
        def _():
            relay(mb + 1)

        saved_before("prod", mb)
        for start in range(0, hidden_width, 256):
            at = slice(start, start + 256)
            gate = dot(n2[...], wg[:, at])
            up = dot(n2[...], wu[:, at])
            sigma = jax.nn.sigmoid(gate)
            gated = gate * sigma
            prod[:, at] = (gated * up).astype(BF16)
            silu[mb, :, at] = gated.astype(BF16)
            slope[mb, :, at] = (up * (sigma * (1.0 + gate * (1.0 - sigma)))).astype(BF16)
        save("prod", mb).start()
        for start in range(0, width, 256):
            at = slice(start, start + 256)
            outs[mb, :, at] = (d_norm[:, at] + dot(prod[...], wd[:, at])).astype(BF16)

        @pl.when(has_after)
        def _():
            for piece in pieces:
                hand_copy(mb, piece).start()

        out_copy(mb, block_out).start()
        return carry

    lax.fori_loop(0, batches, forward, 0)

    for name in ("normed", "att", "n2", "prod"):
        save(name, batches - 1).wait()
    for mb in range(batches):
        out_copy(mb, block_out).wait()

    @pl.when(has_after)
    def _():
        for mb in range(batches):
            for piece in pieces:
                hand_copy(mb, piece).wait_send()


    def add_gain(which, product):
        folded = jnp.sum(product.reshape(product.shape[0] // 8, 8, width), axis=0)
        at = pl.ds(8 * which, 8)
        gains_out[at, :] = gains_out[at, :] + folded

    def attention_back(mb):
        def d_weights(index):
            lanes, here, near = place(index)
            wide_f[index % 2] = dot_nt(vs[mb, near, lanes], split_heads(d_att[here, lanes]))

        def d_soften(index):
            pair, block = items[index]
            for head in range(2):
                at = slice(head * LANES, (head + 1) * LANES)
                weight = probs[mb, pair, block, :, at].astype(F32) * scale[mb, index, :, at]
                moved = weight * wide_f[index % 2, :, at]
                centre = jnp.sum(moved, axis=0, keepdims=True)
                left_b[index % 2, :, at] = (moved - weight * centre).astype(BF16)
                right_b[index % 2, :, at] = weight.astype(BF16)

        def collect(index):
            pair, block = items[index]
            lanes, here, near = place(index)
            d_scores = left_b[index % 2]
            d_keys = dot(d_scores, split_heads(qs[mb, here, lanes]))
            d_values = dot(right_b[index % 2], split_heads(d_att[here, lanes]))
            turned = lax.dot_general(
                ks[mb, near, lanes], d_scores, (((0,), (0,)), ((), ())), preferred_element_type=F32)
            at = pl.ds(rows + block * half, half)
            qs[mb, here, lanes] = rope(
                join_heads(turned) * 0.125, cosine[mb, at, :], sine[mb, at, :], -1).astype(BF16)
            slot = pair % 2
            if block == 0:
                key_f[slot], value_f[slot] = d_keys, d_values
                return
            earlier_k, earlier_v = key_f[slot], value_f[slot]
            pieces = (
                (0, half, earlier_k[:half], earlier_v[:half]),
                (half, band, earlier_k[half:] + d_keys[:rows], earlier_v[half:] + d_values[:rows]),
                (band, 2 * rows, d_keys[rows:], d_values[rows:]),
            )
            for low, high, piece_k, piece_v in pieces:
                ks[mb, low:high, lanes] = rope(
                    piece_k, cosine[mb, low:high, :], sine[mb, low:high, :], -1).astype(BF16)
                vs[mb, low:high, lanes] = piece_v.astype(BF16)

        pipelined(d_weights, d_soften, collect)

    def closes(mb):
        return has_before | (mb < batches - 1) if late else wide >= 0

    def finish(mb):
        for piece in pieces:
            @pl.when(has_right)
            def _(piece=piece):
                back_copy(mb, piece).wait_recv()

            for low in range(piece * PIECE, (piece + 1) * PIECE, BLOCK):
                at = pl.ds(low, BLOCK)
                scaled, inverse = rms_parts(xs[mb, pl.ds(rows + low, BLOCK), :].astype(F32))
                d_normed = d_own[at, :] + halo_in[mb, at, :].astype(F32)
                add_gain(0, d_normed * scaled)
                back = rms_back(d_normed * gain_attn[...], scaled, inverse)
                outs[mb, at, :] = (branch[lax.rem(mb, 2), at, :].astype(F32) + back).astype(BF16)

            @pl.when(has_before)
            def _(piece=piece):
                turn_copy(mb, piece).start()

        out_copy(mb, grad_out).start()

    def backward(mb, carry):
        @pl.when(is_last)
        def _():
            cot_copy(mb).wait()

        @pl.when(has_after)
        def _():
            for piece in pieces:
                turn_copy(mb, piece).wait_recv()

        save("g", mb).start()
        for start in range(0, hidden_width, 256):
            at = slice(start, start + 256)
            d_product = dot_nt(gs[mb], wd[at, :])
            slope[mb, :, at] = (d_product * slope[mb, :, at].astype(F32)).astype(BF16)
            silu[mb, :, at] = (d_product * silu[mb, :, at].astype(F32)).astype(BF16)
        save("dg", mb).start()
        save("du", mb).start()
        for start in range(0, width, 256):
            at = slice(start, start + 256)
            d_norm[:, at] = dot_nt(slope[mb], wg[at, :]) + dot_nt(silu[mb], wu[at, :])
        slot = lax.rem(mb, 2)

        @pl.when(mb >= 2)
        def _():
            save("branch", mb - 2).wait()

        for low in range(0, rows, BLOCK):
            at = slice(low, low + BLOCK)
            scaled, inverse = rms_parts(mixed[mb, at, :].astype(F32))
            d_normed = d_norm[at, :]
            add_gain(1, d_normed * scaled)
            total = gs[mb, at, :].astype(F32) + rms_back(d_normed * gain_mlp[...], scaled, inverse)
            branch[slot, at, :] = total.astype(BF16)
        save("branch", mb).start()
        for start in range(0, width, 256):
            at = slice(start, start + 256)
            d_att[:, at] = dot_nt(branch[slot], wo[at, :]).astype(BF16)

        @pl.when(mb > 0)
        def _():
            finish(mb - 1)

        attention_back(mb)
        save("dq", mb).start()
        save("dk", mb).start()
        save("dv", mb).start()

        @pl.when(has_left & (mb > 0))
        def _():
            for piece in pieces:
                back_copy(mb - 1, piece).wait_send()

        for start in range(0, width, 256):
            at = slice(start, start + 256)
            halo_out[:, at] = (
                dot_nt(ks[mb, halo, :], wk[at, :]) + dot_nt(vs[mb, halo, :], wv[at, :])).astype(BF16)

        @pl.when(has_left & closes(mb))
        def _():
            for piece in pieces:
                back_copy(mb, piece).start()

        for start in range(0, width, 256):
            at = slice(start, start + 256)
            d_own[:, at] = (
                dot_nt(qs[mb], wq[at, :]) + dot_nt(ks[mb, own, :], wk[at, :])
                + dot_nt(vs[mb, own, :], wv[at, :]))
        return carry

    lax.fori_loop(0, batches, backward, 0)
    closed = closes(batches - 1)

    @pl.when(closed)
    def _():
        finish(batches - 1)

    @pl.when(jnp.logical_not(closed))
    def _():
        copies = [pltpu.make_async_copy(d_own, own_out, late_sem.at[0]),
                  pltpu.make_async_copy(halo_out, halo_part_out, late_sem.at[1])]
        for copy in copies:
            copy.start()
        for copy in copies:
            copy.wait()

    for mb in range(batches - 2, batches):
        save("branch", mb).wait()
    for mb in range(batches):
        for name in ("g", "dg", "du", "dq", "dk", "dv"):
            save(name, mb).wait()
    for mb in range(batches - 1):
        out_copy(mb, grad_out).wait()

    @pl.when(closed)
    def _():
        out_copy(batches - 1, grad_out).wait()

    @pl.when(has_left & closed)
    def _():
        for piece in pieces:
            back_copy(batches - 1, piece).wait_send()

    @pl.when(has_before)
    def _():
        for mb in range(batches):
            for piece in pieces:
                turn_copy(mb, piece).wait_send()

    @pl.when(has_right)
    def _():
        for mb in range(batches):
            for piece in pieces:
                own_halo_copy(mb, piece).wait_send()


def any_spec():
    return pl.BlockSpec(memory_space=pl.ANY)


def vmem_spec():
    return pl.BlockSpec(memory_space=pltpu.VMEM)


def trig_table(head_dim, reach):
    half_dim = head_dim // 2
    freqs = np.float32(THETA) ** (-np.arange(half_dim, dtype=np.float32) * np.float32(2.0) / np.float32(head_dim))
    angles = np.arange(reach, dtype=np.float32)[:, None] * np.tile(freqs, LANES // half_dim)[None, :]
    sign = np.tile(np.repeat(np.array([-1.0, 1.0], np.float32), half_dim), LANES // head_dim)
    parts = []
    for table in (np.cos(angles), np.sin(angles) * sign):
        high = table.astype(ml_dtypes.bfloat16)
        low = (table - high.astype(np.float32)).astype(ml_dtypes.bfloat16)
        parts.append(np.concatenate([high, low], axis=1))
    return jnp.asarray(np.stack(parts))


def run_layers(tokens, cotangent, lengths, weights, gain_attn, gain_mlp, late=False):
    batches, rows, width = tokens.shape
    hidden_width = weights[4].shape[2]
    pairs = width // LANES
    band = rows + rows // 2
    one = (batches, rows, width)
    two = (batches, 2 * rows, width)
    wide = (batches, rows, hidden_width)
    outs = [(one, BF16), (one, BF16), (two, BF16), (one, BF16), (one, BF16), (wide, BF16),
            (one, BF16), (one, BF16), (wide, BF16), (wide, BF16), (one, BF16), (two, BF16), (two, BF16),
            (one[1:], F32), (one[1:], BF16), ((16, width), F32)]
    dma = pltpu.SemaphoreType.DMA
    scratch = [pltpu.VMEM(w.shape[1:], BF16) for w in weights] + [
        pltpu.VMEM(two, BF16),
        pltpu.VMEM(one, BF16),
        pltpu.VMEM(two, BF16),
        pltpu.VMEM(two, BF16),
        pltpu.VMEM((batches, pairs, 2, band, rows), BF16),
        pltpu.VMEM(wide, BF16),
        pltpu.VMEM(wide, BF16),
        pltpu.VMEM(one, BF16),
        pltpu.VMEM(two[1:], BF16),
        pltpu.VMEM(one[1:], BF16),
        pltpu.VMEM(one[1:], BF16),
        pltpu.VMEM(wide[1:], BF16),
        pltpu.VMEM(one, BF16),
        pltpu.VMEM(one, BF16),
        pltpu.VMEM(one, BF16),
        pltpu.VMEM(one[1:], BF16),
        pltpu.VMEM((2,) + one[1:], BF16),
        pltpu.VMEM(one[1:], BF16),
        pltpu.VMEM(one[1:], F32),
        pltpu.VMEM(one[1:], F32),
        pltpu.VMEM((batches, 2 * rows, LANES), F32),
        pltpu.VMEM((batches, 2 * rows, LANES), F32),
        pltpu.VMEM((batches, 8, rows), jnp.int32),
        pltpu.VMEM((2, band, rows // 2), F32),
        pltpu.VMEM((batches, 2 * pairs, 1, rows), F32),
        pltpu.VMEM((2, band, rows), F32),
        pltpu.VMEM((2, band, rows), BF16),
        pltpu.VMEM((2, band, rows), BF16),
        pltpu.VMEM((2, band, LANES), F32),
        pltpu.VMEM((2, band, LANES), F32),
        dma((7,)), dma((1,)), dma((2,)), dma((batches,)), dma((batches,)), dma((11, batches)),
    ] + [dma((batches,))] + [dma((batches, rows // PIECE))] * 8
    trig = trig_table(width // HEADS, band)
    return pl.pallas_call(
        functools.partial(layers_kernel, late),
        out_shape=[jax.ShapeDtypeStruct(shape, dtype) for shape, dtype in outs],
        in_specs=[any_spec()] * 2 + [pl.BlockSpec(memory_space=pltpu.SMEM)] + [any_spec()] * 7 + [vmem_spec()] * 2 + [any_spec()],
        out_specs=[any_spec()] * 15 + [vmem_spec()],
        scratch_shapes=scratch,
        compiler_params=pltpu.CompilerParams(
            collective_id=1, has_side_effects=True, vmem_limit_bytes=VMEM_BYTES),
        name="layers",
    )(tokens, cotangent, lengths, *weights, gain_attn, gain_mlp, trig)


LAG = 4
SENDS = 6
LAG_PAIR = 1
LENT = 3
MIX_LENDER = 5
MIX_PARTNER = 4
CROSS = 6
LATE = 8
CHUNK = 256


def dot_tn(left, right):
    return lax.dot_general(
        left, right, (((0,), (0,)), ((), ())), preferred_element_type=F32
    )


class Place:
    def __init__(self, count):
        wide = lax.axis_index("wide")
        self.outer = count // 4
        self.core, self.side, self.depth = lax.rem(wide, 2), lax.rem(wide // 2, 2), wide // 4
        self.core_mate = {"wide": wide + 1 - 2 * self.core}
        self.side_mate = {"wide": wide + 2 - 4 * self.side}
        self.low, self.high = lax.rem(self.depth, 2), self.depth // 2
        self.low_mate = {"wide": wide + 4 - 8 * self.low}
        self.high_mate = {"wide": wide + 8 - 16 * self.high}


class Pairs:
    def __init__(self, place, refs, sems):
        self.place = place
        self.dw, self.out, self.arrived = refs
        self.sent, self.received = sems

    def copy(self, j):
        slot = lax.rem(j, SENDS)
        return pltpu.make_async_remote_copy(
            self.out.at[slot], self.arrived.at[j], self.sent.at[slot], self.received.at[j],
            device_id=self.place.core_mate, device_id_type=MESH)

    def send(self, j):
        slot, held = lax.rem(j, SENDS), lax.rem(j, LAG_PAIR + 1)

        @pl.when(j >= SENDS)
        def _():
            self.copy(j - SENDS).wait_send()

        for index in range(2 * self.place.outer):
            self.out[slot, index] = self.dw[held, 2 * index + 1 - self.place.core].astype(BF16)
        self.copy(j).start()

    def total(self, j, index):
        return self.dw[lax.rem(j, LAG_PAIR + 1), 2 * index + self.place.core] + self.arrived[j, index].astype(F32)

    def drain(self, count):
        for back in range(1, SENDS + 1):
            self.copy(count - back).wait_send()


class Halve:
    def __init__(self, mate, bit, refs, sems, first=0):
        self.mate, self.bit, self.first = mate, bit, first
        self.out, self.own, self.arrived = refs
        self.sent, self.received = sems

    def copy(self, j):
        slot = lax.rem(j, SENDS)
        return pltpu.make_async_remote_copy(
            self.out.at[slot], self.arrived.at[j], self.sent.at[slot], self.received.at[j],
            device_id=self.mate, device_id_type=MESH)

    def free(self, j):
        @pl.when(j >= SENDS + self.first)
        def _():
            self.copy(j - SENDS).wait_send()

    def split(self, j, part, place_of):
        slot, held = lax.rem(j, SENDS), lax.rem(j, LAG + 1)
        for k in range(self.out.shape[1]):
            self.out[slot, k] = part(place_of(k, 1 - self.bit)).astype(BF16)
            self.own[held, k] = part(place_of(k, self.bit)).astype(F32)

    def take_from(self, j, earlier, place_of):
        self.free(j)
        earlier.copy(j).wait_recv()
        self.split(j, lambda index: earlier.total(j, index), place_of)
        self.copy(j).start()

    def total(self, j, index):
        return self.own[lax.rem(j, LAG + 1), index] + self.arrived[j, index].astype(F32)

    def close(self, j):
        self.copy(j).wait_recv()
        return self.total(j, 0)

    def drain(self, count):
        for back in range(1, SENDS + 1):
            j = count - back

            @pl.when(j >= self.first)
            def _(j=j):
                self.copy(j).wait_send()


def lowest(k, bit):
    return 2 * k + bit


class Lent:
    def __init__(self, refs, sems, section, chunks):
        self.x_out, self.x_in, self.r_out, self.r_in = refs
        self.x_send, self.x_recv, self.r_send, self.r_recv = sems
        self.lender = section == 0
        self.lent = self.x_in.shape[0]
        self.partner = {"section": 1 - section}
        self.first = jnp.where(self.lender, self.lent, 0)
        self.computed = chunks
        self.count = jnp.where(self.lender, chunks, chunks + self.lent)

    def x_copy(self, j):
        return pltpu.make_async_remote_copy(
            self.x_out.at[j], self.x_in.at[j], self.x_send.at[j], self.x_recv.at[j],
            device_id=self.partner, device_id_type=MESH)

    def r_copy(self, j):
        return pltpu.make_async_remote_copy(
            self.r_out.at[j], self.r_in.at[j], self.r_send.at[j], self.r_recv.at[j],
            device_id=self.partner, device_id_type=MESH)

    def give(self, j, pairs):
        pairs.copy(j).wait_recv()
        for index in range(self.x_out.shape[1]):
            self.x_out[j, index] = pairs.total(j, index).astype(BF16)
        self.x_copy(j).start()

    def give_back(self, j):
        @pl.when(j == self.computed)
        def _():
            pl.semaphore_wait(pltpu.get_barrier_semaphore(), 1)

        self.r_copy(j - self.computed).start()

    def drain(self, result):
        @pl.when(self.lender)
        def _():
            for j in range(self.lent):
                self.x_copy(j).wait_send()
                self.r_copy(j).wait_recv()
                result[j] = self.r_in[j]

        @pl.when(jnp.logical_not(self.lender))
        def _():
            for j in range(self.lent):
                self.r_copy(j).wait_send()


def weight_kernel(
    normed_in, att_in, n2_in, prod_in, g_in, db_in, dg_in, du_in, dq_in, dk_in, dv_in,
    own_in, halo_part_in, tokens, gains, gain_attn,
    out_m, out_d, late_grad,
    normed, att, n2, prod, g, dy, late_own, late_part, late_halo, late_x, late_branch, late_gain, late_sem, *rest,
):
    rest = list(rest)

    def take(number):
        taken, rest[:number] = rest[:number], []
        return taken

    section, wide, count = lax.axis_index("section"), lax.axis_index("wide"), lax.axis_size("wide")
    batches, rows, width = g_in.shape
    hidden_width = prod_in.shape[2]
    own = pl.ds(rows, rows)
    m_count, d_count = out_m.shape[0], out_d.shape[0]
    per_wide, per_narrow = hidden_width // CHUNK, width // CHUNK
    place = Place(count)
    lent = Lent(take(4), take(4), section, d_count)
    pairs_m, pairs_d = Pairs(place, take(3), take(2)), Pairs(place, take(3), take(2))
    mates = ((place.side_mate, place.side), (place.low_mate, place.low), (place.high_mate, place.high))
    side_m, low_m, high_m = [Halve(*mate, take(3), take(2)) for mate in mates]
    side_d, low_d, high_d = [Halve(*mate, take(3), take(2), lent.first) for mate in mates]
    low_z, high_z, side_z = [Halve(*mates[index], take(3), take(2)) for index in (1, 2, 0)]
    x_sem, dy_sem = take(2)
    z_count = m_count // CROSS
    y_count = m_count - z_count
    has_left, has_right = wide > 0, wide < count - 1

    late_loads = [
        pltpu.make_async_copy(source, target, late_sem.at[index])
        for index, (source, target) in enumerate((
            (halo_part_in, late_part), (own_in, late_own), (tokens.at[batches - 1], late_x),
            (db_in.at[batches - 1], late_branch)))]
    late_copy = pltpu.make_async_remote_copy(
        late_part, late_halo, late_sem.at[4], late_sem.at[5], device_id={"wide": wide - 1}, device_id_type=MESH)

    def finish_late():
        for copy in late_loads[1:]:
            copy.wait()
        pl.when(has_right)(lambda: late_copy.wait_recv())
        for low in range(0, rows, BLOCK):
            at = pl.ds(low, BLOCK)
            scaled, inverse = rms_parts(late_x[at, :].astype(F32))
            d_normed = late_own[at, :] + late_halo[at, :].astype(F32)
            product = (d_normed * scaled).reshape(BLOCK // 8, 8, width)
            late_gain[...] = late_gain[...] + jnp.sum(product, axis=0)
            back = rms_back(d_normed * gain_attn[...], scaled, inverse)
            late_grad[at, :] = (late_branch[at, :].astype(F32) + back).astype(BF16)


    loads = ((n2_in, n2), (att_in, att), (normed_in, normed), (prod_in, prod), (g_in, g))

    def x_copy(index):
        source, target = loads[index]
        return pltpu.make_async_copy(source, target, x_sem.at[index])

    kinds = ((dg_in, per_wide), (du_in, per_wide), (db_in, per_narrow), (dq_in, per_narrow), (dk_in, per_narrow), (dv_in, per_narrow))

    def each_load(j, act):
        slot = lax.rem(j, 2)
        base = 0
        for index, (source, parts) in enumerate(kinds):
            @pl.when((j >= base) & (j < base + parts))
            def _(source=source, base=base, index=index):
                lanes = pl.ds(pl.multiple_of((j - base) * CHUNK, CHUNK), CHUNK)
                target = dy.at[slot] if index >= 4 else dy.at[slot, :, own]
                act(pltpu.make_async_copy(source.at[:, :, lanes], target, dy_sem.at[slot]))
            base += parts
        return base

    x_copy(0).start()
    each_load(jnp.int32(0), lambda copy: copy.start())

    @pl.when(lent.lender)
    def _():
        for copy in late_loads:
            copy.start()

    for index in (3, 4, 1, 2):
        x_copy(index).start()
    late_gain[...] = jnp.zeros(late_gain.shape, F32)

    @pl.when(jnp.logical_not(has_right))
    def _():
        late_halo[...] = jnp.zeros(late_halo.shape, BF16)

    barrier = pltpu.get_barrier_semaphore()
    peers = [place.core_mate, place.side_mate, place.low_mate, place.high_mate]
    for peer in peers:
        pl.semaphore_signal(barrier, inc=1, device_id=peer, device_id_type=MESH)
    for condition, step in ((has_left, -1), (has_right, 1)):
        @pl.when(condition)
        def _(step=step):
            pl.semaphore_signal(barrier, inc=1, device_id={"wide": wide + step}, device_id_type=MESH)

    kv_first = 2 * per_wide + 2 * per_narrow
    kv_last = kv_first + 2 * per_narrow
    narrow_first = 2 * per_wide

    def compute_m(j):
        slot, held = lax.rem(j, 2), lax.rem(j, LAG_PAIR + 1)

        @pl.when(j + 1 < kv_last)
        def _():
            each_load(j + 1, lambda copy: copy.start())

        def write(left, right):
            product = dot_tn(left.reshape(-1, width), right.reshape(-1, CHUNK))
            pairs_m.dw[held] = product.reshape(pairs_m.dw.shape[1:])

        @pl.when(j < kv_last)
        def _():
            each_load(j, lambda copy: copy.wait())

        for index, first in enumerate((0, narrow_first, narrow_first + per_narrow)):
            @pl.when(j == first)
            def _(index=index):
                x_copy(index).wait()

        @pl.when(j < narrow_first)
        def _():
            write(n2[...], dy[slot, :, own, :])

        @pl.when((j >= narrow_first) & (j < narrow_first + per_narrow))
        def _():
            write(att[...], dy[slot, :, own, :])

        @pl.when((j >= narrow_first + per_narrow) & (j < kv_first))
        def _():
            write(normed[:, own, :], dy[slot, :, own, :])

        @pl.when((j >= kv_first) & (j < kv_last))
        def _():
            write(normed[...], dy[slot])

        @pl.when(j == kv_last)
        def _():
            first = jnp.sum(gains[0:8, :] + late_gain[...], axis=0, keepdims=True)
            second = jnp.sum(gains[8:16, :], axis=0, keepdims=True)
            row = lax.broadcasted_iota(jnp.int32, (LANES, width), 0)
            placed = jnp.where(row == 0, first, jnp.where(row == 1, second, 0.0))
            columns = placed.T
            pairs_m.dw[held] = jnp.concatenate([columns, columns], axis=1).reshape(pairs_m.dw.shape[1:])

    def compute_d(j):
        held = lax.rem(j, LAG_PAIR + 1)

        @pl.when(j == 0)
        def _():
            x_copy(3).wait()
            x_copy(4).wait()

        lanes = pl.ds(pl.multiple_of(j * LANES, LANES), LANES)
        product = dot_tn(prod[...].reshape(-1, hidden_width), g[:, :, lanes].reshape(-1, LANES))
        pairs_d.dw[held] = product.reshape(pairs_d.dw.shape[1:])

    compute_m(jnp.int32(0))
    greeted = len(peers) + has_left.astype(jnp.int32) + has_right.astype(jnp.int32)
    pl.semaphore_wait(barrier, greeted + lent.lender.astype(jnp.int32))
    pl.semaphore_signal(barrier, inc=1, device_id=lent.partner, device_id_type=MESH)

    @pl.when(lent.lender)
    def _():
        late_loads[0].wait()
        pl.when(has_left)(lambda: late_copy.start())


    def on_chunk(s, act_m, act_d):
        period = jnp.where(lent.lender, MIX_LENDER, MIX_PARTNER)
        turn = jnp.where(lent.lender, s // MIX_LENDER, s // MIX_PARTNER)
        spot = s - period * turn
        mixed = turn < lent.count
        j_m = jnp.where(mixed, (period - 1) * turn + spot, s - lent.count)
        j_d = turn
        is_d = (s >= 0) & mixed & (spot == period - 1)
        is_m = (s >= 0) & (j_m < m_count) & jnp.logical_not(is_d)

        @pl.when(is_m)
        def _():
            act_m(j_m)

        @pl.when(is_d)
        def _():
            act_d(j_d)

    def either(act_y, act_z):
        def act(j):
            crossing = lax.rem(j, CROSS) == CROSS - 1
            pl.when(jnp.logical_not(crossing))(lambda: act_y(j, j - j // CROSS))
            pl.when(crossing)(lambda: act_z(j, j // CROSS))
        return act

    def nothing(*_):
        pass

    def below(limit, act):
        return lambda j: pl.when(j < limit)(lambda: act(j))

    def reduced(act):
        return lambda j: pl.when(j >= lent.first)(lambda: act(j))

    def open_y(j, c):
        side_m.free(c)
        pairs_m.copy(j).wait_recv()
        side_m.split(c, lambda index: pairs_m.total(j, index), lowest)
        side_m.copy(c).start()

    def open_z(j, z):
        low_z.free(z)
        pairs_m.copy(j).wait_recv()
        low_z.split(z, lambda index: pairs_m.total(j, index), lambda k, bit: ((k // 2) * 2 + bit) * 2 + k % 2)
        low_z.copy(z).start()

    def open_d(j):
        pl.when(j < lent.first)(lambda: lent.give(j, pairs_d))

        @pl.when(j >= lent.first)
        def _():
            side_d.free(j)

            @pl.when(j < d_count)
            def _():
                pairs_d.copy(j).wait_recv()
                side_d.split(j, lambda index: pairs_d.total(j, index), lowest)

            @pl.when(j >= d_count)
            def _():
                lent.x_copy(j - d_count).wait_recv()
                side_d.split(j, lambda index: lent.x_in[j - d_count, index], lowest)

            side_d.copy(j).start()

    def close_y(j, c):
        out_m[j] = high_m.close(c)

    def close_z(j, z):
        out_m[j] = side_z.close(z)

    def close_d(j):
        total = high_d.close(j)

        @pl.when(j < d_count)
        def _():
            out_d[j] = total

        @pl.when(j >= d_count)
        def _():
            lent.r_out[j - d_count] = total
            lent.give_back(j)

    def step(s, carry):
        pl.when(lent.lender & (s == LATE))(finish_late)
        on_chunk(jnp.where(s == 0, -1, s), compute_m, below(d_count, compute_d))
        on_chunk(s, pairs_m.send, below(d_count, pairs_d.send))
        on_chunk(s - LAG_PAIR, either(open_y, open_z), open_d)
        on_chunk(
            s - LAG_PAIR - LAG,
            either(lambda j, c: low_m.take_from(c, side_m, lowest),
                   lambda j, z: high_z.take_from(z, low_z, lambda k, bit: 2 * bit + k)),
            reduced(lambda j: low_d.take_from(j, side_d, lowest)))
        on_chunk(
            s - LAG_PAIR - 2 * LAG,
            either(lambda j, c: high_m.take_from(c, low_m, lowest),
                   lambda j, z: side_z.take_from(z, high_z, lowest)),
            reduced(lambda j: high_d.take_from(j, low_d, lowest)))
        on_chunk(s - LAG_PAIR - 3 * LAG, either(close_y, close_z), reduced(close_d))
        return carry

    total = d_count + lent.lent
    steps = max(m_count + total, MIX_PARTNER * total, MIX_LENDER * d_count)
    lax.fori_loop(0, steps + LAG_PAIR + 3 * LAG, step, 0)
    pairs_m.drain(m_count)
    pairs_d.drain(d_count)
    for stage in (side_m, low_m, high_m):
        stage.drain(y_count)
    for stage in (side_d, low_d, high_d):
        stage.drain(lent.count)
    for stage in (low_z, high_z, side_z):
        stage.drain(z_count)
    lent.drain(out_d)
    pl.when(lent.lender & has_left)(lambda: late_copy.wait_send())


def run_weights(normed, att, n2, prod, g, db, dg, du, dq, dk, dv, own, part, tokens, gains, gain_attn, count):
    batches, rows, width = g.shape
    hidden_width = prod.shape[2]
    m_count = 2 * (hidden_width // CHUNK) + 4 * (width // CHUNK) + 1
    d_count = width // LANES

    dma = pltpu.SemaphoreType.DMA
    block_m, block_d = (width // count, CHUNK), (hidden_width // count, LANES)
    z_count = m_count // CROSS
    y_count = m_count - z_count

    def pairs(chunks, block):
        return [
            pltpu.VMEM((LAG_PAIR + 1, count) + block, F32),
            pltpu.VMEM((SENDS, count // 2) + block, BF16),
            pltpu.VMEM((chunks, count // 2) + block, BF16),
            dma((SENDS,)), dma((chunks,)),
        ]

    def halves(chunks, block):
        refs = []
        for blocks in (count // 4, count // 8, count // 16):
            refs += [
                pltpu.VMEM((SENDS, blocks) + block, BF16),
                pltpu.VMEM((LAG + 1, blocks) + block, F32),
                pltpu.VMEM((chunks, blocks) + block, BF16),
                dma((SENDS,)), dma((chunks,)),
            ]
        return refs

    ladders = [
        pltpu.VMEM((LENT, count // 2) + block_d, BF16),
        pltpu.VMEM((LENT, count // 2) + block_d, BF16),
        pltpu.VMEM((LENT,) + block_d, F32),
        pltpu.VMEM((LENT,) + block_d, F32),
    ] + [dma((LENT,))] * 4
    ladders += pairs(m_count, block_m) + pairs(d_count, block_d)
    ladders += halves(y_count, block_m) + halves(d_count + LENT, block_d) + halves(z_count, block_m)
    return pl.pallas_call(
        weight_kernel,
        out_shape=[
            jax.ShapeDtypeStruct((m_count,) + block_m, F32),
            jax.ShapeDtypeStruct((d_count,) + block_d, F32),
            jax.ShapeDtypeStruct(part.shape, BF16),
        ],
        in_specs=[any_spec()] * 14 + [vmem_spec()] * 2,
        out_specs=[vmem_spec()] * 3,
        scratch_shapes=[
            pltpu.VMEM(normed.shape, BF16),
            pltpu.VMEM(att.shape, BF16),
            pltpu.VMEM(n2.shape, BF16),
            pltpu.VMEM(prod.shape, BF16),
            pltpu.VMEM(g.shape, BF16),
            pltpu.VMEM((2, batches, 2 * rows, CHUNK), BF16),
            pltpu.VMEM(own.shape, F32),
        ] + [pltpu.VMEM(part.shape, BF16)] * 4 + [
            pltpu.VMEM((8, width), F32),
            pltpu.SemaphoreType.DMA((6,)),
        ] + ladders + [
            pltpu.SemaphoreType.DMA((5,)),
            pltpu.SemaphoreType.DMA((2,)),
        ],
        compiler_params=pltpu.CompilerParams(
            collective_id=3, has_side_effects=True, vmem_limit_bytes=VMEM_BYTES),
        name="weights",
    )(normed, att, n2, prod, g, db, dg, du, dq, dk, dv, own, part, tokens, gains, gain_attn)


def summed_weights(normed, att, n2, prod, g, db, dg, du, dq, dk, dv, gains):
    def outer_sum(left, right):
        total = lax.dot_general(
            left, right, (((0, 1), (0, 1)), ((), ())), preferred_element_type=F32)
        return lax.psum_scatter(total[None], "wide", scatter_dimension=1, tiled=True)

    rows = g.shape[1]
    normed_own = normed[:, rows:]
    gain_rows = gains.reshape(2, 8, -1).sum(axis=1)
    gain_parts = [
        lax.psum_scatter(gain_rows[i:i + 1], "wide", scatter_dimension=1, tiled=True) for i in range(2)]
    return (
        outer_sum(normed_own, dq), outer_sum(normed, dk), outer_sum(normed, dv), outer_sum(att, db),
        outer_sum(n2, dg), outer_sum(n2, du), outer_sum(prod, g), *gain_parts,
    )


def arrange_kernel(sizes, block, grads, late, chunks_m, chunks_d, block_out, grad_out, *rest):
    outs, (held_block, held_grads, held_m, held_d), (load_sem, store_sem) = rest[:9], rest[9:13], rest[13:]
    batches = block.shape[0]
    loads, stores = [], []
    for mb in range(batches):
        loads += [(block.at[mb], held_block.at[mb]), (grads.at[mb], held_grads.at[mb])]
        stores += [(held_block.at[mb], block_out.at[0, mb]), (held_grads.at[mb], grad_out.at[0, mb])]
    first_load = len(loads)
    groups = [pl.ds(base, min(8, chunks_m.shape[0] - base)) for base in range(0, chunks_m.shape[0], 8)]
    loads += [(chunks_m.at[group], held_m.at[group]) for group in groups] + [(chunks_d, held_d)]
    base = 0
    for size, index in zip(sizes, (4, 5, 3, 0, 1, 2)):
        for part in range(size):
            stores.append((held_m.at[base + part], outs[index].at[0, :, pl.ds(part * CHUNK, CHUNK)]))
        base += size
    for part in range(chunks_d.shape[0]):
        stores.append((held_d.at[part], outs[6].at[0, :, pl.ds(part * LANES, LANES)]))
    loads = [pltpu.make_async_copy(*pair, load_sem.at[index]) for index, pair in enumerate(loads)]
    stores = [pltpu.make_async_copy(*pair, store_sem.at[index]) for index, pair in enumerate(stores)]
    is_late = lax.axis_index("section") == 0
    last = first_load - 1
    late_load = pltpu.make_async_copy(late, held_grads.at[batches - 1], load_sem.at[last])
    pl.when(is_late)(lambda: late_load.start())
    pl.when(jnp.logical_not(is_late))(lambda: loads[last].start())
    for index, copy in reversed(list(enumerate(loads))):
        if index != last:
            copy.start()
    for copy in loads[first_load:]:
        copy.wait()
    for copy in stores[first_load:]:
        copy.start()
    for index in range(first_load):
        loads[index].wait()
        stores[index].start()
    turned = held_m[base, :, :LANES].T
    outs[7][...] = turned[0:1, :]
    outs[8][...] = turned[1:2, :]
    for copy in stores:
        copy.wait()


def arrange(block, grads, late, chunks_m, chunks_d, sizes):
    own, own_d = chunks_m.shape[1], chunks_d.shape[1]
    width, hidden_width = block.shape[2], CHUNK * sizes[0]
    shapes = [(1,) + block.shape] * 2
    narrow, broad = (1, own, width), (1, own, hidden_width)
    matrices = [narrow] * 4 + [broad] * 2 + [(1, own_d, width)]
    out_shape = [jax.ShapeDtypeStruct(shape, BF16) for shape in shapes]
    out_shape += [jax.ShapeDtypeStruct(shape, F32) for shape in matrices + [(1, own)] * 2]
    copies = sum(sizes) + chunks_d.shape[0] + 2 * block.shape[0]
    return pl.pallas_call(
        functools.partial(arrange_kernel, sizes),
        out_shape=out_shape,
        in_specs=[any_spec()] * 5,
        out_specs=[any_spec()] * 9 + [vmem_spec()] * 2,
        scratch_shapes=[pltpu.VMEM(held.shape, held.dtype) for held in (block, grads, chunks_m, chunks_d)]
        + [pltpu.SemaphoreType.DMA((2 * block.shape[0] + pl.cdiv(chunks_m.shape[0], 8) + 1,)), pltpu.SemaphoreType.DMA((copies,))],
        compiler_params=pltpu.CompilerParams(vmem_limit_bytes=VMEM_BYTES),
        name="arrange",
    )(block, grads, late, chunks_m, chunks_d)


def per_device(
    tokens, cotangent, seg_lengths, w_query, w_key, w_value, w_output, w_gate, w_up, w_down, gain_attn, gain_mlp,
):
    weights = (w_query, w_key, w_value, w_output, w_gate, w_up, w_down)
    lengths = seg_lengths.reshape(seg_lengths.shape[0], -1)
    count = lax.axis_size("wide")
    width, hidden_width = w_gate.shape[1:]
    whole_tiles = count == 16 and width % (16 * count) == 0 and hidden_width % (16 * count) == 0
    block_out, input_grads, *saved, own, part, gains = run_layers(
        tokens, cotangent, lengths, weights, gain_attn, gain_mlp, late=whole_tiles)
    if not whole_tiles:
        return (block_out[None], input_grads[None], *summed_weights(*saved, gains))
    out_m, out_d, late = run_weights(*saved, own, part, tokens, gains, gain_attn, count)
    sizes = (hidden_width // CHUNK,) * 2 + (width // CHUNK,) * 4
    return tuple(arrange(block_out, input_grads, late, out_m, out_d, sizes))


def solution(mesh):
    in_specs = (
        P(None, "wide", None),
        P(None, "wide", None),
        P(),
        *[P("section", None, None)] * 7,
        *[P("section", None)] * 2,
    )
    out_specs = (
        *[P("section", None, "wide", None)] * 2,
        *[P("section", "wide", None)] * 7,
        *[P("section", "wide")] * 2,
    )
    return jax.shard_map(
        per_device, mesh=mesh, in_specs=in_specs, out_specs=out_specs, check_vma=False
    )
```
